32 devices in a mesh: dp: 4 (over y, x), expert: 8 (over z, core).
Axes of the slice: x: 2, y: 2, z: 4, core: 2. Of those that a mesh axis runs over, the one named last changes fastest.
Arguments:
- tokens: bfloat16 [4096, 2048], P(('dp', 'expert')), may hold values from -6 to 6
- cotangent: bfloat16 [4096, 2048], P(('dp', 'expert')), may hold values from -0.3984375 to 0.3984375
- routing: int32 [4096, 8], P(('dp', 'expert')), may hold values from 0 to 7, as said below
- router_route_weights: float32 [4096, 8], P(('dp', 'expert')), may hold values from 0.1 to 1
- route_replica_choice: int32 [4096, 8], P(('dp', 'expert')), may hold values from 0 to 11
- device_expert_table: int32 [8], replicated, may hold values from 0 to 7, as said below
- gate_up_weight: bfloat16 [8, 2048, 1536], P('expert'), may hold values from -1 to 1, as said below
- down_weight: bfloat16 [8, 768, 2048], P('expert'), may hold values from -1 to 1, as said below
- adapter_down_maps: bfloat16 [8, 2048, 128], P('expert'), may hold values from -1 to 1, as said below
- adapter_up_maps: bfloat16 [8, 2, 64, 768], P('expert'), may hold values from -2 to 2, as said below
Outputs:
- mixed: bfloat16 [4096, 2048], P(('dp', 'expert'))
- grad_a: float32 [8, 2048, 128], P('expert')
- grad_b: float32 [8, 2, 64, 768], P('expert')
The draws below stay inside these ranges and needn't reach their ends.
Inputs may be any that keep to these rules, and one draw needn't show every extreme that they name: `routing`: each row names 8 different experts; experts held by more entries of device_expert_table are chosen more often. `device_expert_table`: every expert of 0 to 7 is held by one to four entries. `gate_up_weight`: entries of device_expert_table that are equal hold equal matrices. `down_weight`: entries of device_expert_table that are equal hold equal matrices. `adapter_down_maps`: entries of device_expert_table that are equal hold equal matrices. `adapter_up_maps`: entries of device_expert_table that are equal hold equal matrices.
All inputs are finite; a program needn't handle non-finite values.
Results may differ from the reference program's by a relative error of at most 0.006.
Values may be sent and summed in bfloat16 or wider, within the bound.
No kernel may reach another device: no remote copies, remote signals or barrier semaphores. Data moves between devices by JAX's collectives and lax.ppermute only.
A program may use at most 128 MiB of HBM per device.

```python
import math
import jax
import jax.numpy as jnp
from jax import lax

D = 2048
FF = 768
RANK = 64
TOP = 8
TOK_DEV = 128
SLOTS = 8
EXPERTS = 8
CAP = 128
TOKENS = 4096
N_DP = 4


def place_slots(key):
    extra_slots = SLOTS - EXPERTS
    heavy_count = (extra_slots + 7) // 8 if extra_slots >= 3 else 0
    expert_order = jax.random.permutation(jax.random.fold_in(key, 101), EXPERTS)
    chosen = jnp.concatenate([jnp.arange(3 * heavy_count, dtype=jnp.int32) // 3, heavy_count + jnp.arange(extra_slots - 3 * heavy_count, dtype=jnp.int32)])
    entries = jnp.concatenate([jnp.arange(EXPERTS, dtype=jnp.int32), expert_order[chosen].astype(jnp.int32)])
    shuffle = jax.random.permutation(jax.random.fold_in(key, 102), SLOTS)
    return entries[shuffle].astype(jnp.int32)


def expert_copies(placement, inner_key, shape, scale):

    def one_slot(expert_id):
        slot_key = jax.random.fold_in(inner_key, expert_id)
        normal_like = jax.random.normal(jax.random.fold_in(slot_key, 1), shape, jnp.float32)
        normal_like = jnp.clip(normal_like, -4.0, 4.0)
        return scale * normal_like
    return jax.vmap(one_slot)(placement)


def draw_routing(key, part):
    placement = place_slots(key)
    key = jax.random.fold_in(key, 15)
    expert_ids = jnp.arange(EXPERTS, dtype=jnp.int32)
    copies = jnp.sum((expert_ids[:, None] == placement[None, :]).astype(jnp.int32), axis=1)
    noise = jax.random.randint(key, (TOKENS, EXPERTS), 0, 1024, dtype=jnp.int32)
    score = (noise + 160 * (copies[None, :] - 1)) * EXPERTS + expert_ids[None, :]
    values, picked = lax.top_k(score, TOP)
    return picked.astype(jnp.int32)


def draw_device_expert_table(key, part):
    return place_slots(key)


def draw_gate_up_weight(key, part):
    placement = place_slots(key)
    key = jax.random.fold_in(key, 11)
    return expert_copies(placement, key, (D, 2 * FF), D ** (-0.5)).astype(jnp.bfloat16)


def draw_down_weight(key, part):
    placement = place_slots(key)
    key = jax.random.fold_in(key, 12)
    return expert_copies(placement, key, (FF, D), FF ** (-0.5)).astype(jnp.bfloat16)


def draw_adapter_down_maps(key, part):
    placement = place_slots(key)
    key = jax.random.fold_in(key, 13)
    return expert_copies(placement, key, (D, 2 * RANK), D ** (-0.5)).astype(jnp.bfloat16)


def draw_adapter_up_maps(key, part):
    placement = place_slots(key)
    key = jax.random.fold_in(key, 14)
    return expert_copies(placement, key, (2, RANK, FF), RANK ** (-0.5)).astype(jnp.bfloat16)


def set_ends(drawn, key, least, high):
    longest = drawn.shape.index(max(drawn.shape))
    spots = []
    for shift in (0, 1):
        where = [jax.random.randint(jax.random.fold_in(key, axis), (), 0, length) for axis, length in enumerate(drawn.shape)]
        where[longest] = (where[longest] + shift) % drawn.shape[longest]
        spots.append(tuple(where))
    return drawn.at[spots[0]].set(least).at[spots[1]].set(high)


def shard_levels(rng, shape, shards, low, largest):
    factor_of = 1.0
    for dim, shards_of in shards:
        draws = jax.random.uniform(jax.random.fold_in(jax.random.fold_in(rng, 6), dim), (shards_of,), jnp.float32, low / len(shards), largest / len(shards))
        factor_of = factor_of * jnp.repeat(jnp.exp(draws), shape[dim] // shards_of).reshape((-1,) + (1,) * (len(shape) - 1 - dim))
    return factor_of


def bell_draw(own_key, dims, deviation, most, pieces=(), kind=jnp.bfloat16):
    values = jax.random.normal(own_key, dims, jnp.float32) * deviation
    if len(pieces) > 0:
        values = shard_levels(own_key, dims, pieces, -0.22, 0.18) * values
    return jnp.clip(values, min=-most, max=most).astype(kind)


def setup_inputs(seed: int = 0) -> dict:
    key_of = jax.random.split(jax.random.key(seed), 11)
    return {
        "tokens": bell_draw(key_of[0], (TOKENS, D), 1.0, 6.0, ((0, 32),)),
        "cotangent": bell_draw(key_of[1], (TOKENS, D), 0.0625, 0.3984375, ((0, 32),)),
        "routing": draw_routing(jax.random.fold_in(key_of[10], 71), 0),
        "router_route_weights": jnp.clip(jnp.exp(math.log(1.0) - 2.3025851 * jax.random.uniform(key_of[3], (TOKENS, TOP), jnp.float32) ** shard_levels(key_of[3], (TOKENS, TOP), ((0, 32),), -0.2, 0.2)), 0.1, 1.0),
        "route_replica_choice": set_ends(jax.random.randint(key_of[4], (TOKENS, TOP), 0, 12), jax.random.fold_in(key_of[4], 1), 0, 11).astype(jnp.int32),
        "device_expert_table": draw_device_expert_table(jax.random.fold_in(key_of[10], 71), 0),
        "gate_up_weight": draw_gate_up_weight(jax.random.fold_in(key_of[10], 71), 0),
        "down_weight": draw_down_weight(jax.random.fold_in(key_of[10], 71), 0),
        "adapter_down_maps": draw_adapter_down_maps(jax.random.fold_in(key_of[10], 71), 0),
        "adapter_up_maps": draw_adapter_up_maps(jax.random.fold_in(key_of[10], 71), 0),
    }


ADAPTER_SCALE = 0.5


def route_rows(routing, route_replica_choice, device_expert_table, capacity):
    slot_total = device_expert_table.shape[0]
    route_total = routing.shape[0] * routing.shape[1]
    expert_flat = routing.reshape(-1).astype(jnp.int32)
    holds_mask = (expert_flat[:, None] == device_expert_table[None, :]).astype(jnp.int32)
    copies = jnp.sum(holds_mask, axis=1).astype(jnp.int32)
    wanted = (route_replica_choice.reshape(-1).astype(jnp.int32) % copies).astype(jnp.int32)
    before = (jnp.cumsum(holds_mask, axis=1).astype(jnp.int32) - holds_mask).astype(jnp.int32)
    picked = (holds_mask * (before == wanted[:, None]).astype(jnp.int32)).astype(jnp.int32)
    ahead_of = (jnp.cumsum(picked, axis=0).astype(jnp.int32) - picked).astype(jnp.int32)
    position = jnp.sum(picked * ahead_of, axis=1).astype(jnp.int32)
    target = jnp.sum(picked * jnp.arange(slot_total, dtype=jnp.int32)[None, :], axis=1).astype(jnp.int32)
    kept_mask = position < capacity
    dest_index = jnp.where(kept_mask, target * capacity + position, slot_total * capacity).astype(jnp.int32)
    source = jnp.full((slot_total * capacity,), route_total, jnp.int32)
    source = source.at[dest_index].set(jnp.arange(route_total, dtype=jnp.int32), mode="drop")
    return kept_mask, dest_index, source


def expert_apply_forward(rows_in, gate_up, down, adapt_a, adapt_b):
    adapter_rank_count = adapt_b.shape[1]
    hidden_width = adapt_b.shape[2]
    reduced_rank_rows = jnp.dot(rows_in, adapt_a, preferred_element_type=jnp.float32).astype(jnp.bfloat16)
    base_preactivation = jnp.dot(rows_in, gate_up, preferred_element_type=jnp.float32)
    adapter_gate_delta = jnp.dot(reduced_rank_rows[:, :adapter_rank_count], adapt_b[0], preferred_element_type=jnp.float32)
    adapter_up_delta = jnp.dot(reduced_rank_rows[:, adapter_rank_count:], adapt_b[1], preferred_element_type=jnp.float32)
    gate_preactivation = base_preactivation[:, :hidden_width] + ADAPTER_SCALE * adapter_gate_delta
    up_preactivation = base_preactivation[:, hidden_width:] + ADAPTER_SCALE * adapter_up_delta
    sigmoid_gate = jax.nn.sigmoid(gate_preactivation)
    active = gate_preactivation * sigmoid_gate
    hidden = (active * up_preactivation).astype(jnp.bfloat16)
    layer_output = jnp.dot(hidden, down, preferred_element_type=jnp.float32).astype(jnp.bfloat16)
    return layer_output, (reduced_rank_rows, gate_preactivation, up_preactivation, sigmoid_gate, active)


def expert_backward(rows_in, scaled, down, adapt_b, saved_residuals):
    reduced_rank_rows, gate_preactivation, up_preactivation, sigmoid_gate, active = saved_residuals
    adapter_rank_count = adapt_b.shape[1]
    back_hidden = lax.dot_general(scaled, down, (((1,), (1,)), ((), ())), preferred_element_type=jnp.float32)
    up_preactivation_gradient = (back_hidden * active).astype(jnp.bfloat16)
    slope = sigmoid_gate * (1.0 + gate_preactivation * (1.0 - sigmoid_gate))
    gate_preactivation_gradient = (back_hidden * up_preactivation * slope).astype(jnp.bfloat16)
    row_dimension_numbers = (((0,), (0,)), ((), ()))
    gate_up_map_gradient = ADAPTER_SCALE * lax.dot_general(reduced_rank_rows[:, :adapter_rank_count], gate_preactivation_gradient, row_dimension_numbers, preferred_element_type=jnp.float32)
    up_map_gradient = ADAPTER_SCALE * lax.dot_general(reduced_rank_rows[:, adapter_rank_count:], up_preactivation_gradient, row_dimension_numbers, preferred_element_type=jnp.float32)
    cols_dims = (((1,), (1,)), ((), ()))
    gate_reduced_rows = lax.dot_general(gate_preactivation_gradient, adapt_b[0], cols_dims, preferred_element_type=jnp.float32)
    up_reduced_rows = lax.dot_general(up_preactivation_gradient, adapt_b[1], cols_dims, preferred_element_type=jnp.float32)
    reduced_gradient = (ADAPTER_SCALE * jnp.concatenate([gate_reduced_rows, up_reduced_rows], axis=1)).astype(jnp.bfloat16)
    grad_adapt_a = lax.dot_general(rows_in, reduced_gradient, row_dimension_numbers, preferred_element_type=jnp.float32)
    return grad_adapt_a, jnp.stack([gate_up_map_gradient, up_map_gradient])


def reference(tokens, cotangent, routing, router_route_weights, route_replica_choice, device_expert_table, gate_up_weight, down_weight, adapter_down_maps, adapter_up_maps):
    groups = N_DP * SLOTS
    route_total = TOK_DEV * TOP
    kept_mask, dest_index, source = jax.vmap(route_rows, in_axes=(0, 0, None, None))(
        routing.reshape(groups, TOK_DEV, TOP), route_replica_choice.reshape(groups, TOK_DEV, TOP), device_expert_table, CAP)
    valid_route_mask = source < route_total
    safe_route = jnp.minimum(source, route_total - 1).astype(jnp.int32)
    block_start = (jnp.arange(groups, dtype=jnp.int32) * TOK_DEV)[:, None]
    route_token_index = (block_start + safe_route // TOP).astype(jnp.int32)
    route_weight_rows = jnp.take_along_axis(router_route_weights.reshape(groups, route_total), safe_route, axis=1)

    def grouped_by_device(table):
        return table.reshape(groups, SLOTS, CAP).transpose(1, 0, 2).reshape(SLOTS, groups * CAP)

    def per_slot(accum, element_list):
        index_row, valid_row, weight_row, gate_up, down, adapt_a, adapt_b = element_list
        zero_row = jnp.zeros((), jnp.bfloat16)
        rows_in = jnp.where(valid_row[:, None], tokens[index_row], zero_row).astype(jnp.bfloat16)
        product = (weight_row[:, None] * cotangent[index_row].astype(jnp.float32)).astype(jnp.bfloat16)
        scaled = jnp.where(valid_row[:, None], product, zero_row).astype(jnp.bfloat16)
        layer_output, saved_residuals = expert_apply_forward(rows_in, gate_up, down, adapt_a, adapt_b)
        grad_adapt_a, grad_adapt_b = expert_backward(rows_in, scaled, down, adapt_b, saved_residuals)
        contrib = jnp.where(valid_row[:, None], weight_row[:, None] * layer_output.astype(jnp.float32), jnp.zeros((), jnp.float32))
        accum = accum.at[index_row].add(contrib)
        return accum, (grad_adapt_a, grad_adapt_b)

    accum_start = jnp.zeros((TOKENS, D), jnp.float32)
    element_list = (grouped_by_device(route_token_index), grouped_by_device(valid_route_mask), grouped_by_device(route_weight_rows), gate_up_weight, down_weight, adapter_down_maps, adapter_up_maps)
    accum, (slot_a, slot_b) = lax.scan(per_slot, accum_start, element_list)
    mixed = accum.astype(jnp.bfloat16)
    same = (device_expert_table[:, None] == device_expert_table[None, :]).astype(jnp.float32)
    grad_a = jnp.dot(same, slot_a.reshape(SLOTS, -1), precision=lax.Precision.HIGHEST).reshape(slot_a.shape)
    grad_b = jnp.dot(same, slot_b.reshape(SLOTS, -1), precision=lax.Precision.HIGHEST).reshape(slot_b.shape)
    return mixed, grad_a, grad_b
```

```python
import jax
import jax.numpy as jnp
from jax import lax
from jax.sharding import PartitionSpec as P

ADAPTER_SCALE = 0.5


def route_rows(routing, route_replica_choice, device_expert_table, capacity):
    slot_total = device_expert_table.shape[0]
    route_total = routing.shape[0] * routing.shape[1]
    expert_flat = routing.reshape(-1)
    holds_mask = (expert_flat[:, None] == device_expert_table[None, :]).astype(jnp.int32)
    copies = jnp.sum(holds_mask, axis=1)
    wanted = route_replica_choice.reshape(-1) % copies
    before = jnp.cumsum(holds_mask, axis=1) - holds_mask
    picked = holds_mask * (before == wanted[:, None]).astype(jnp.int32)
    ahead_of = jnp.cumsum(picked, axis=0) - picked
    position = jnp.sum(picked * ahead_of, axis=1)
    target = jnp.sum(picked * jnp.arange(slot_total, dtype=jnp.int32)[None, :], axis=1)
    kept_mask = position < capacity
    dest_index = jnp.where(kept_mask, target * capacity + position, slot_total * capacity)
    source = jnp.full((slot_total * capacity,), route_total, jnp.int32)
    source = source.at[dest_index].set(jnp.arange(route_total, dtype=jnp.int32), mode="drop")
    return (kept_mask, dest_index, source)


def expert_apply_forward(rows_in, gate_up, down, adapt_a, adapt_b):
    adapter_rank_count = adapt_b.shape[1]
    hidden_width = adapt_b.shape[2]
    reduced_rank_rows = jnp.dot(rows_in, adapt_a, preferred_element_type=jnp.float32).astype(
        jnp.bfloat16
    )
    base_preactivation = jnp.dot(rows_in, gate_up, preferred_element_type=jnp.float32)
    adapter_gate_delta = jnp.dot(
        reduced_rank_rows[:, :adapter_rank_count], adapt_b[0], preferred_element_type=jnp.float32
    )
    adapter_up_delta = jnp.dot(
        reduced_rank_rows[:, adapter_rank_count:], adapt_b[1], preferred_element_type=jnp.float32
    )
    gate_preactivation = base_preactivation[:, :hidden_width] + ADAPTER_SCALE * adapter_gate_delta
    up_preactivation = base_preactivation[:, hidden_width:] + ADAPTER_SCALE * adapter_up_delta
    sigmoid_gate = jax.nn.sigmoid(gate_preactivation)
    active = gate_preactivation * sigmoid_gate
    hidden = (active * up_preactivation).astype(jnp.bfloat16)
    layer_output = jnp.dot(hidden, down, preferred_element_type=jnp.float32).astype(jnp.bfloat16)
    return (
        layer_output,
        (reduced_rank_rows, gate_preactivation, up_preactivation, sigmoid_gate, active),
    )


def expert_backward(rows_in, scaled, down, adapt_b, saved_residuals):
    reduced_rank_rows, gate_preactivation, up_preactivation, sigmoid_gate, active = saved_residuals
    adapter_rank_count = adapt_b.shape[1]
    back_hidden = lax.dot_general(
        scaled, down, (((1,), (1,)), ((), ())), preferred_element_type=jnp.float32
    )
    up_preactivation_gradient = (back_hidden * active).astype(jnp.bfloat16)
    slope = sigmoid_gate * (1.0 + gate_preactivation * (1.0 - sigmoid_gate))
    gate_preactivation_gradient = (back_hidden * up_preactivation * slope).astype(jnp.bfloat16)
    row_dimension_numbers = (((0,), (0,)), ((), ()))
    gate_up_map_gradient = ADAPTER_SCALE * lax.dot_general(
        reduced_rank_rows[:, :adapter_rank_count],
        gate_preactivation_gradient,
        row_dimension_numbers,
        preferred_element_type=jnp.float32,
    )
    up_map_gradient = ADAPTER_SCALE * lax.dot_general(
        reduced_rank_rows[:, adapter_rank_count:],
        up_preactivation_gradient,
        row_dimension_numbers,
        preferred_element_type=jnp.float32,
    )
    cols_dims = (((1,), (1,)), ((), ()))
    gate_reduced_rows = lax.dot_general(
        gate_preactivation_gradient, adapt_b[0], cols_dims, preferred_element_type=jnp.float32
    )
    up_reduced_rows = lax.dot_general(
        up_preactivation_gradient, adapt_b[1], cols_dims, preferred_element_type=jnp.float32
    )
    reduced_gradient = (
        ADAPTER_SCALE * jnp.concatenate([gate_reduced_rows, up_reduced_rows], axis=1)
    ).astype(jnp.bfloat16)
    grad_adapt_a = lax.dot_general(
        rows_in, reduced_gradient, row_dimension_numbers, preferred_element_type=jnp.float32
    )
    return (grad_adapt_a, jnp.stack([gate_up_map_gradient, up_map_gradient]))


def sparse_body(
    tokens,
    cotangent,
    routing,
    router_route_weights,
    route_replica_choice,
    device_expert_table,
    gate_up_weight,
    down_weight,
    adapter_down_maps,
    adapter_up_maps,
):
    slot_total = lax.axis_size("expert")
    tok_rows = tokens.shape[0]
    model_feature_width = tokens.shape[1]
    top_routes = routing.shape[1]
    route_total = tok_rows * top_routes
    capacity = route_total // slot_total
    kept_mask, dest_index, source = route_rows(
        routing, route_replica_choice, device_expert_table, capacity
    )
    valid_route_mask = source < route_total
    safe_route = jnp.minimum(source, route_total - 1)
    route_token_index = safe_route // top_routes
    weight_flat = router_route_weights.reshape(-1)
    route_weight_rows = weight_flat[safe_route]
    zero_row = jnp.zeros((), jnp.bfloat16)
    rows_out = jnp.where(valid_route_mask[:, None], tokens[route_token_index], zero_row).reshape(
        slot_total, capacity, model_feature_width
    )
    product = (
        route_weight_rows[:, None] * cotangent[route_token_index].astype(jnp.float32)
    ).astype(jnp.bfloat16)
    scaled_out = jnp.where(valid_route_mask[:, None], product, zero_row).reshape(
        slot_total, capacity, model_feature_width
    )
    rows_in = lax.all_to_all(rows_out, "expert", split_axis=0, concat_axis=0, tiled=True)
    flattened_rows = rows_in.reshape(-1, model_feature_width)
    layer_output, saved_residuals = expert_apply_forward(
        flattened_rows, gate_up_weight[0], down_weight[0], adapter_down_maps[0], adapter_up_maps[0]
    )
    returned = lax.all_to_all(
        layer_output.reshape(slot_total, capacity, model_feature_width),
        "expert",
        split_axis=0,
        concat_axis=0,
        tiled=True,
    )
    returned = returned.reshape(-1, model_feature_width)
    picked_rows = returned[jnp.minimum(dest_index, slot_total * capacity - 1)]
    weighted = jnp.where(
        kept_mask[:, None],
        weight_flat[:, None] * picked_rows.astype(jnp.float32),
        jnp.zeros((), jnp.float32),
    )
    mixed = jnp.sum(weighted.reshape(tok_rows, top_routes, model_feature_width), axis=1).astype(
        jnp.bfloat16
    )
    scaled_input_rows = lax.all_to_all(
        scaled_out, "expert", split_axis=0, concat_axis=0, tiled=True
    )
    grad_adapt_a, grad_adapt_b = expert_backward(
        flattened_rows,
        scaled_input_rows.reshape(-1, model_feature_width),
        down_weight[0],
        adapter_up_maps[0],
        saved_residuals,
    )
    piece_a = grad_adapt_a.reshape(slot_total, -1)
    piece_b = grad_adapt_b.reshape(slot_total, -1)
    expert_total = max(top_routes, slot_total // 2)
    members = (
        jnp.arange(expert_total, dtype=jnp.int32)[:, None] == device_expert_table[None, :]
    ).astype(jnp.float32)
    piece_a, piece_b = lax.psum((piece_a, piece_b), "dp")
    got_a, got_b = (
        lax.all_to_all(piece_a, "expert", split_axis=0, concat_axis=0, tiled=True),
        lax.all_to_all(piece_b, "expert", split_axis=0, concat_axis=0, tiled=True),
    )
    expert_a = jnp.dot(members, got_a, precision=lax.Precision.HIGHEST)
    expert_b = jnp.dot(members, got_b, precision=lax.Precision.HIGHEST)
    back_dims = (((0,), (0,)), ((), ()))
    spread_a = lax.dot_general(members, expert_a, back_dims, precision=lax.Precision.HIGHEST)
    spread_b = lax.dot_general(members, expert_b, back_dims, precision=lax.Precision.HIGHEST)
    summed_a, summed_b = (
        lax.all_to_all(spread_a, "expert", split_axis=0, concat_axis=0, tiled=True),
        lax.all_to_all(spread_b, "expert", split_axis=0, concat_axis=0, tiled=True),
    )
    grad_a = summed_a.reshape(grad_adapt_a.shape)[None]
    grad_b = summed_b.reshape(grad_adapt_b.shape)[None]
    return (mixed, grad_a, grad_b)


def dense_route_weights(routing, weights, choice, table, capacity):
    holds = (routing[:, :, None] == table[None, None, :]).astype(jnp.int32)
    copies = jnp.sum(holds, axis=2)
    wanted = choice % copies
    before = jnp.cumsum(holds, axis=2) - holds
    picked = holds * (before == wanted[:, :, None]).astype(jnp.int32)
    taken = jnp.sum(picked, axis=1)
    rank = jnp.cumsum(taken, axis=0) - taken
    route_weight = jnp.sum(picked.astype(jnp.float32) * weights[:, :, None], axis=1)
    return jnp.where(rank < capacity, route_weight, 0.0)


def dense_body(
    tokens,
    cotangent,
    routing,
    router_route_weights,
    route_replica_choice,
    device_expert_table,
    gate_up_weight,
    down_weight,
    adapter_down_maps,
    adapter_up_maps,
):
    slot_total = lax.axis_size("expert")
    capacity = tokens.shape[0] * routing.shape[1] // slot_total
    me = lax.axis_index("expert")
    weight_table = dense_route_weights(
        routing, router_route_weights, route_replica_choice, device_expert_table, capacity
    )
    rows = lax.all_gather(tokens, "expert", tiled=True)
    weight_all = lax.all_gather(weight_table, "expert", tiled=True)
    w = lax.dynamic_slice_in_dim(weight_all, me, 1, axis=1)
    cot = lax.all_gather(cotangent, "expert", tiled=True)
    layer_output, saved = expert_apply_forward(
        rows, gate_up_weight[0], down_weight[0], adapter_down_maps[0], adapter_up_maps[0]
    )
    part = (w * layer_output.astype(jnp.float32)).astype(jnp.bfloat16)
    mixed = lax.psum_scatter(part, "expert", scatter_dimension=0, tiled=True)
    scaled = (w * cot.astype(jnp.float32)).astype(jnp.bfloat16)
    grad_a, grad_b = expert_backward(rows, scaled, down_weight[0], adapter_up_maps[0], saved)
    grad_a, grad_b = lax.psum((grad_a, grad_b), "dp")
    return mixed, grad_a[None], grad_b[None]


def body(*arrays):
    if lax.axis_size("expert") == arrays[2].shape[1]:
        return dense_body(*arrays)
    return sparse_body(*arrays)


def solution(mesh):
    return jax.shard_map(
        body,
        mesh=mesh,
        in_specs=(
            P(("dp", "expert"), None),
            P(("dp", "expert"), None),
            P(("dp", "expert"), None),
            P(("dp", "expert"), None),
            P(("dp", "expert"), None),
            P(),
            P("expert", None, None),
            P("expert", None, None),
            P("expert", None, None),
            P("expert", None, None, None),
        ),
        out_specs=(
            P(("dp", "expert"), None),
            P("expert", None, None),
            P("expert", None, None, None),
        ),
        check_vma=False,
    )
```

```python
import jax
import jax.numpy as jnp
from jax import lax
from jax.sharding import PartitionSpec as P

ADAPTER_SCALE = 0.5


def route_rows(routing, route_replica_choice, device_expert_table, capacity):
    slot_total = device_expert_table.shape[0]
    route_total = routing.shape[0] * routing.shape[1]
    expert_flat = routing.reshape(-1)
    holds_mask = (expert_flat[:, None] == device_expert_table[None, :]).astype(jnp.int32)
    copies = jnp.sum(holds_mask, axis=1)
    wanted = route_replica_choice.reshape(-1) % copies
    before = jnp.cumsum(holds_mask, axis=1) - holds_mask
    picked = holds_mask * (before == wanted[:, None]).astype(jnp.int32)
    ahead_of = jnp.cumsum(picked, axis=0) - picked
    position = jnp.sum(picked * ahead_of, axis=1)
    target = jnp.sum(picked * jnp.arange(slot_total, dtype=jnp.int32)[None, :], axis=1)
    kept_mask = position < capacity
    dest_index = jnp.where(kept_mask, target * capacity + position, slot_total * capacity)
    source = jnp.full((slot_total * capacity,), route_total, jnp.int32)
    source = source.at[dest_index].set(jnp.arange(route_total, dtype=jnp.int32), mode="drop")
    return (kept_mask, dest_index, source)


def expert_apply_forward(rows_in, gate_up, down, adapt_a, adapt_b):
    adapter_rank_count = adapt_b.shape[1]
    hidden_width = adapt_b.shape[2]
    reduced_rank_rows = jnp.dot(rows_in, adapt_a, preferred_element_type=jnp.float32).astype(
        jnp.bfloat16
    )
    base_preactivation = jnp.dot(rows_in, gate_up, preferred_element_type=jnp.float32)
    adapter_gate_delta = jnp.dot(
        reduced_rank_rows[:, :adapter_rank_count], adapt_b[0], preferred_element_type=jnp.float32
    )
    adapter_up_delta = jnp.dot(
        reduced_rank_rows[:, adapter_rank_count:], adapt_b[1], preferred_element_type=jnp.float32
    )
    gate_preactivation = base_preactivation[:, :hidden_width] + ADAPTER_SCALE * adapter_gate_delta
    up_preactivation = base_preactivation[:, hidden_width:] + ADAPTER_SCALE * adapter_up_delta
    sigmoid_gate = jax.nn.sigmoid(gate_preactivation)
    active = gate_preactivation * sigmoid_gate
    hidden = (active * up_preactivation).astype(jnp.bfloat16)
    layer_output = jnp.dot(hidden, down, preferred_element_type=jnp.float32).astype(jnp.bfloat16)
    return (
        layer_output,
        (reduced_rank_rows, gate_preactivation, up_preactivation, sigmoid_gate, active),
    )


def expert_backward(rows_in, scaled, down, adapt_b, saved_residuals):
    reduced_rank_rows, gate_preactivation, up_preactivation, sigmoid_gate, active = saved_residuals
    adapter_rank_count = adapt_b.shape[1]
    back_hidden = lax.dot_general(
        scaled, down, (((1,), (1,)), ((), ())), preferred_element_type=jnp.float32
    )
    up_preactivation_gradient = (back_hidden * active).astype(jnp.bfloat16)
    slope = sigmoid_gate * (1.0 + gate_preactivation * (1.0 - sigmoid_gate))
    gate_preactivation_gradient = (back_hidden * up_preactivation * slope).astype(jnp.bfloat16)
    row_dimension_numbers = (((0,), (0,)), ((), ()))
    gate_up_map_gradient = ADAPTER_SCALE * lax.dot_general(
        reduced_rank_rows[:, :adapter_rank_count],
        gate_preactivation_gradient,
        row_dimension_numbers,
        preferred_element_type=jnp.float32,
    )
    up_map_gradient = ADAPTER_SCALE * lax.dot_general(
        reduced_rank_rows[:, adapter_rank_count:],
        up_preactivation_gradient,
        row_dimension_numbers,
        preferred_element_type=jnp.float32,
    )
    cols_dims = (((1,), (1,)), ((), ()))
    gate_reduced_rows = lax.dot_general(
        gate_preactivation_gradient, adapt_b[0], cols_dims, preferred_element_type=jnp.float32
    )
    up_reduced_rows = lax.dot_general(
        up_preactivation_gradient, adapt_b[1], cols_dims, preferred_element_type=jnp.float32
    )
    reduced_gradient = (
        ADAPTER_SCALE * jnp.concatenate([gate_reduced_rows, up_reduced_rows], axis=1)
    ).astype(jnp.bfloat16)
    grad_adapt_a = lax.dot_general(
        rows_in, reduced_gradient, row_dimension_numbers, preferred_element_type=jnp.float32
    )
    return (grad_adapt_a, jnp.stack([gate_up_map_gradient, up_map_gradient]))


def sparse_body(
    tokens,
    cotangent,
    routing,
    router_route_weights,
    route_replica_choice,
    device_expert_table,
    gate_up_weight,
    down_weight,
    adapter_down_maps,
    adapter_up_maps,
):
    slot_total = lax.axis_size("expert")
    tok_rows = tokens.shape[0]
    model_feature_width = tokens.shape[1]
    top_routes = routing.shape[1]
    route_total = tok_rows * top_routes
    capacity = route_total // slot_total
    kept_mask, dest_index, source = route_rows(
        routing, route_replica_choice, device_expert_table, capacity
    )
    valid_route_mask = source < route_total
    safe_route = jnp.minimum(source, route_total - 1)
    route_token_index = safe_route // top_routes
    weight_flat = router_route_weights.reshape(-1)
    route_weight_rows = weight_flat[safe_route]
    zero_row = jnp.zeros((), jnp.bfloat16)
    rows_out = jnp.where(valid_route_mask[:, None], tokens[route_token_index], zero_row).reshape(
        slot_total, capacity, model_feature_width
    )
    product = (
        route_weight_rows[:, None] * cotangent[route_token_index].astype(jnp.float32)
    ).astype(jnp.bfloat16)
    scaled_out = jnp.where(valid_route_mask[:, None], product, zero_row).reshape(
        slot_total, capacity, model_feature_width
    )
    rows_in = lax.all_to_all(rows_out, "expert", split_axis=0, concat_axis=0, tiled=True)
    flattened_rows = rows_in.reshape(-1, model_feature_width)
    layer_output, saved_residuals = expert_apply_forward(
        flattened_rows, gate_up_weight[0], down_weight[0], adapter_down_maps[0], adapter_up_maps[0]
    )
    returned = lax.all_to_all(
        layer_output.reshape(slot_total, capacity, model_feature_width),
        "expert",
        split_axis=0,
        concat_axis=0,
        tiled=True,
    )
    returned = returned.reshape(-1, model_feature_width)
    picked_rows = returned[jnp.minimum(dest_index, slot_total * capacity - 1)]
    weighted = jnp.where(
        kept_mask[:, None],
        weight_flat[:, None] * picked_rows.astype(jnp.float32),
        jnp.zeros((), jnp.float32),
    )
    mixed = jnp.sum(weighted.reshape(tok_rows, top_routes, model_feature_width), axis=1).astype(
        jnp.bfloat16
    )
    scaled_input_rows = lax.all_to_all(
        scaled_out, "expert", split_axis=0, concat_axis=0, tiled=True
    )
    grad_adapt_a, grad_adapt_b = expert_backward(
        flattened_rows,
        scaled_input_rows.reshape(-1, model_feature_width),
        down_weight[0],
        adapter_up_maps[0],
        saved_residuals,
    )
    piece_a = grad_adapt_a.reshape(slot_total, -1)
    piece_b = grad_adapt_b.reshape(slot_total, -1)
    expert_total = max(top_routes, slot_total // 2)
    members = (
        jnp.arange(expert_total, dtype=jnp.int32)[:, None] == device_expert_table[None, :]
    ).astype(jnp.float32)
    piece_a, piece_b = lax.psum((piece_a, piece_b), "dp")
    got_a, got_b = (
        lax.all_to_all(piece_a, "expert", split_axis=0, concat_axis=0, tiled=True),
        lax.all_to_all(piece_b, "expert", split_axis=0, concat_axis=0, tiled=True),
    )
    expert_a = jnp.dot(members, got_a, precision=lax.Precision.HIGHEST)
    expert_b = jnp.dot(members, got_b, precision=lax.Precision.HIGHEST)
    back_dims = (((0,), (0,)), ((), ()))
    spread_a = lax.dot_general(members, expert_a, back_dims, precision=lax.Precision.HIGHEST)
    spread_b = lax.dot_general(members, expert_b, back_dims, precision=lax.Precision.HIGHEST)
    summed_a, summed_b = (
        lax.all_to_all(spread_a, "expert", split_axis=0, concat_axis=0, tiled=True),
        lax.all_to_all(spread_b, "expert", split_axis=0, concat_axis=0, tiled=True),
    )
    grad_a = summed_a.reshape(grad_adapt_a.shape)[None]
    grad_b = summed_b.reshape(grad_adapt_b.shape)[None]
    return (mixed, grad_a, grad_b)


def dense_route_weights(routing, weights, choice, table, capacity):
    holds = (routing[:, :, None] == table[None, None, :]).astype(jnp.int32)
    copies = jnp.sum(holds, axis=2)
    wanted = choice % copies
    before = jnp.cumsum(holds, axis=2) - holds
    picked = holds * (before == wanted[:, :, None]).astype(jnp.int32)
    taken = jnp.sum(picked, axis=1)
    rank = jnp.cumsum(taken, axis=0) - taken
    route_weight = jnp.sum(picked.astype(jnp.float32) * weights[:, :, None], axis=1)
    return jnp.where(rank < capacity, route_weight, 0.0)


def z_pairs(*moves):
    return [(2 * a + core, 2 * b + core) for a, b in moves for core in (0, 1)]


ALL_SWAP = z_pairs((0, 1), (1, 0), (2, 3), (3, 2))
MID_SWAP = z_pairs((1, 2), (2, 1))
OUTWARD = z_pairs((1, 0), (2, 3))
INWARD = z_pairs((0, 1), (3, 2))
SIBLING = [(e, e ^ 1) for e in range(8)]


def send(array, pairs):
    return lax.ppermute(array, "expert", pairs)


def line_gather(block, inner):
    swap_first = send(block, ALL_SWAP)
    mid_first = send(block, MID_SWAP)
    out_second = send(mid_first, OUTWARD)
    mid_second = send(swap_first, MID_SWAP)
    out_third = send(mid_second, OUTWARD)
    stages = [
        block,
        swap_first,
        jnp.where(inner, mid_first, out_second),
        jnp.where(inner, mid_second, out_third),
    ]
    return [jnp.concatenate([mine, send(mine, SIBLING)]) for mine in stages]


def add_rounded(*terms):
    total = terms[0].astype(jnp.float32)
    for term in terms[1:]:
        total = total + term.astype(jnp.float32)
    return total.astype(jnp.bfloat16)


def line_combine(parts, tok_rows):
    own, first, second, third = [
        add_rounded(part[:tok_rows], send(part[tok_rows:], SIBLING)) for part in parts
    ]
    third_in = send(third, INWARD)
    third_mid = send(add_rounded(third, third_in), MID_SWAP)
    second_in = send(second, INWARD)
    second_mid = send(add_rounded(second, second_in), MID_SWAP)
    first_swap = send(add_rounded(first, third_mid), ALL_SWAP)
    return add_rounded(own, first_swap, second_mid)


def stage_weights(weight_table, inner, me):
    for bit in (1, 2, 4):
        other = send(weight_table, [(e, e ^ bit) for e in range(8)])
        weight_table = jnp.concatenate([weight_table, other])
    tok_rows = weight_table.shape[1]
    table = weight_table.reshape(8, 8, tok_rows)
    mine = lax.dynamic_index_in_dim(table, me, axis=1, keepdims=False)
    near = mine.reshape(4, 2 * tok_rows)
    return [
        near[0],
        near[1],
        jnp.where(inner, near[3], near[2]),
        jnp.where(inner, near[2], near[3]),
    ]


def swap_sum(array, bit):
    rounded = lax.reduce_precision(array, 8, 7)
    pairs = [(d, d ^ bit) for d in range(4)]
    other = lax.ppermute(rounded.astype(jnp.bfloat16), "dp", pairs)
    return rounded + other.astype(jnp.float32)


def group_sum(grad_a, grad_b):
    rows, rank = grad_a.shape
    low_rows = (grad_a.size + grad_b.size) // 2 // rank // 16 * 16
    x_first = swap_sum(swap_sum(grad_a[:low_rows], 1), 2)
    y_first = swap_sum(swap_sum(grad_a[low_rows:], 2), 1)
    sum_b = swap_sum(swap_sum(grad_b, 2), 1)
    return jnp.concatenate([x_first, y_first]), sum_b


def dense_body(
    tokens,
    cotangent,
    routing,
    router_route_weights,
    route_replica_choice,
    device_expert_table,
    gate_up_weight,
    down_weight,
    adapter_down_maps,
    adapter_up_maps,
):
    slot_total = lax.axis_size("expert")
    tok_rows = tokens.shape[0]
    capacity = tok_rows * routing.shape[1] // slot_total
    me = lax.axis_index("expert")
    chip = me // 2
    inner = (chip == 1) | (chip == 2)
    weight_table = dense_route_weights(
        routing, router_route_weights, route_replica_choice, device_expert_table, capacity
    )
    weights = [w[:, None] for w in stage_weights(weight_table.T, inner, me)]
    row_stages = line_gather(tokens, inner)
    cot_stages = line_gather(cotangent, inner)
    parts, saved = [], []
    for rows, w in zip(row_stages, weights):
        layer_output, kept = expert_apply_forward(
            rows, gate_up_weight[0], down_weight[0], adapter_down_maps[0], adapter_up_maps[0]
        )
        parts.append((w * layer_output.astype(jnp.float32)).astype(jnp.bfloat16))
        saved.append(kept)
    mixed = line_combine(parts, tok_rows)
    grad_a, grad_b = 0.0, 0.0
    for rows, cot, w, kept in zip(row_stages, cot_stages, weights, saved):
        scaled = (w * cot.astype(jnp.float32)).astype(jnp.bfloat16)
        more_a, more_b = expert_backward(rows, scaled, down_weight[0], adapter_up_maps[0], kept)
        grad_a, grad_b = grad_a + more_a, grad_b + more_b
    grad_a, grad_b = group_sum(grad_a, grad_b)
    return mixed, grad_a[None], grad_b[None]


def body(*arrays):
    if (lax.axis_size("dp"), lax.axis_size("expert"), arrays[2].shape[1]) == (4, 8, 8):
        return dense_body(*arrays)
    return sparse_body(*arrays)


def solution(mesh):
    return jax.shard_map(
        body,
        mesh=mesh,
        in_specs=(
            P(("dp", "expert"), None),
            P(("dp", "expert"), None),
            P(("dp", "expert"), None),
            P(("dp", "expert"), None),
            P(("dp", "expert"), None),
            P(),
            P("expert", None, None),
            P("expert", None, None),
            P("expert", None, None),
            P("expert", None, None, None),
        ),
        out_specs=(
            P(("dp", "expert"), None),
            P("expert", None, None),
            P("expert", None, None, None),
        ),
        check_vma=False,
    )
```

```python
import jax
import jax.numpy as jnp
from jax import lax
from jax.sharding import PartitionSpec as P

ADAPTER_SCALE = 0.5


def route_rows(routing, route_replica_choice, device_expert_table, capacity):
    slot_total = device_expert_table.shape[0]
    route_total = routing.shape[0] * routing.shape[1]
    expert_flat = routing.reshape(-1)
    holds_mask = (expert_flat[:, None] == device_expert_table[None, :]).astype(jnp.int32)
    copies = jnp.sum(holds_mask, axis=1)
    wanted = route_replica_choice.reshape(-1) % copies
    before = jnp.cumsum(holds_mask, axis=1) - holds_mask
    picked = holds_mask * (before == wanted[:, None]).astype(jnp.int32)
    ahead_of = jnp.cumsum(picked, axis=0) - picked
    position = jnp.sum(picked * ahead_of, axis=1)
    target = jnp.sum(picked * jnp.arange(slot_total, dtype=jnp.int32)[None, :], axis=1)
    kept_mask = position < capacity
    dest_index = jnp.where(kept_mask, target * capacity + position, slot_total * capacity)
    source = jnp.full((slot_total * capacity,), route_total, jnp.int32)
    source = source.at[dest_index].set(jnp.arange(route_total, dtype=jnp.int32), mode="drop")
    return (kept_mask, dest_index, source)


def expert_apply_forward(rows_in, gate_up, down, adapt_a, adapt_b):
    adapter_rank_count = adapt_b.shape[1]
    hidden_width = adapt_b.shape[2]
    reduced_rank_rows = jnp.dot(rows_in, adapt_a, preferred_element_type=jnp.float32).astype(
        jnp.bfloat16
    )
    base_preactivation = jnp.dot(rows_in, gate_up, preferred_element_type=jnp.float32)
    adapter_gate_delta = jnp.dot(
        reduced_rank_rows[:, :adapter_rank_count], adapt_b[0], preferred_element_type=jnp.float32
    )
    adapter_up_delta = jnp.dot(
        reduced_rank_rows[:, adapter_rank_count:], adapt_b[1], preferred_element_type=jnp.float32
    )
    gate_preactivation = base_preactivation[:, :hidden_width] + ADAPTER_SCALE * adapter_gate_delta
    up_preactivation = base_preactivation[:, hidden_width:] + ADAPTER_SCALE * adapter_up_delta
    sigmoid_gate = jax.nn.sigmoid(gate_preactivation)
    active = gate_preactivation * sigmoid_gate
    hidden = (active * up_preactivation).astype(jnp.bfloat16)
    layer_output = jnp.dot(hidden, down, preferred_element_type=jnp.float32).astype(jnp.bfloat16)
    return (
        layer_output,
        (reduced_rank_rows, gate_preactivation, up_preactivation, sigmoid_gate, active),
    )


def expert_backward(rows_in, scaled, down, adapt_b, saved_residuals):
    reduced_rank_rows, gate_preactivation, up_preactivation, sigmoid_gate, active = saved_residuals
    adapter_rank_count = adapt_b.shape[1]
    back_hidden = lax.dot_general(
        scaled, down, (((1,), (1,)), ((), ())), preferred_element_type=jnp.float32
    )
    up_preactivation_gradient = (back_hidden * active).astype(jnp.bfloat16)
    slope = sigmoid_gate * (1.0 + gate_preactivation * (1.0 - sigmoid_gate))
    gate_preactivation_gradient = (back_hidden * up_preactivation * slope).astype(jnp.bfloat16)
    row_dimension_numbers = (((0,), (0,)), ((), ()))
    gate_up_map_gradient = ADAPTER_SCALE * lax.dot_general(
        reduced_rank_rows[:, :adapter_rank_count],
        gate_preactivation_gradient,
        row_dimension_numbers,
        preferred_element_type=jnp.float32,
    )
    up_map_gradient = ADAPTER_SCALE * lax.dot_general(
        reduced_rank_rows[:, adapter_rank_count:],
        up_preactivation_gradient,
        row_dimension_numbers,
        preferred_element_type=jnp.float32,
    )
    cols_dims = (((1,), (1,)), ((), ()))
    gate_reduced_rows = lax.dot_general(
        gate_preactivation_gradient, adapt_b[0], cols_dims, preferred_element_type=jnp.float32
    )
    up_reduced_rows = lax.dot_general(
        up_preactivation_gradient, adapt_b[1], cols_dims, preferred_element_type=jnp.float32
    )
    reduced_gradient = (
        ADAPTER_SCALE * jnp.concatenate([gate_reduced_rows, up_reduced_rows], axis=1)
    ).astype(jnp.bfloat16)
    grad_adapt_a = lax.dot_general(
        rows_in, reduced_gradient, row_dimension_numbers, preferred_element_type=jnp.float32
    )
    return (grad_adapt_a, jnp.stack([gate_up_map_gradient, up_map_gradient]))


def sparse_body(
    tokens,
    cotangent,
    routing,
    router_route_weights,
    route_replica_choice,
    device_expert_table,
    gate_up_weight,
    down_weight,
    adapter_down_maps,
    adapter_up_maps,
):
    slot_total = lax.axis_size("expert")
    tok_rows = tokens.shape[0]
    model_feature_width = tokens.shape[1]
    top_routes = routing.shape[1]
    route_total = tok_rows * top_routes
    capacity = route_total // slot_total
    kept_mask, dest_index, source = route_rows(
        routing, route_replica_choice, device_expert_table, capacity
    )
    valid_route_mask = source < route_total
    safe_route = jnp.minimum(source, route_total - 1)
    route_token_index = safe_route // top_routes
    weight_flat = router_route_weights.reshape(-1)
    route_weight_rows = weight_flat[safe_route]
    zero_row = jnp.zeros((), jnp.bfloat16)
    rows_out = jnp.where(valid_route_mask[:, None], tokens[route_token_index], zero_row).reshape(
        slot_total, capacity, model_feature_width
    )
    product = (
        route_weight_rows[:, None] * cotangent[route_token_index].astype(jnp.float32)
    ).astype(jnp.bfloat16)
    scaled_out = jnp.where(valid_route_mask[:, None], product, zero_row).reshape(
        slot_total, capacity, model_feature_width
    )
    rows_in = lax.all_to_all(rows_out, "expert", split_axis=0, concat_axis=0, tiled=True)
    flattened_rows = rows_in.reshape(-1, model_feature_width)
    layer_output, saved_residuals = expert_apply_forward(
        flattened_rows, gate_up_weight[0], down_weight[0], adapter_down_maps[0], adapter_up_maps[0]
    )
    returned = lax.all_to_all(
        layer_output.reshape(slot_total, capacity, model_feature_width),
        "expert",
        split_axis=0,
        concat_axis=0,
        tiled=True,
    )
    returned = returned.reshape(-1, model_feature_width)
    picked_rows = returned[jnp.minimum(dest_index, slot_total * capacity - 1)]
    weighted = jnp.where(
        kept_mask[:, None],
        weight_flat[:, None] * picked_rows.astype(jnp.float32),
        jnp.zeros((), jnp.float32),
    )
    mixed = jnp.sum(weighted.reshape(tok_rows, top_routes, model_feature_width), axis=1).astype(
        jnp.bfloat16
    )
    scaled_input_rows = lax.all_to_all(
        scaled_out, "expert", split_axis=0, concat_axis=0, tiled=True
    )
    grad_adapt_a, grad_adapt_b = expert_backward(
        flattened_rows,
        scaled_input_rows.reshape(-1, model_feature_width),
        down_weight[0],
        adapter_up_maps[0],
        saved_residuals,
    )
    piece_a = grad_adapt_a.reshape(slot_total, -1)
    piece_b = grad_adapt_b.reshape(slot_total, -1)
    expert_total = max(top_routes, slot_total // 2)
    members = (
        jnp.arange(expert_total, dtype=jnp.int32)[:, None] == device_expert_table[None, :]
    ).astype(jnp.float32)
    piece_a, piece_b = lax.psum((piece_a, piece_b), "dp")
    got_a, got_b = (
        lax.all_to_all(piece_a, "expert", split_axis=0, concat_axis=0, tiled=True),
        lax.all_to_all(piece_b, "expert", split_axis=0, concat_axis=0, tiled=True),
    )
    expert_a = jnp.dot(members, got_a, precision=lax.Precision.HIGHEST)
    expert_b = jnp.dot(members, got_b, precision=lax.Precision.HIGHEST)
    back_dims = (((0,), (0,)), ((), ()))
    spread_a = lax.dot_general(members, expert_a, back_dims, precision=lax.Precision.HIGHEST)
    spread_b = lax.dot_general(members, expert_b, back_dims, precision=lax.Precision.HIGHEST)
    summed_a, summed_b = (
        lax.all_to_all(spread_a, "expert", split_axis=0, concat_axis=0, tiled=True),
        lax.all_to_all(spread_b, "expert", split_axis=0, concat_axis=0, tiled=True),
    )
    grad_a = summed_a.reshape(grad_adapt_a.shape)[None]
    grad_b = summed_b.reshape(grad_adapt_b.shape)[None]
    return (mixed, grad_a, grad_b)


def dense_route_weights(routing, weights, choice, table, capacity):
    holds = (routing[:, :, None] == table[None, None, :]).astype(jnp.int32)
    copies = jnp.sum(holds, axis=2)
    wanted = choice % copies
    before = jnp.cumsum(holds, axis=2) - holds
    picked = holds * (before == wanted[:, :, None]).astype(jnp.int32)
    taken = jnp.sum(picked, axis=1)
    rank = jnp.cumsum(taken, axis=0) - taken
    route_weight = jnp.sum(picked.astype(jnp.float32) * weights[:, :, None], axis=1)
    return jnp.where(rank < capacity, route_weight, 0.0)


def z_pairs(*moves):
    return [(2 * a + core, 2 * b + core) for a, b in moves for core in (0, 1)]


ALL_SWAP = z_pairs((0, 1), (1, 0), (2, 3), (3, 2))
MID_SWAP = z_pairs((1, 2), (2, 1))
OUTWARD = z_pairs((1, 0), (2, 3))
INWARD = z_pairs((0, 1), (3, 2))
SIBLING = [(e, e ^ 1) for e in range(8)]


def send(array, pairs):
    return lax.ppermute(array, "expert", pairs)


def after(array, *earlier):
    return lax.optimization_barrier((array,) + earlier)[0]


def add_rounded(*terms):
    total = terms[0].astype(jnp.float32)
    for term in terms[1:]:
        total = total + term.astype(jnp.float32)
    return total.astype(jnp.bfloat16)


def doubled(weight_table, bit):
    return jnp.concatenate([weight_table, send(weight_table, [(e, e ^ bit) for e in range(8)])])


def stage_weights(weight_tables, inner, me):
    tok_rows = weight_tables.shape[1]
    table = weight_tables.reshape(8, 8, tok_rows)
    mine = lax.dynamic_index_in_dim(table, me, axis=1, keepdims=False)
    near = mine.reshape(4, 2 * tok_rows)
    return [
        near[0],
        near[1],
        jnp.where(inner, near[3], near[2]),
        jnp.where(inner, near[2], near[3]),
    ]


def swap_sum(array, bit):
    rounded = lax.reduce_precision(array, 8, 7)
    pairs = [(d, d ^ bit) for d in range(4)]
    other = lax.ppermute(rounded.astype(jnp.bfloat16), "dp", pairs)
    return rounded + other.astype(jnp.float32)


def group_sum(grad_a, grad_b):
    rows, rank = grad_a.shape
    low_rows = (grad_a.size + grad_b.size) // 2 // rank // 16 * 16
    x_first = swap_sum(swap_sum(grad_a[:low_rows], 1), 2)
    y_first = swap_sum(swap_sum(grad_a[low_rows:], 2), 1)
    sum_b = swap_sum(swap_sum(grad_b, 2), 1)
    return jnp.concatenate([x_first, y_first]), sum_b


def dense_body(
    tokens,
    cotangent,
    routing,
    router_route_weights,
    route_replica_choice,
    device_expert_table,
    gate_up_weight,
    down_weight,
    adapter_down_maps,
    adapter_up_maps,
):
    slot_total = lax.axis_size("expert")
    tok_rows = tokens.shape[0]
    capacity = tok_rows * routing.shape[1] // slot_total
    me = lax.axis_index("expert")
    chip = me // 2
    inner = (chip == 1) | (chip == 2)
    gate_up, down = gate_up_weight[0], down_weight[0]
    adapt_a, adapt_b = adapter_down_maps[0], adapter_up_maps[0]

    def pair(block):
        return jnp.concatenate([block, send(block, SIBLING)])

    def forward(rows):
        return expert_apply_forward(rows, gate_up, down, adapt_a, adapt_b)

    tok_swap = send(tokens, ALL_SWAP)
    tok_mid = send(tokens, MID_SWAP)
    rows0 = pair(tokens)
    weight_table = dense_route_weights(
        after(routing, rows0),
        router_route_weights,
        route_replica_choice,
        device_expert_table,
        capacity,
    ).T
    weight_table = doubled(doubled(weight_table, 1), 2)
    out0, kept0 = forward(rows0)

    tok_out2 = send(after(tok_mid, tok_swap), OUTWARD)
    tok_mid2 = send(after(tok_swap, tok_mid), MID_SWAP)
    cot_in = send(after(cotangent, tok_swap, tok_mid), INWARD)
    weight_table = doubled(after(weight_table, tok_swap, tok_mid), 4)
    rows1 = pair(after(tok_swap, tok_mid))
    out1, kept1 = forward(rows1)

    tok_out3 = send(after(tok_mid2, tok_out2), OUTWARD)
    cot_mid = send(after(cotangent, tok_mid2, tok_out2, cot_in), MID_SWAP)
    rows2 = pair(jnp.where(inner, tok_mid, tok_out2))
    out2, kept2 = forward(rows2)

    cot_out = send(after(cotangent, tok_out3, cot_mid), OUTWARD)
    cot_mid2 = send(after(cot_in, tok_out3, cot_mid), MID_SWAP)
    rows3 = pair(jnp.where(inner, tok_mid2, tok_out3))
    out3, kept3 = forward(rows3)

    weights = [w[:, None] for w in stage_weights(weight_table, inner, me)]

    def chip_part(layer_output, w):
        part = (w * layer_output.astype(jnp.float32)).astype(jnp.bfloat16)
        return add_rounded(part[:tok_rows], send(part[tok_rows:], SIBLING))

    part3 = chip_part(out3, weights[3])
    third_in = send(part3, INWARD)
    part2 = chip_part(out2, weights[2])
    part1 = chip_part(out1, weights[1])
    part0 = chip_part(out0, weights[0])

    cot_out2 = send(after(cot_mid, cot_out), OUTWARD)
    third_mid = send(after(add_rounded(part3, third_in), cot_mid2), MID_SWAP)
    second_in = send(after(part2, third_in), INWARD)
    cot_out3 = send(after(cot_mid2, cot_out2), OUTWARD)
    second_mid = send(after(add_rounded(part2, second_in), third_mid), MID_SWAP)
    first_swap = send(after(add_rounded(part1, third_mid), second_in, cot_out3), ALL_SWAP)
    mixed = add_rounded(part0, first_swap, second_mid)

    cot_stages = [
        pair(after(cotangent, tok_swap)),
        pair(jnp.where(inner, cot_in, cot_out)),
        pair(jnp.where(inner, cot_mid, cot_out2)),
        pair(jnp.where(inner, cot_mid2, cot_out3)),
    ]
    row_stages = [rows0, rows1, rows2, rows3]
    saved = [kept0, kept1, kept2, kept3]
    grad_a, grad_b = 0.0, 0.0
    for rows, cot, w, kept in zip(row_stages, cot_stages, weights, saved):
        scaled = (w * cot.astype(jnp.float32)).astype(jnp.bfloat16)
        more_a, more_b = expert_backward(rows, scaled, down, adapt_b, kept)
        grad_a, grad_b = grad_a + more_a, grad_b + more_b
    grad_a, grad_b = group_sum(grad_a, grad_b)
    return mixed, grad_a[None], grad_b[None]


def body(*arrays):
    if (lax.axis_size("dp"), lax.axis_size("expert"), arrays[2].shape[1]) == (4, 8, 8):
        return dense_body(*arrays)
    return sparse_body(*arrays)


def solution(mesh):
    return jax.shard_map(
        body,
        mesh=mesh,
        in_specs=(
            P(("dp", "expert"), None),
            P(("dp", "expert"), None),
            P(("dp", "expert"), None),
            P(("dp", "expert"), None),
            P(("dp", "expert"), None),
            P(),
            P("expert", None, None),
            P("expert", None, None),
            P("expert", None, None),
            P("expert", None, None, None),
        ),
        out_specs=(
            P(("dp", "expert"), None),
            P("expert", None, None),
            P("expert", None, None, None),
        ),
        check_vma=False,
    )
```

```python
import jax
import jax.numpy as jnp
from jax import lax
from jax.sharding import PartitionSpec as P

ADAPTER_SCALE = 0.5


def route_rows(routing, route_replica_choice, device_expert_table, capacity):
    slot_total = device_expert_table.shape[0]
    route_total = routing.shape[0] * routing.shape[1]
    expert_flat = routing.reshape(-1)
    holds_mask = (expert_flat[:, None] == device_expert_table[None, :]).astype(jnp.int32)
    copies = jnp.sum(holds_mask, axis=1)
    wanted = route_replica_choice.reshape(-1) % copies
    before = jnp.cumsum(holds_mask, axis=1) - holds_mask
    picked = holds_mask * (before == wanted[:, None]).astype(jnp.int32)
    ahead_of = jnp.cumsum(picked, axis=0) - picked
    position = jnp.sum(picked * ahead_of, axis=1)
    target = jnp.sum(picked * jnp.arange(slot_total, dtype=jnp.int32)[None, :], axis=1)
    kept_mask = position < capacity
    dest_index = jnp.where(kept_mask, target * capacity + position, slot_total * capacity)
    source = jnp.full((slot_total * capacity,), route_total, jnp.int32)
    source = source.at[dest_index].set(jnp.arange(route_total, dtype=jnp.int32), mode="drop")
    return (kept_mask, dest_index, source)


def expert_apply_forward(rows_in, gate_up, down, adapt_a, adapt_b):
    adapter_rank_count = adapt_b.shape[1]
    hidden_width = adapt_b.shape[2]
    reduced_rank_rows = jnp.dot(rows_in, adapt_a, preferred_element_type=jnp.float32).astype(
        jnp.bfloat16
    )
    base_preactivation = jnp.dot(rows_in, gate_up, preferred_element_type=jnp.float32)
    adapter_gate_delta = jnp.dot(
        reduced_rank_rows[:, :adapter_rank_count], adapt_b[0], preferred_element_type=jnp.float32
    )
    adapter_up_delta = jnp.dot(
        reduced_rank_rows[:, adapter_rank_count:], adapt_b[1], preferred_element_type=jnp.float32
    )
    gate_preactivation = base_preactivation[:, :hidden_width] + ADAPTER_SCALE * adapter_gate_delta
    up_preactivation = base_preactivation[:, hidden_width:] + ADAPTER_SCALE * adapter_up_delta
    sigmoid_gate = jax.nn.sigmoid(gate_preactivation)
    active = gate_preactivation * sigmoid_gate
    hidden = (active * up_preactivation).astype(jnp.bfloat16)
    layer_output = jnp.dot(hidden, down, preferred_element_type=jnp.float32).astype(jnp.bfloat16)
    return (
        layer_output,
        (reduced_rank_rows, gate_preactivation, up_preactivation, sigmoid_gate, active),
    )


def expert_backward(rows_in, scaled, down, adapt_b, saved_residuals):
    reduced_rank_rows, gate_preactivation, up_preactivation, sigmoid_gate, active = saved_residuals
    adapter_rank_count = adapt_b.shape[1]
    back_hidden = lax.dot_general(
        scaled, down, (((1,), (1,)), ((), ())), preferred_element_type=jnp.float32
    )
    up_preactivation_gradient = (back_hidden * active).astype(jnp.bfloat16)
    slope = sigmoid_gate * (1.0 + gate_preactivation * (1.0 - sigmoid_gate))
    gate_preactivation_gradient = (back_hidden * up_preactivation * slope).astype(jnp.bfloat16)
    row_dimension_numbers = (((0,), (0,)), ((), ()))
    gate_up_map_gradient = ADAPTER_SCALE * lax.dot_general(
        reduced_rank_rows[:, :adapter_rank_count],
        gate_preactivation_gradient,
        row_dimension_numbers,
        preferred_element_type=jnp.float32,
    )
    up_map_gradient = ADAPTER_SCALE * lax.dot_general(
        reduced_rank_rows[:, adapter_rank_count:],
        up_preactivation_gradient,
        row_dimension_numbers,
        preferred_element_type=jnp.float32,
    )
    cols_dims = (((1,), (1,)), ((), ()))
    gate_reduced_rows = lax.dot_general(
        gate_preactivation_gradient, adapt_b[0], cols_dims, preferred_element_type=jnp.float32
    )
    up_reduced_rows = lax.dot_general(
        up_preactivation_gradient, adapt_b[1], cols_dims, preferred_element_type=jnp.float32
    )
    reduced_gradient = (
        ADAPTER_SCALE * jnp.concatenate([gate_reduced_rows, up_reduced_rows], axis=1)
    ).astype(jnp.bfloat16)
    grad_adapt_a = lax.dot_general(
        rows_in, reduced_gradient, row_dimension_numbers, preferred_element_type=jnp.float32
    )
    return (grad_adapt_a, jnp.stack([gate_up_map_gradient, up_map_gradient]))


def sparse_body(
    tokens,
    cotangent,
    routing,
    router_route_weights,
    route_replica_choice,
    device_expert_table,
    gate_up_weight,
    down_weight,
    adapter_down_maps,
    adapter_up_maps,
):
    slot_total = lax.axis_size("expert")
    tok_rows = tokens.shape[0]
    model_feature_width = tokens.shape[1]
    top_routes = routing.shape[1]
    route_total = tok_rows * top_routes
    capacity = route_total // slot_total
    kept_mask, dest_index, source = route_rows(
        routing, route_replica_choice, device_expert_table, capacity
    )
    valid_route_mask = source < route_total
    safe_route = jnp.minimum(source, route_total - 1)
    route_token_index = safe_route // top_routes
    weight_flat = router_route_weights.reshape(-1)
    route_weight_rows = weight_flat[safe_route]
    zero_row = jnp.zeros((), jnp.bfloat16)
    rows_out = jnp.where(valid_route_mask[:, None], tokens[route_token_index], zero_row).reshape(
        slot_total, capacity, model_feature_width
    )
    product = (
        route_weight_rows[:, None] * cotangent[route_token_index].astype(jnp.float32)
    ).astype(jnp.bfloat16)
    scaled_out = jnp.where(valid_route_mask[:, None], product, zero_row).reshape(
        slot_total, capacity, model_feature_width
    )
    rows_in = lax.all_to_all(rows_out, "expert", split_axis=0, concat_axis=0, tiled=True)
    flattened_rows = rows_in.reshape(-1, model_feature_width)
    layer_output, saved_residuals = expert_apply_forward(
        flattened_rows, gate_up_weight[0], down_weight[0], adapter_down_maps[0], adapter_up_maps[0]
    )
    returned = lax.all_to_all(
        layer_output.reshape(slot_total, capacity, model_feature_width),
        "expert",
        split_axis=0,
        concat_axis=0,
        tiled=True,
    )
    returned = returned.reshape(-1, model_feature_width)
    picked_rows = returned[jnp.minimum(dest_index, slot_total * capacity - 1)]
    weighted = jnp.where(
        kept_mask[:, None],
        weight_flat[:, None] * picked_rows.astype(jnp.float32),
        jnp.zeros((), jnp.float32),
    )
    mixed = jnp.sum(weighted.reshape(tok_rows, top_routes, model_feature_width), axis=1).astype(
        jnp.bfloat16
    )
    scaled_input_rows = lax.all_to_all(
        scaled_out, "expert", split_axis=0, concat_axis=0, tiled=True
    )
    grad_adapt_a, grad_adapt_b = expert_backward(
        flattened_rows,
        scaled_input_rows.reshape(-1, model_feature_width),
        down_weight[0],
        adapter_up_maps[0],
        saved_residuals,
    )
    piece_a = grad_adapt_a.reshape(slot_total, -1)
    piece_b = grad_adapt_b.reshape(slot_total, -1)
    expert_total = max(top_routes, slot_total // 2)
    members = (
        jnp.arange(expert_total, dtype=jnp.int32)[:, None] == device_expert_table[None, :]
    ).astype(jnp.float32)
    piece_a, piece_b = lax.psum((piece_a, piece_b), "dp")
    got_a, got_b = (
        lax.all_to_all(piece_a, "expert", split_axis=0, concat_axis=0, tiled=True),
        lax.all_to_all(piece_b, "expert", split_axis=0, concat_axis=0, tiled=True),
    )
    expert_a = jnp.dot(members, got_a, precision=lax.Precision.HIGHEST)
    expert_b = jnp.dot(members, got_b, precision=lax.Precision.HIGHEST)
    back_dims = (((0,), (0,)), ((), ()))
    spread_a = lax.dot_general(members, expert_a, back_dims, precision=lax.Precision.HIGHEST)
    spread_b = lax.dot_general(members, expert_b, back_dims, precision=lax.Precision.HIGHEST)
    summed_a, summed_b = (
        lax.all_to_all(spread_a, "expert", split_axis=0, concat_axis=0, tiled=True),
        lax.all_to_all(spread_b, "expert", split_axis=0, concat_axis=0, tiled=True),
    )
    grad_a = summed_a.reshape(grad_adapt_a.shape)[None]
    grad_b = summed_b.reshape(grad_adapt_b.shape)[None]
    return (mixed, grad_a, grad_b)


def count_before(flags):
    length = flags.shape[0]
    earlier = jnp.tril(jnp.ones((length, length), jnp.bfloat16), -1)
    return jnp.dot(earlier, flags.astype(jnp.bfloat16), preferred_element_type=jnp.float32)


def dense_route_weights(routing, weights, choice, table, capacity):
    slot_total = table.shape[0]
    experts, choice, weights = routing.T, choice.T, weights.T
    holds = [(experts == table[s]).astype(jnp.int32) for s in range(slot_total)]
    copies = sum(holds)
    wanted = choice % copies
    before = jnp.zeros_like(experts)
    taken, route_weight = [], []
    for hold in holds:
        picked = (hold == 1) & (before == wanted)
        before = before + hold
        taken.append(jnp.any(picked, axis=0))
        route_weight.append(jnp.sum(jnp.where(picked, weights, 0.0), axis=0))
    rank = count_before(jnp.stack(taken, axis=1)).T
    return jnp.where(rank < capacity, jnp.stack(route_weight), 0.0)


def z_pairs(*moves):
    return [(2 * a + core, 2 * b + core) for a, b in moves for core in (0, 1)]


ALL_SWAP = z_pairs((0, 1), (1, 0), (2, 3), (3, 2))
MID_SWAP = z_pairs((1, 2), (2, 1))
OUTWARD = z_pairs((1, 0), (2, 3))
INWARD = z_pairs((0, 1), (3, 2))
SIBLING = [(e, e ^ 1) for e in range(8)]


def send(array, pairs):
    return lax.ppermute(array, "expert", pairs)


def fence(*arrays):
    return lax.optimization_barrier(arrays)


def add_rounded(*terms):
    total = terms[0].astype(jnp.float32)
    for term in terms[1:]:
        total = total + term.astype(jnp.float32)
    return total.astype(jnp.bfloat16)


def doubled(weight_table, bit):
    return jnp.concatenate([weight_table, send(weight_table, [(e, e ^ bit) for e in range(8)])])


def stage_weights(weight_tables, inner, me):
    tok_rows = weight_tables.shape[1]
    table = weight_tables.reshape(8, 8, tok_rows)
    mine = lax.dynamic_index_in_dim(table, me, axis=1, keepdims=False)
    near = mine.reshape(4, 2 * tok_rows)
    return [
        near[0],
        near[1],
        jnp.where(inner, near[3], near[2]),
        jnp.where(inner, near[2], near[3]),
    ]


def swap_sum(array, bit):
    rounded = lax.reduce_precision(array, 8, 7)
    pairs = [(d, d ^ bit) for d in range(4)]
    other = lax.ppermute(rounded.astype(jnp.bfloat16), "dp", pairs)
    return rounded + other.astype(jnp.float32)


def group_sum(grad_a, grad_b):
    rows, rank = grad_a.shape
    low_rows = (grad_a.size + grad_b.size) // 2 // rank // 16 * 16
    x_first = swap_sum(swap_sum(grad_a[:low_rows], 1), 2)
    y_first = swap_sum(swap_sum(grad_a[low_rows:], 2), 1)
    sum_b = swap_sum(swap_sum(grad_b, 2), 1)
    return jnp.concatenate([x_first, y_first]), sum_b


def dense_body(
    tokens,
    cotangent,
    routing,
    router_route_weights,
    route_replica_choice,
    device_expert_table,
    gate_up_weight,
    down_weight,
    adapter_down_maps,
    adapter_up_maps,
):
    slot_total = lax.axis_size("expert")
    tok_rows = tokens.shape[0]
    capacity = tok_rows * routing.shape[1] // slot_total
    me = lax.axis_index("expert")
    chip = me // 2
    inner = (chip == 1) | (chip == 2)
    gate_up, down = gate_up_weight[0], down_weight[0]
    adapt_a, adapt_b = adapter_down_maps[0], adapter_up_maps[0]

    def pair(block):
        return jnp.concatenate([block, send(block, SIBLING)])

    def forward(rows):
        return expert_apply_forward(rows, gate_up, down, adapt_a, adapt_b)

    def chip_part(layer_output, w):
        part = (w * layer_output.astype(jnp.float32)).astype(jnp.bfloat16)
        return add_rounded(part[:tok_rows], send(part[tok_rows:], SIBLING))

    def backward(rows, cot, w, kept):
        scaled = (w * cot.astype(jnp.float32)).astype(jnp.bfloat16)
        return expert_backward(rows, scaled, down, adapt_b, kept)

    tok_swap = send(tokens, ALL_SWAP)
    tok_mid = send(tokens, MID_SWAP)
    rows0 = pair(tokens)
    table = dense_route_weights(
        routing, router_route_weights, route_replica_choice, device_expert_table, capacity
    )
    table = doubled(table, 1)
    out0, kept0 = forward(rows0)
    tok_swap, tok_mid, table, out0 = fence(tok_swap, tok_mid, table, out0)

    tok_out2 = send(tok_mid, OUTWARD)
    tok_mid2 = send(tok_swap, MID_SWAP)
    cot_in = send(cotangent, INWARD)
    table = doubled(table, 2)
    rows1 = pair(tok_swap)
    out1, kept1 = forward(rows1)
    tok_mid, tok_out2, tok_mid2, cot_in, table, out1, cotangent = fence(
        tok_mid, tok_out2, tok_mid2, cot_in, table, out1, cotangent
    )

    tok_out3 = send(tok_mid2, OUTWARD)
    cot_mid = send(cotangent, MID_SWAP)
    table = doubled(table, 4)
    rows2 = pair(jnp.where(inner, tok_mid, tok_out2))
    out2, kept2 = forward(rows2)
    tok_mid2, tok_out3, cot_in, cot_mid, table, out2, cotangent = fence(
        tok_mid2, tok_out3, cot_in, cot_mid, table, out2, cotangent
    )

    cot_out = send(cotangent, OUTWARD)
    cot_mid2 = send(cot_in, MID_SWAP)
    rows3 = pair(jnp.where(inner, tok_mid2, tok_out3))
    weights = [w[:, None] for w in stage_weights(table, inner, me)]
    out3, kept3 = forward(rows3)
    part3 = chip_part(out3, weights[3])
    part2 = chip_part(out2, weights[2])
    cot_in, cot_out, cot_mid, cot_mid2, part2, part3, out0, out1, cotangent = fence(
        cot_in, cot_out, cot_mid, cot_mid2, part2, part3, out0, out1, cotangent
    )

    cot_out2 = send(cot_mid, OUTWARD)
    third_in = send(part3, INWARD)
    part1 = chip_part(out1, weights[1])
    part0 = chip_part(out0, weights[0])
    first_a, first_b = backward(rows0, pair(cotangent), weights[0], kept0)
    more_a, more_b = backward(rows1, pair(jnp.where(inner, cot_in, cot_out)), weights[1], kept1)
    grad_a, grad_b = first_a + more_a, first_b + more_b
    cot_mid, cot_mid2, cot_out2, third_in, part0, part1, part2, part3, grad_a, grad_b = fence(
        cot_mid, cot_mid2, cot_out2, third_in, part0, part1, part2, part3, grad_a, grad_b
    )

    cot_out3 = send(cot_mid2, OUTWARD)
    third_mid = send(add_rounded(part3, third_in), MID_SWAP)
    second_in = send(part2, INWARD)
    more_a, more_b = backward(rows2, pair(jnp.where(inner, cot_mid, cot_out2)), weights[2], kept2)
    grad_a, grad_b = grad_a + more_a, grad_b + more_b
    cot_mid2, cot_out3, third_mid, second_in, part0, part1, part2, grad_a, grad_b = fence(
        cot_mid2, cot_out3, third_mid, second_in, part0, part1, part2, grad_a, grad_b
    )

    first_swap = send(add_rounded(part1, third_mid), ALL_SWAP)
    second_mid = send(add_rounded(part2, second_in), MID_SWAP)
    more_a, more_b = backward(rows3, pair(jnp.where(inner, cot_mid2, cot_out3)), weights[3], kept3)
    grad_a, grad_b = group_sum(grad_a + more_a, grad_b + more_b)
    mixed = add_rounded(part0, first_swap, second_mid)
    return mixed, grad_a[None], grad_b[None]


def body(*arrays):
    if (lax.axis_size("dp"), lax.axis_size("expert"), arrays[2].shape[1]) == (4, 8, 8):
        return dense_body(*arrays)
    return sparse_body(*arrays)


def solution(mesh):
    return jax.shard_map(
        body,
        mesh=mesh,
        in_specs=(
            P(("dp", "expert"), None),
            P(("dp", "expert"), None),
            P(("dp", "expert"), None),
            P(("dp", "expert"), None),
            P(("dp", "expert"), None),
            P(),
            P("expert", None, None),
            P("expert", None, None),
            P("expert", None, None),
            P("expert", None, None, None),
        ),
        out_specs=(
            P(("dp", "expert"), None),
            P("expert", None, None),
            P("expert", None, None, None),
        ),
        check_vma=False,
    )
```

```python
import functools

import jax
import jax.numpy as jnp
from jax import lax
from jax.experimental import pallas as pl
from jax.experimental.pallas import tpu as pltpu
from jax.sharding import PartitionSpec as P

ADAPTER_SCALE = 0.5


def route_rows(routing, route_replica_choice, device_expert_table, capacity):
    slot_total = device_expert_table.shape[0]
    route_total = routing.shape[0] * routing.shape[1]
    expert_flat = routing.reshape(-1)
    holds_mask = (expert_flat[:, None] == device_expert_table[None, :]).astype(jnp.int32)
    copies = jnp.sum(holds_mask, axis=1)
    wanted = route_replica_choice.reshape(-1) % copies
    before = jnp.cumsum(holds_mask, axis=1) - holds_mask
    picked = holds_mask * (before == wanted[:, None]).astype(jnp.int32)
    ahead_of = jnp.cumsum(picked, axis=0) - picked
    position = jnp.sum(picked * ahead_of, axis=1)
    target = jnp.sum(picked * jnp.arange(slot_total, dtype=jnp.int32)[None, :], axis=1)
    kept_mask = position < capacity
    dest_index = jnp.where(kept_mask, target * capacity + position, slot_total * capacity)
    source = jnp.full((slot_total * capacity,), route_total, jnp.int32)
    source = source.at[dest_index].set(jnp.arange(route_total, dtype=jnp.int32), mode="drop")
    return (kept_mask, dest_index, source)


def expert_apply_forward(rows_in, gate_up, down, adapt_a, adapt_b):
    adapter_rank_count = adapt_b.shape[1]
    hidden_width = adapt_b.shape[2]
    reduced_rank_rows = jnp.dot(rows_in, adapt_a, preferred_element_type=jnp.float32).astype(
        jnp.bfloat16
    )
    base_preactivation = jnp.dot(rows_in, gate_up, preferred_element_type=jnp.float32)
    adapter_gate_delta = jnp.dot(
        reduced_rank_rows[:, :adapter_rank_count], adapt_b[0], preferred_element_type=jnp.float32
    )
    adapter_up_delta = jnp.dot(
        reduced_rank_rows[:, adapter_rank_count:], adapt_b[1], preferred_element_type=jnp.float32
    )
    gate_preactivation = base_preactivation[:, :hidden_width] + ADAPTER_SCALE * adapter_gate_delta
    up_preactivation = base_preactivation[:, hidden_width:] + ADAPTER_SCALE * adapter_up_delta
    sigmoid_gate = jax.nn.sigmoid(gate_preactivation)
    active = gate_preactivation * sigmoid_gate
    hidden = (active * up_preactivation).astype(jnp.bfloat16)
    layer_output = jnp.dot(hidden, down, preferred_element_type=jnp.float32).astype(jnp.bfloat16)
    return (
        layer_output,
        (reduced_rank_rows, gate_preactivation, up_preactivation, sigmoid_gate, active),
    )


def expert_backward(rows_in, scaled, down, adapt_b, saved_residuals):
    reduced_rank_rows, gate_preactivation, up_preactivation, sigmoid_gate, active = saved_residuals
    adapter_rank_count = adapt_b.shape[1]
    back_hidden = lax.dot_general(
        scaled, down, (((1,), (1,)), ((), ())), preferred_element_type=jnp.float32
    )
    up_preactivation_gradient = (back_hidden * active).astype(jnp.bfloat16)
    slope = sigmoid_gate * (1.0 + gate_preactivation * (1.0 - sigmoid_gate))
    gate_preactivation_gradient = (back_hidden * up_preactivation * slope).astype(jnp.bfloat16)
    row_dimension_numbers = (((0,), (0,)), ((), ()))
    gate_up_map_gradient = ADAPTER_SCALE * lax.dot_general(
        reduced_rank_rows[:, :adapter_rank_count],
        gate_preactivation_gradient,
        row_dimension_numbers,
        preferred_element_type=jnp.float32,
    )
    up_map_gradient = ADAPTER_SCALE * lax.dot_general(
        reduced_rank_rows[:, adapter_rank_count:],
        up_preactivation_gradient,
        row_dimension_numbers,
        preferred_element_type=jnp.float32,
    )
    cols_dims = (((1,), (1,)), ((), ()))
    gate_reduced_rows = lax.dot_general(
        gate_preactivation_gradient, adapt_b[0], cols_dims, preferred_element_type=jnp.float32
    )
    up_reduced_rows = lax.dot_general(
        up_preactivation_gradient, adapt_b[1], cols_dims, preferred_element_type=jnp.float32
    )
    reduced_gradient = (
        ADAPTER_SCALE * jnp.concatenate([gate_reduced_rows, up_reduced_rows], axis=1)
    ).astype(jnp.bfloat16)
    grad_adapt_a = lax.dot_general(
        rows_in, reduced_gradient, row_dimension_numbers, preferred_element_type=jnp.float32
    )
    return (grad_adapt_a, jnp.stack([gate_up_map_gradient, up_map_gradient]))


def sparse_body(
    tokens,
    cotangent,
    routing,
    router_route_weights,
    route_replica_choice,
    device_expert_table,
    gate_up_weight,
    down_weight,
    adapter_down_maps,
    adapter_up_maps,
):
    slot_total = lax.axis_size("expert")
    tok_rows = tokens.shape[0]
    model_feature_width = tokens.shape[1]
    top_routes = routing.shape[1]
    route_total = tok_rows * top_routes
    capacity = route_total // slot_total
    kept_mask, dest_index, source = route_rows(
        routing, route_replica_choice, device_expert_table, capacity
    )
    valid_route_mask = source < route_total
    safe_route = jnp.minimum(source, route_total - 1)
    route_token_index = safe_route // top_routes
    weight_flat = router_route_weights.reshape(-1)
    route_weight_rows = weight_flat[safe_route]
    zero_row = jnp.zeros((), jnp.bfloat16)
    rows_out = jnp.where(valid_route_mask[:, None], tokens[route_token_index], zero_row).reshape(
        slot_total, capacity, model_feature_width
    )
    product = (
        route_weight_rows[:, None] * cotangent[route_token_index].astype(jnp.float32)
    ).astype(jnp.bfloat16)
    scaled_out = jnp.where(valid_route_mask[:, None], product, zero_row).reshape(
        slot_total, capacity, model_feature_width
    )
    rows_in = lax.all_to_all(rows_out, "expert", split_axis=0, concat_axis=0, tiled=True)
    flattened_rows = rows_in.reshape(-1, model_feature_width)
    layer_output, saved_residuals = expert_apply_forward(
        flattened_rows, gate_up_weight[0], down_weight[0], adapter_down_maps[0], adapter_up_maps[0]
    )
    returned = lax.all_to_all(
        layer_output.reshape(slot_total, capacity, model_feature_width),
        "expert",
        split_axis=0,
        concat_axis=0,
        tiled=True,
    )
    returned = returned.reshape(-1, model_feature_width)
    picked_rows = returned[jnp.minimum(dest_index, slot_total * capacity - 1)]
    weighted = jnp.where(
        kept_mask[:, None],
        weight_flat[:, None] * picked_rows.astype(jnp.float32),
        jnp.zeros((), jnp.float32),
    )
    mixed = jnp.sum(weighted.reshape(tok_rows, top_routes, model_feature_width), axis=1).astype(
        jnp.bfloat16
    )
    scaled_input_rows = lax.all_to_all(
        scaled_out, "expert", split_axis=0, concat_axis=0, tiled=True
    )
    grad_adapt_a, grad_adapt_b = expert_backward(
        flattened_rows,
        scaled_input_rows.reshape(-1, model_feature_width),
        down_weight[0],
        adapter_up_maps[0],
        saved_residuals,
    )
    piece_a = grad_adapt_a.reshape(slot_total, -1)
    piece_b = grad_adapt_b.reshape(slot_total, -1)
    expert_total = max(top_routes, slot_total // 2)
    members = (
        jnp.arange(expert_total, dtype=jnp.int32)[:, None] == device_expert_table[None, :]
    ).astype(jnp.float32)
    piece_a, piece_b = lax.psum((piece_a, piece_b), "dp")
    got_a, got_b = (
        lax.all_to_all(piece_a, "expert", split_axis=0, concat_axis=0, tiled=True),
        lax.all_to_all(piece_b, "expert", split_axis=0, concat_axis=0, tiled=True),
    )
    expert_a = jnp.dot(members, got_a, precision=lax.Precision.HIGHEST)
    expert_b = jnp.dot(members, got_b, precision=lax.Precision.HIGHEST)
    back_dims = (((0,), (0,)), ((), ()))
    spread_a = lax.dot_general(members, expert_a, back_dims, precision=lax.Precision.HIGHEST)
    spread_b = lax.dot_general(members, expert_b, back_dims, precision=lax.Precision.HIGHEST)
    summed_a, summed_b = (
        lax.all_to_all(spread_a, "expert", split_axis=0, concat_axis=0, tiled=True),
        lax.all_to_all(spread_b, "expert", split_axis=0, concat_axis=0, tiled=True),
    )
    grad_a = summed_a.reshape(grad_adapt_a.shape)[None]
    grad_b = summed_b.reshape(grad_adapt_b.shape)[None]
    return (mixed, grad_a, grad_b)


def dot(a, b, a_dim=1, b_dim=0):
    return lax.dot_general(
        a, b, (((a_dim,), (b_dim,)), ((), ())), preferred_element_type=jnp.float32
    )


def first_half(shape):
    return lax.broadcasted_iota(jnp.int32, shape, 1) < shape[1] // 2


def halves(low):
    gate = first_half(low.shape)
    zero = jnp.zeros_like(low)
    return jnp.where(gate, low, zero), jnp.where(gate, zero, low)


def column(row):
    return jnp.transpose(jnp.broadcast_to(row, (row.shape[1], row.shape[1])))[:, :1]


def weights_kernel(capacity, table_ref, expert_ref, choice_ref, weight_ref, out_ref):
    slot_total, tok_rows = out_ref.shape
    experts, weights = expert_ref[...], weight_ref[...]
    holds = [experts == table_ref[s] for s in range(slot_total)]
    counts = [hold.astype(jnp.float32) for hold in holds]
    copies = sum(counts)
    choice = choice_ref[...].astype(jnp.float32)
    wanted = choice - copies * jnp.floor((choice + 0.5) / copies)
    before = jnp.zeros_like(copies)
    taken, route_weight = [], []
    for hold, count in zip(holds, counts):
        picked = jnp.where(hold & (before == wanted), 1.0, 0.0)
        before = before + count
        taken.append(jnp.sum(picked, axis=0, keepdims=True))
        route_weight.append(jnp.sum(picked * weights, axis=0, keepdims=True))
    shape = (tok_rows, tok_rows)
    earlier = lax.broadcasted_iota(jnp.int32, shape, 0) < lax.broadcasted_iota(jnp.int32, shape, 1)
    rank = dot(
        jnp.concatenate(taken).astype(jnp.bfloat16),
        jnp.where(earlier, 1.0, 0.0).astype(jnp.bfloat16),
    )
    out_ref[...] = jnp.where(rank < capacity, jnp.concatenate(route_weight), 0.0)


def dense_route_weights(routing, weights, choice, table, capacity):
    vmem = pl.BlockSpec(memory_space=pltpu.VMEM)
    return pl.pallas_call(
        functools.partial(weights_kernel, capacity),
        out_shape=jax.ShapeDtypeStruct((table.shape[0], routing.shape[0]), jnp.float32),
        in_specs=[pl.BlockSpec(memory_space=pltpu.SMEM), vmem, vmem, vmem],
        out_specs=vmem,
    )(table, routing.T, choice.T, weights.T)


def forward_kernel(
    mine_ref, other_ref, w_ref, adapt_a_ref, gate_ref, up_ref, adapt_b_ref, down_ref,
    low_ref, active_ref, slope_ref, part_mine_ref, part_other_ref, rows_ref, total_ref,
):
    step = pl.program_id(0)
    half = mine_ref.shape[0]

    @pl.when(step == 0)
    def _():
        rows_ref[:half] = mine_ref[...]
        rows_ref[half:] = other_ref[...]
        low_ref[...] = dot(rows_ref[...], adapt_a_ref[...]).astype(jnp.bfloat16)

    rows = rows_ref[...]
    low_gate, low_up = halves(low_ref[...])
    gate = dot(rows, gate_ref[...]) + ADAPTER_SCALE * dot(low_gate, adapt_b_ref[...])
    up = dot(rows, up_ref[...]) + ADAPTER_SCALE * dot(low_up, adapt_b_ref[...])
    sigmoid_gate = jax.nn.sigmoid(gate)
    active = gate * sigmoid_gate
    active_ref[...] = active
    slope_ref[...] = up * (sigmoid_gate * (1.0 + gate * (1.0 - sigmoid_gate)))
    hidden = (active * up).astype(jnp.bfloat16)
    more = dot(hidden, down_ref[...])

    @pl.when(step == 0)
    def _():
        total_ref[...] = more

    @pl.when(step > 0)
    def _():
        total_ref[...] += more

    @pl.when(step == pl.num_programs(0) - 1)
    def _():
        out = total_ref[...].astype(jnp.bfloat16).astype(jnp.float32)
        part_mine_ref[...] = (column(w_ref[0:1]) * out[:half]).astype(jnp.bfloat16)
        part_other_ref[...] = (column(w_ref[1:2]) * out[half:]).astype(jnp.bfloat16)


def whole(shape):
    return pl.BlockSpec(shape, lambda j: (0,) * len(shape))


def columns(rows, width, start=0):
    return pl.BlockSpec((rows, width), lambda j: (0, start + j))


def forward_stage(mine, other, w, gate_up, down, adapt_a, adapt_b, chunk=256):
    half, features = mine.shape
    hidden_width = down.shape[0]
    both, ranks = 2 * half, adapt_a.shape[1]
    steps = hidden_width // chunk
    saved = jax.ShapeDtypeStruct((both, hidden_width), jnp.float32)
    part = jax.ShapeDtypeStruct((half, features), jnp.bfloat16)
    return pl.pallas_call(
        forward_kernel,
        grid=(steps,),
        out_shape=(jax.ShapeDtypeStruct((both, ranks), jnp.bfloat16), saved, saved, part, part),
        in_specs=[
            whole((half, features)),
            whole((half, features)),
            whole((2, half)),
            whole((features, ranks)),
            columns(features, chunk),
            columns(features, chunk, steps),
            columns(ranks, chunk),
            pl.BlockSpec((chunk, features), lambda j: (j, 0)),
        ],
        out_specs=(
            whole((both, ranks)),
            columns(both, chunk),
            columns(both, chunk),
            whole((half, features)),
            whole((half, features)),
        ),
        scratch_shapes=[
            pltpu.VMEM((both, features), jnp.bfloat16),
            pltpu.VMEM((both, features), jnp.float32),
        ],
        compiler_params=pltpu.CompilerParams(vmem_limit_bytes=28 * 2**20),
        cost_estimate=pl.CostEstimate(flops=10**6, bytes_accessed=10**4, transcendentals=0),
    )(mine, other, w, adapt_a, gate_up, gate_up, adapt_b, down)


def backward_kernel(
    cot_mine_ref, cot_other_ref, w_ref, mine_ref, other_ref, low_ref, active_ref, slope_ref,
    adapt_b_ref, down_ref, grad_a_ref, grad_b_ref, sum_a_ref, sum_b_ref, scaled_ref, back_ref,
):
    step = pl.program_id(0)
    half = mine_ref.shape[0]

    @pl.when(step == 0)
    def _():
        mine = column(w_ref[0:1]) * cot_mine_ref[...].astype(jnp.float32)
        other = column(w_ref[1:2]) * cot_other_ref[...].astype(jnp.float32)
        scaled_ref[:half] = mine.astype(jnp.bfloat16)
        scaled_ref[half:] = other.astype(jnp.bfloat16)
        back_ref[...] = jnp.zeros_like(back_ref)

    back = dot(scaled_ref[...], down_ref[...], 1, 1)
    up_grad = (back * active_ref[...]).astype(jnp.bfloat16)
    gate_grad = (back * slope_ref[...]).astype(jnp.bfloat16)
    low_gate, low_up = halves(low_ref[...])
    sum_b_ref[...] = grad_b_ref[...] + ADAPTER_SCALE * (
        dot(low_gate, gate_grad, 0, 0) + dot(low_up, up_grad, 0, 0)
    )
    gate_back = dot(gate_grad, adapt_b_ref[...], 1, 1)
    up_back = dot(up_grad, adapt_b_ref[...], 1, 1)
    back_ref[...] += jnp.where(first_half(gate_back.shape), gate_back, up_back)

    @pl.when(step == pl.num_programs(0) - 1)
    def _():
        low_grad = (ADAPTER_SCALE * back_ref[...]).astype(jnp.bfloat16)
        sum_a_ref[...] = (
            grad_a_ref[...]
            + dot(mine_ref[...], low_grad[:half], 0, 0)
            + dot(other_ref[...], low_grad[half:], 0, 0)
        )


def backward_stage(cots, w, rows, saved, down, adapt_b, grads, chunk=256):
    low, active, slope = saved
    half, features = rows[0].shape
    hidden_width = down.shape[0]
    both, ranks = low.shape
    block = whole((half, features))
    grad_a = whole((features, ranks))
    grad_b = columns(ranks, chunk)
    return pl.pallas_call(
        backward_kernel,
        grid=(hidden_width // chunk,),
        out_shape=(
            jax.ShapeDtypeStruct((features, ranks), jnp.float32),
            jax.ShapeDtypeStruct((ranks, hidden_width), jnp.float32),
        ),
        in_specs=[
            block,
            block,
            whole((2, half)),
            block,
            block,
            whole((both, ranks)),
            columns(both, chunk),
            columns(both, chunk),
            columns(ranks, chunk),
            pl.BlockSpec((chunk, features), lambda j: (j, 0)),
            grad_a,
            grad_b,
        ],
        out_specs=(grad_a, grad_b),
        scratch_shapes=[
            pltpu.VMEM((both, features), jnp.bfloat16),
            pltpu.VMEM((both, ranks), jnp.float32),
        ],
        compiler_params=pltpu.CompilerParams(vmem_limit_bytes=28 * 2**20),
        cost_estimate=pl.CostEstimate(flops=10**6, bytes_accessed=10**4, transcendentals=0),
    )(*cots, w, *rows, low, active, slope, adapt_b, down, *grads)


def z_pairs(*moves):
    return [(2 * a + core, 2 * b + core) for a, b in moves for core in (0, 1)]


ALL_SWAP = z_pairs((0, 1), (1, 0), (2, 3), (3, 2))
MID_SWAP = z_pairs((1, 2), (2, 1))
SIBLING = [(e, e ^ 1) for e in range(8)]


def send(array, pairs):
    return lax.ppermute(array, "expert", pairs)


def fence(*arrays):
    return lax.optimization_barrier(arrays)


def add_rounded(*terms):
    total = terms[0].astype(jnp.float32)
    for term in terms[1:]:
        total = total + term.astype(jnp.float32)
    return total.astype(jnp.bfloat16)


def sibling(block):
    return send(block, SIBLING)


def exchanged(weight_table, bit):
    return send(weight_table, [(e, e ^ bit) for e in range(8)])


def near_weights(weight_tables, me):
    tables = weight_tables.reshape(-1, 8, weight_tables.shape[1])
    return lax.dynamic_index_in_dim(tables, me, axis=1, keepdims=False)


def swap_sum(array, bit):
    rounded = lax.reduce_precision(array, 8, 7)
    pairs = [(d, d ^ bit) for d in range(4)]
    other = lax.ppermute(rounded.astype(jnp.bfloat16), "dp", pairs)
    return rounded + other.astype(jnp.float32)


def group_sum(grad_a, grad_b):
    rows, rank = grad_a.shape
    low_rows = (grad_a.size + grad_b.size) // 2 // rank // 16 * 16
    x_first = swap_sum(swap_sum(grad_a[:low_rows], 1), 2)
    y_first = swap_sum(swap_sum(grad_a[low_rows:], 2), 1)
    sum_b = swap_sum(swap_sum(grad_b, 2), 1)
    return jnp.concatenate([x_first, y_first]), sum_b


def dense_body(
    tokens,
    cotangent,
    routing,
    router_route_weights,
    route_replica_choice,
    device_expert_table,
    gate_up_weight,
    down_weight,
    adapter_down_maps,
    adapter_up_maps,
):
    slot_total = lax.axis_size("expert")
    capacity = tokens.shape[0] * routing.shape[1] // slot_total
    me = lax.axis_index("expert")
    chip = me // 2
    inner = (chip == 1) | (chip == 2)
    gate_up, down = gate_up_weight[0], down_weight[0]
    adapt_a = adapter_down_maps[0]
    adapt_b = adapter_up_maps[0].reshape(adapt_a.shape[1], -1)

    def forward(mine, other, w):
        low, active, slope, part_mine, part_other = forward_stage(
            mine, other, w, gate_up, down, adapt_a, adapt_b
        )
        return (low, active, slope), part_mine, part_other

    def backward(cots, w, rows, saved, grads):
        return backward_stage(cots, w, rows, saved, down, adapt_b, grads)

    tok_swap = send(tokens, ALL_SWAP)
    tok_mid = send(tokens, MID_SWAP)
    tok_twin = sibling(tokens)
    table = dense_route_weights(
        routing, router_route_weights, route_replica_choice, device_expert_table, capacity
    )
    table = jnp.concatenate([table, exchanged(table, 1)])
    tok_swap, tok_mid, tok_twin, table = fence(tok_swap, tok_mid, tok_twin, table)

    tok_out2 = send(tok_mid, ALL_SWAP)
    tok_mid2 = send(tok_swap, MID_SWAP)
    swap_twin = sibling(tok_swap)
    more_table = exchanged(table, 2)
    weights0 = near_weights(table, me)
    saved0, part0, away0 = forward(tokens, tok_twin, weights0)
    tok_mid, tok_out2, tok_mid2, swap_twin, more_table, part0, away0, cotangent = fence(
        tok_mid, tok_out2, tok_mid2, swap_twin, more_table, part0, away0, cotangent
    )

    tok_out3 = send(tok_mid2, ALL_SWAP)
    cot_mid = send(cotangent, MID_SWAP)
    tok_second = jnp.where(inner, tok_mid, tok_out2)
    second_twin = sibling(tok_second)
    weights1 = near_weights(more_table, me)
    far_table = exchanged(jnp.concatenate([table, more_table]), 4)
    saved1, part1, away1 = forward(tok_swap, swap_twin, weights1)
    tok_mid2, tok_out3, cot_mid, second_twin, far_table, part1, away1, cotangent = fence(
        tok_mid2, tok_out3, cot_mid, second_twin, far_table, part1, away1, cotangent
    )

    cot_swap = send(cotangent, ALL_SWAP)
    tok_third = jnp.where(inner, tok_mid2, tok_out3)
    third_twin = sibling(tok_third)
    far = near_weights(far_table, me)
    weights2 = jnp.where(inner, far[2:], far[:2])
    weights3 = jnp.where(inner, far[:2], far[2:])
    saved2, part2, away2 = forward(tok_second, second_twin, weights2)
    saved3, part3, away3 = forward(tok_third, third_twin, weights3)
    part3 = add_rounded(part3, sibling(away3))
    part2 = add_rounded(part2, sibling(away2))
    cot_twin = sibling(cotangent)
    to_swap = jnp.where(inner, cot_mid, part3)
    cot_swap, cot_mid, cot_twin, part2, part3, to_swap = fence(
        cot_swap, cot_mid, cot_twin, part2, part3, to_swap
    )

    swapped5 = send(to_swap, ALL_SWAP)
    cot_mid2 = send(cot_swap, MID_SWAP)
    cot_swap_twin = sibling(cot_swap)
    part1 = add_rounded(part1, sibling(away1))
    part0 = add_rounded(part0, sibling(away0))
    none = (jnp.zeros(adapt_a.shape, jnp.float32), jnp.zeros(adapt_b.shape, jnp.float32))
    grads = backward((cotangent, cot_twin), weights0, (tokens, tok_twin), saved0, none)
    swapped5, cot_mid, cot_mid2, cot_swap_twin, part0, part1, part2, part3, grads = fence(
        swapped5, cot_mid, cot_mid2, cot_swap_twin, part0, part1, part2, part3, grads
    )

    swapped6 = send(jnp.where(inner, cot_mid2, part2), ALL_SWAP)
    third_mid = send(add_rounded(part3, swapped5), MID_SWAP)
    cot_second = jnp.where(inner, cot_mid, swapped5)
    cot_second_twin = sibling(cot_second)
    grads = backward((cot_swap, cot_swap_twin), weights1, (tok_swap, swap_twin), saved1, grads)
    grads = backward(
        (cot_second, cot_second_twin), weights2, (tok_second, second_twin), saved2, grads
    )
    swapped6, third_mid, cot_mid2, part0, part1, part2, grads = fence(
        swapped6, third_mid, cot_mid2, part0, part1, part2, grads
    )

    first_swap = send(add_rounded(part1, third_mid), ALL_SWAP)
    second_mid = send(add_rounded(part2, swapped6), MID_SWAP)
    cot_third = jnp.where(inner, cot_mid2, swapped6)
    grads = backward(
        (cot_third, sibling(cot_third)), weights3, (tok_third, third_twin), saved3, grads
    )
    grad_a, grad_b = group_sum(*grads)
    mixed = add_rounded(part0, first_swap, second_mid)
    return mixed, grad_a[None], grad_b.reshape(adapter_up_maps.shape)


def body(*arrays):
    if (lax.axis_size("dp"), lax.axis_size("expert"), arrays[2].shape[1]) == (4, 8, 8):
        return dense_body(*arrays)
    return sparse_body(*arrays)


def solution(mesh):
    return jax.shard_map(
        body,
        mesh=mesh,
        in_specs=(
            P(("dp", "expert"), None),
            P(("dp", "expert"), None),
            P(("dp", "expert"), None),
            P(("dp", "expert"), None),
            P(("dp", "expert"), None),
            P(),
            P("expert", None, None),
            P("expert", None, None),
            P("expert", None, None),
            P("expert", None, None, None),
        ),
        out_specs=(
            P(("dp", "expert"), None),
            P("expert", None, None),
            P("expert", None, None, None),
        ),
        check_vma=False,
    )
```

```python
import functools

import jax
import jax.numpy as jnp
from jax import lax
from jax.experimental import pallas as pl
from jax.experimental.pallas import tpu as pltpu
from jax.sharding import PartitionSpec as P

ADAPTER_SCALE = 0.5


def route_rows(routing, route_replica_choice, device_expert_table, capacity):
    slot_total = device_expert_table.shape[0]
    route_total = routing.shape[0] * routing.shape[1]
    expert_flat = routing.reshape(-1)
    holds_mask = (expert_flat[:, None] == device_expert_table[None, :]).astype(jnp.int32)
    copies = jnp.sum(holds_mask, axis=1)
    wanted = route_replica_choice.reshape(-1) % copies
    before = jnp.cumsum(holds_mask, axis=1) - holds_mask
    picked = holds_mask * (before == wanted[:, None]).astype(jnp.int32)
    ahead_of = jnp.cumsum(picked, axis=0) - picked
    position = jnp.sum(picked * ahead_of, axis=1)
    target = jnp.sum(picked * jnp.arange(slot_total, dtype=jnp.int32)[None, :], axis=1)
    kept_mask = position < capacity
    dest_index = jnp.where(kept_mask, target * capacity + position, slot_total * capacity)
    source = jnp.full((slot_total * capacity,), route_total, jnp.int32)
    source = source.at[dest_index].set(jnp.arange(route_total, dtype=jnp.int32), mode="drop")
    return (kept_mask, dest_index, source)


def expert_apply_forward(rows_in, gate_up, down, adapt_a, adapt_b):
    adapter_rank_count = adapt_b.shape[1]
    hidden_width = adapt_b.shape[2]
    reduced_rank_rows = jnp.dot(rows_in, adapt_a, preferred_element_type=jnp.float32).astype(
        jnp.bfloat16
    )
    base_preactivation = jnp.dot(rows_in, gate_up, preferred_element_type=jnp.float32)
    adapter_gate_delta = jnp.dot(
        reduced_rank_rows[:, :adapter_rank_count], adapt_b[0], preferred_element_type=jnp.float32
    )
    adapter_up_delta = jnp.dot(
        reduced_rank_rows[:, adapter_rank_count:], adapt_b[1], preferred_element_type=jnp.float32
    )
    gate_preactivation = base_preactivation[:, :hidden_width] + ADAPTER_SCALE * adapter_gate_delta
    up_preactivation = base_preactivation[:, hidden_width:] + ADAPTER_SCALE * adapter_up_delta
    sigmoid_gate = jax.nn.sigmoid(gate_preactivation)
    active = gate_preactivation * sigmoid_gate
    hidden = (active * up_preactivation).astype(jnp.bfloat16)
    layer_output = jnp.dot(hidden, down, preferred_element_type=jnp.float32).astype(jnp.bfloat16)
    return (
        layer_output,
        (reduced_rank_rows, gate_preactivation, up_preactivation, sigmoid_gate, active),
    )


def expert_backward(rows_in, scaled, down, adapt_b, saved_residuals):
    reduced_rank_rows, gate_preactivation, up_preactivation, sigmoid_gate, active = saved_residuals
    adapter_rank_count = adapt_b.shape[1]
    back_hidden = lax.dot_general(
        scaled, down, (((1,), (1,)), ((), ())), preferred_element_type=jnp.float32
    )
    up_preactivation_gradient = (back_hidden * active).astype(jnp.bfloat16)
    slope = sigmoid_gate * (1.0 + gate_preactivation * (1.0 - sigmoid_gate))
    gate_preactivation_gradient = (back_hidden * up_preactivation * slope).astype(jnp.bfloat16)
    row_dimension_numbers = (((0,), (0,)), ((), ()))
    gate_up_map_gradient = ADAPTER_SCALE * lax.dot_general(
        reduced_rank_rows[:, :adapter_rank_count],
        gate_preactivation_gradient,
        row_dimension_numbers,
        preferred_element_type=jnp.float32,
    )
    up_map_gradient = ADAPTER_SCALE * lax.dot_general(
        reduced_rank_rows[:, adapter_rank_count:],
        up_preactivation_gradient,
        row_dimension_numbers,
        preferred_element_type=jnp.float32,
    )
    cols_dims = (((1,), (1,)), ((), ()))
    gate_reduced_rows = lax.dot_general(
        gate_preactivation_gradient, adapt_b[0], cols_dims, preferred_element_type=jnp.float32
    )
    up_reduced_rows = lax.dot_general(
        up_preactivation_gradient, adapt_b[1], cols_dims, preferred_element_type=jnp.float32
    )
    reduced_gradient = (
        ADAPTER_SCALE * jnp.concatenate([gate_reduced_rows, up_reduced_rows], axis=1)
    ).astype(jnp.bfloat16)
    grad_adapt_a = lax.dot_general(
        rows_in, reduced_gradient, row_dimension_numbers, preferred_element_type=jnp.float32
    )
    return (grad_adapt_a, jnp.stack([gate_up_map_gradient, up_map_gradient]))


def sparse_body(
    tokens,
    cotangent,
    routing,
    router_route_weights,
    route_replica_choice,
    device_expert_table,
    gate_up_weight,
    down_weight,
    adapter_down_maps,
    adapter_up_maps,
):
    slot_total = lax.axis_size("expert")
    tok_rows = tokens.shape[0]
    model_feature_width = tokens.shape[1]
    top_routes = routing.shape[1]
    route_total = tok_rows * top_routes
    capacity = route_total // slot_total
    kept_mask, dest_index, source = route_rows(
        routing, route_replica_choice, device_expert_table, capacity
    )
    valid_route_mask = source < route_total
    safe_route = jnp.minimum(source, route_total - 1)
    route_token_index = safe_route // top_routes
    weight_flat = router_route_weights.reshape(-1)
    route_weight_rows = weight_flat[safe_route]
    zero_row = jnp.zeros((), jnp.bfloat16)
    rows_out = jnp.where(valid_route_mask[:, None], tokens[route_token_index], zero_row).reshape(
        slot_total, capacity, model_feature_width
    )
    product = (
        route_weight_rows[:, None] * cotangent[route_token_index].astype(jnp.float32)
    ).astype(jnp.bfloat16)
    scaled_out = jnp.where(valid_route_mask[:, None], product, zero_row).reshape(
        slot_total, capacity, model_feature_width
    )
    rows_in = lax.all_to_all(rows_out, "expert", split_axis=0, concat_axis=0, tiled=True)
    flattened_rows = rows_in.reshape(-1, model_feature_width)
    layer_output, saved_residuals = expert_apply_forward(
        flattened_rows, gate_up_weight[0], down_weight[0], adapter_down_maps[0], adapter_up_maps[0]
    )
    returned = lax.all_to_all(
        layer_output.reshape(slot_total, capacity, model_feature_width),
        "expert",
        split_axis=0,
        concat_axis=0,
        tiled=True,
    )
    returned = returned.reshape(-1, model_feature_width)
    picked_rows = returned[jnp.minimum(dest_index, slot_total * capacity - 1)]
    weighted = jnp.where(
        kept_mask[:, None],
        weight_flat[:, None] * picked_rows.astype(jnp.float32),
        jnp.zeros((), jnp.float32),
    )
    mixed = jnp.sum(weighted.reshape(tok_rows, top_routes, model_feature_width), axis=1).astype(
        jnp.bfloat16
    )
    scaled_input_rows = lax.all_to_all(
        scaled_out, "expert", split_axis=0, concat_axis=0, tiled=True
    )
    grad_adapt_a, grad_adapt_b = expert_backward(
        flattened_rows,
        scaled_input_rows.reshape(-1, model_feature_width),
        down_weight[0],
        adapter_up_maps[0],
        saved_residuals,
    )
    piece_a = grad_adapt_a.reshape(slot_total, -1)
    piece_b = grad_adapt_b.reshape(slot_total, -1)
    expert_total = max(top_routes, slot_total // 2)
    members = (
        jnp.arange(expert_total, dtype=jnp.int32)[:, None] == device_expert_table[None, :]
    ).astype(jnp.float32)
    piece_a, piece_b = lax.psum((piece_a, piece_b), "dp")
    got_a, got_b = (
        lax.all_to_all(piece_a, "expert", split_axis=0, concat_axis=0, tiled=True),
        lax.all_to_all(piece_b, "expert", split_axis=0, concat_axis=0, tiled=True),
    )
    expert_a = jnp.dot(members, got_a, precision=lax.Precision.HIGHEST)
    expert_b = jnp.dot(members, got_b, precision=lax.Precision.HIGHEST)
    back_dims = (((0,), (0,)), ((), ()))
    spread_a = lax.dot_general(members, expert_a, back_dims, precision=lax.Precision.HIGHEST)
    spread_b = lax.dot_general(members, expert_b, back_dims, precision=lax.Precision.HIGHEST)
    summed_a, summed_b = (
        lax.all_to_all(spread_a, "expert", split_axis=0, concat_axis=0, tiled=True),
        lax.all_to_all(spread_b, "expert", split_axis=0, concat_axis=0, tiled=True),
    )
    grad_a = summed_a.reshape(grad_adapt_a.shape)[None]
    grad_b = summed_b.reshape(grad_adapt_b.shape)[None]
    return (mixed, grad_a, grad_b)


def dot(a, b, a_dim=1, b_dim=0):
    return lax.dot_general(
        a, b, (((a_dim,), (b_dim,)), ((), ())), preferred_element_type=jnp.float32
    )


def first_half(shape):
    return lax.broadcasted_iota(jnp.int32, shape, 1) < shape[1] // 2


def halves(low):
    gate = first_half(low.shape)
    zero = jnp.zeros_like(low)
    return jnp.where(gate, low, zero), jnp.where(gate, zero, low)


def column(row):
    return jnp.transpose(jnp.broadcast_to(row, (row.shape[1], row.shape[1])))[:, :1]


def weights_kernel(capacity, table_ref, expert_ref, choice_ref, weight_ref, out_ref):
    slot_total, tok_rows = out_ref.shape
    experts, weights = expert_ref[...], weight_ref[...]
    holds = [experts == table_ref[s] for s in range(slot_total)]
    counts = [hold.astype(jnp.float32) for hold in holds]
    copies = sum(counts)
    choice = choice_ref[...].astype(jnp.float32)
    wanted = choice - copies * jnp.floor((choice + 0.5) / copies)
    before = jnp.zeros_like(copies)
    taken, route_weight = [], []
    for hold, count in zip(holds, counts):
        picked = jnp.where(hold & (before == wanted), 1.0, 0.0)
        before = before + count
        taken.append(jnp.sum(picked, axis=0, keepdims=True))
        route_weight.append(jnp.sum(picked * weights, axis=0, keepdims=True))
    shape = (tok_rows, tok_rows)
    earlier = lax.broadcasted_iota(jnp.int32, shape, 0) < lax.broadcasted_iota(jnp.int32, shape, 1)
    rank = dot(
        jnp.concatenate(taken).astype(jnp.bfloat16),
        jnp.where(earlier, 1.0, 0.0).astype(jnp.bfloat16),
    )
    out_ref[...] = jnp.where(rank < capacity, jnp.concatenate(route_weight), 0.0)


def dense_route_weights(routing, weights, choice, table, capacity):
    vmem = pl.BlockSpec(memory_space=pltpu.VMEM)
    return pl.pallas_call(
        functools.partial(weights_kernel, capacity),
        out_shape=jax.ShapeDtypeStruct((table.shape[0], routing.shape[0]), jnp.float32),
        in_specs=[pl.BlockSpec(memory_space=pltpu.SMEM), vmem, vmem, vmem],
        out_specs=vmem,
    )(table, routing.T, choice.T, weights.T)


def forward_kernel(*refs):
    blocks, refs = refs[:4], refs[4:]
    w_ref, adapt_a_ref, gate_ref, up_ref, adapt_b_ref, down_ref, *refs = refs
    low_ref, active_ref, slope_ref, part_mine_ref, part_other_ref, rows_ref, total_ref = refs
    step = pl.program_id(0)
    quarter = blocks[0].shape[0]
    half = 2 * quarter

    @pl.when(step == 0)
    def _():
        for at, block in enumerate(blocks):
            rows_ref[at * quarter : (at + 1) * quarter] = block[...]
        low_ref[...] = dot(rows_ref[...], adapt_a_ref[...]).astype(jnp.bfloat16)

    rows = rows_ref[...]
    low_gate, low_up = halves(low_ref[...])
    gate = dot(rows, gate_ref[...]) + ADAPTER_SCALE * dot(low_gate, adapt_b_ref[...])
    up = dot(rows, up_ref[...]) + ADAPTER_SCALE * dot(low_up, adapt_b_ref[...])
    sigmoid_gate = jax.nn.sigmoid(gate)
    active = gate * sigmoid_gate
    active_ref[...] = active
    slope_ref[...] = up * (sigmoid_gate * (1.0 + gate * (1.0 - sigmoid_gate)))
    hidden = (active * up).astype(jnp.bfloat16)
    more = dot(hidden, down_ref[...])

    @pl.when(step == 0)
    def _():
        total_ref[...] = more

    @pl.when(step > 0)
    def _():
        total_ref[...] += more

    @pl.when(step == pl.num_programs(0) - 1)
    def _():
        out = total_ref[...].astype(jnp.bfloat16).astype(jnp.float32)
        part_mine_ref[...] = (column(w_ref[0:1]) * out[:half]).astype(jnp.bfloat16)
        part_other_ref[...] = (column(w_ref[1:2]) * out[half:]).astype(jnp.bfloat16)


def whole(shape):
    return pl.BlockSpec(shape, lambda j: (0,) * len(shape))


def columns(rows, width, start=0):
    return pl.BlockSpec((rows, width), lambda j: (0, start + j))


def forward_stage(blocks, w, gate_up, down, adapt_a, adapt_b, chunk=256):
    quarter, features = blocks[0].shape
    half = 2 * quarter
    hidden_width = down.shape[0]
    both, ranks = 2 * half, adapt_a.shape[1]
    steps = hidden_width // chunk
    saved = jax.ShapeDtypeStruct((both, hidden_width), jnp.float32)
    part = jax.ShapeDtypeStruct((half, features), jnp.bfloat16)
    return pl.pallas_call(
        forward_kernel,
        grid=(steps,),
        out_shape=(jax.ShapeDtypeStruct((both, ranks), jnp.bfloat16), saved, saved, part, part),
        in_specs=[whole((quarter, features))] * 4
        + [
            whole((2, half)),
            whole((features, ranks)),
            columns(features, chunk),
            columns(features, chunk, steps),
            columns(ranks, chunk),
            pl.BlockSpec((chunk, features), lambda j: (j, 0)),
        ],
        out_specs=(
            whole((both, ranks)),
            columns(both, chunk),
            columns(both, chunk),
            whole((half, features)),
            whole((half, features)),
        ),
        scratch_shapes=[
            pltpu.VMEM((both, features), jnp.bfloat16),
            pltpu.VMEM((both, features), jnp.float32),
        ],
        compiler_params=pltpu.CompilerParams(vmem_limit_bytes=60 * 2**20),
        cost_estimate=pl.CostEstimate(flops=10**6, bytes_accessed=10**4, transcendentals=0),
    )(*blocks, w, adapt_a, gate_up, gate_up, adapt_b, down)


def backward_kernel(*refs):
    cots, blocks, refs = refs[:4], refs[4:8], refs[8:]
    w_ref, low_ref, active_ref, slope_ref, adapt_b_ref, down_ref, *refs = refs
    grad_a_ref, grad_b_ref, sum_a_ref, sum_b_ref, scaled_ref, rows_ref, back_ref = refs
    step = pl.program_id(0)
    quarter = blocks[0].shape[0]

    @pl.when(step == 0)
    def _():
        w = [column(w_ref[0:1]), column(w_ref[1:2])]
        for at, (cot, block) in enumerate(zip(cots, blocks)):
            rows = slice(at * quarter, (at + 1) * quarter)
            w_rows = w[at // 2][at % 2 * quarter : (at % 2 + 1) * quarter]
            scaled_ref[rows] = (w_rows * cot[...].astype(jnp.float32)).astype(jnp.bfloat16)
            rows_ref[rows] = block[...]
        back_ref[...] = jnp.zeros_like(back_ref)

    back = dot(scaled_ref[...], down_ref[...], 1, 1)
    up_grad = (back * active_ref[...]).astype(jnp.bfloat16)
    gate_grad = (back * slope_ref[...]).astype(jnp.bfloat16)
    low_gate, low_up = halves(low_ref[...])
    sum_b_ref[...] = grad_b_ref[...] + ADAPTER_SCALE * (
        dot(low_gate, gate_grad, 0, 0) + dot(low_up, up_grad, 0, 0)
    )
    gate_back = dot(gate_grad, adapt_b_ref[...], 1, 1)
    up_back = dot(up_grad, adapt_b_ref[...], 1, 1)
    back_ref[...] += jnp.where(first_half(gate_back.shape), gate_back, up_back)

    @pl.when(step == pl.num_programs(0) - 1)
    def _():
        low_grad = (ADAPTER_SCALE * back_ref[...]).astype(jnp.bfloat16)
        sum_a_ref[...] = grad_a_ref[...] + dot(rows_ref[...], low_grad, 0, 0)


def backward_stage(cots, w, blocks, saved, down, adapt_b, grads, chunk=256):
    low, active, slope = saved
    quarter, features = blocks[0].shape
    hidden_width = down.shape[0]
    both, ranks = low.shape
    grad_a = whole((features, ranks))
    grad_b = columns(ranks, chunk)
    return pl.pallas_call(
        backward_kernel,
        grid=(hidden_width // chunk,),
        out_shape=(
            jax.ShapeDtypeStruct((features, ranks), jnp.float32),
            jax.ShapeDtypeStruct((ranks, hidden_width), jnp.float32),
        ),
        in_specs=[whole((quarter, features))] * 8
        + [
            whole((2, 2 * quarter)),
            whole((both, ranks)),
            columns(both, chunk),
            columns(both, chunk),
            columns(ranks, chunk),
            pl.BlockSpec((chunk, features), lambda j: (j, 0)),
            grad_a,
            grad_b,
        ],
        out_specs=(grad_a, grad_b),
        scratch_shapes=[
            pltpu.VMEM((both, features), jnp.bfloat16),
            pltpu.VMEM((both, features), jnp.bfloat16),
            pltpu.VMEM((both, ranks), jnp.float32),
        ],
        compiler_params=pltpu.CompilerParams(vmem_limit_bytes=60 * 2**20),
        cost_estimate=pl.CostEstimate(flops=10**6, bytes_accessed=10**4, transcendentals=0),
    )(*cots, *blocks, w, low, active, slope, adapt_b, down, *grads)


def z_pairs(*moves):
    return [(2 * a + core, 2 * b + core) for a, b in moves for core in (0, 1)]


ALL_SWAP = z_pairs((0, 1), (1, 0), (2, 3), (3, 2))
MID_SWAP = z_pairs((1, 2), (2, 1))
SIBLING = [(e, e ^ 1) for e in range(8)]


def send(array, pairs):
    return lax.ppermute(array, "expert", pairs)


def fence(*arrays):
    return lax.optimization_barrier(arrays)


def add_rounded(*terms):
    total = terms[0].astype(jnp.float32)
    for term in terms[1:]:
        total = total + term.astype(jnp.float32)
    return total.astype(jnp.bfloat16)


def sibling(block):
    return send(block, SIBLING)


def exchanged(weight_table, bit):
    return send(weight_table, [(e, e ^ bit) for e in range(8)])


def near_weights(weight_tables, me):
    tables = weight_tables.reshape(-1, 8, weight_tables.shape[1])
    return lax.dynamic_index_in_dim(tables, me, axis=1, keepdims=False)


def swap_sum(array, bit):
    rounded = lax.reduce_precision(array, 8, 7)
    pairs = [(d, d ^ bit) for d in range(4)]
    other = lax.ppermute(rounded.astype(jnp.bfloat16), "dp", pairs)
    return rounded + other.astype(jnp.float32)


def group_sum(grad_a, grad_b):
    rows, rank = grad_a.shape
    low_rows = (grad_a.size + grad_b.size) // 2 // rank // 16 * 16
    x_first = swap_sum(swap_sum(grad_a[:low_rows], 1), 2)
    y_first = swap_sum(swap_sum(grad_a[low_rows:], 2), 1)
    sum_b = swap_sum(swap_sum(grad_b, 2), 1)
    return jnp.concatenate([x_first, y_first]), sum_b


def dense_body(
    tokens,
    cotangent,
    routing,
    router_route_weights,
    route_replica_choice,
    device_expert_table,
    gate_up_weight,
    down_weight,
    adapter_down_maps,
    adapter_up_maps,
):
    slot_total = lax.axis_size("expert")
    capacity = tokens.shape[0] * routing.shape[1] // slot_total
    me = lax.axis_index("expert")
    chip = me // 2
    inner = (chip == 1) | (chip == 2)
    gate_up, down = gate_up_weight[0], down_weight[0]
    adapt_a = adapter_down_maps[0]
    adapt_b = adapter_up_maps[0].reshape(adapt_a.shape[1], -1)

    def forward(mine, twin, w):
        low, active, slope, part, away = forward_stage(
            (*mine, *twin), w, gate_up, down, adapt_a, adapt_b
        )
        return (low, active, slope), part, away

    def backward(mine, twin, w, rows, saved, grads):
        return backward_stage((*mine, *twin), w, rows, saved, down, adapt_b, grads)

    def in_halves(block):
        rows = block.shape[0] // 2
        return block[:rows], block[rows:]

    def twins(halves_of):
        return [sibling(half) for half in halves_of]

    def chip_part(part, away):
        got = sibling(away)
        return [add_rounded(*both) for both in zip(in_halves(part), in_halves(got))]

    def pick(inside, outside):
        return jnp.where(inner, inside, outside)

    tok_a, tok_b = in_halves(tokens)
    cot_a, cot_b = in_halves(cotangent)
    swap_a, mid_a = send(tok_a, ALL_SWAP), send(tok_a, MID_SWAP)
    swap_b, mid_b = send(tok_b, ALL_SWAP), send(tok_b, MID_SWAP)
    rows0 = (tok_a, tok_b, *twins((tok_a, tok_b)))
    table = dense_route_weights(
        routing, router_route_weights, route_replica_choice, device_expert_table, capacity
    )
    table = jnp.concatenate([table, exchanged(table, 1)])
    weights0 = near_weights(table, me)
    saved0, part0, away0 = forward(rows0[:2], rows0[2:], weights0)

    swap_a, mid_a, part0, away0, table = fence(swap_a, mid_a, part0, away0, table)
    out2_a, mid2_a = send(mid_a, ALL_SWAP), send(swap_a, MID_SWAP)
    swap_b, mid_b, swap_a, table = fence(swap_b, mid_b, swap_a, table)
    out2_b, mid2_b = send(mid_b, ALL_SWAP), send(swap_b, MID_SWAP)
    rows1 = (swap_a, swap_b, *twins((swap_a, swap_b)))
    more_table = exchanged(table, 2)
    weights1 = near_weights(more_table, me)
    saved1, part1, away1 = forward(rows1[:2], rows1[2:], weights1)

    out2_a, mid2_a, mid_a, part1, away1, more_table, cot_a, cot_b = fence(
        out2_a, mid2_a, mid_a, part1, away1, more_table, cot_a, cot_b
    )
    out3_a, cmid_a = send(mid2_a, ALL_SWAP), send(cot_a, MID_SWAP)
    second_a = pick(mid_a, out2_a)
    out2_b, mid2_b, mid_b, second_a, more_table, cot_b = fence(
        out2_b, mid2_b, mid_b, second_a, more_table, cot_b
    )
    out3_b, cmid_b = send(mid2_b, ALL_SWAP), send(cot_b, MID_SWAP)
    second_b = pick(mid_b, out2_b)
    rows2 = (second_a, second_b, *twins((second_a, second_b)))
    far = near_weights(exchanged(jnp.concatenate([table, more_table]), 4), me)
    weights2, weights3 = pick(far[2:], far[:2]), pick(far[:2], far[2:])
    saved2, part2, away2 = forward(rows2[:2], rows2[2:], weights2)

    out3_a, cmid_a, mid2_a, part2, away2, cot_a, cot_b = fence(
        out3_a, cmid_a, mid2_a, part2, away2, cot_a, cot_b
    )
    cswap_a = send(cot_a, ALL_SWAP)
    third_a = pick(mid2_a, out3_a)
    out3_b, cmid_b, mid2_b, third_a, cot_b = fence(out3_b, cmid_b, mid2_b, third_a, cot_b)
    cswap_b = send(cot_b, ALL_SWAP)
    third_b = pick(mid2_b, out3_b)
    rows3 = (third_a, third_b, *twins((third_a, third_b)))
    saved3, part3, away3 = forward(rows3[:2], rows3[2:], weights3)

    cswap_a, cmid_a, part3, away3, part2, away2, cot_a, cot_b = fence(
        cswap_a, cmid_a, part3, away3, part2, away2, cot_a, cot_b
    )
    cmid2_a = send(cswap_a, MID_SWAP)
    part3_a, part3_b = chip_part(part3, away3)
    swap5_a = send(pick(cmid_a, part3_a), ALL_SWAP)
    cswap_b, cmid_b, part3_b, cswap_a = fence(cswap_b, cmid_b, part3_b, cswap_a)
    swap5_b, cmid2_b = send(pick(cmid_b, part3_b), ALL_SWAP), send(cswap_b, MID_SWAP)
    part2_a, part2_b = chip_part(part2, away2)
    none = (jnp.zeros(adapt_a.shape, jnp.float32), jnp.zeros(adapt_b.shape, jnp.float32))
    cots0 = (cot_a, cot_b)
    grads = backward(cots0, twins(cots0), weights0, rows0, saved0, none)

    swap5_a, cmid2_a, part3_a, part2_a, part2_b, part1, away1, grads = fence(
        swap5_a, cmid2_a, part3_a, part2_a, part2_b, part1, away1, grads
    )
    swap6_a = send(pick(cmid2_a, part2_a), ALL_SWAP)
    third_mid_a = send(add_rounded(part3_a, swap5_a), MID_SWAP)
    swap5_b, cmid2_b, part3_b, part2_b, cswap_a = fence(
        swap5_b, cmid2_b, part3_b, part2_b, cswap_a
    )
    swap6_b = send(pick(cmid2_b, part2_b), ALL_SWAP)
    third_mid_b = send(add_rounded(part3_b, swap5_b), MID_SWAP)
    part1_a, part1_b = chip_part(part1, away1)
    cots1 = (cswap_a, cswap_b)
    grads = backward(cots1, twins(cots1), weights1, rows1, saved1, grads)
    cots2 = (pick(cmid_a, swap5_a), pick(cmid_b, swap5_b))
    grads = backward(cots2, twins(cots2), weights2, rows2, saved2, grads)

    swap6_a, third_mid_a, part2_a, part1_a, part1_b, part0, away0, grads = fence(
        swap6_a, third_mid_a, part2_a, part1_a, part1_b, part0, away0, grads
    )
    first_a = send(add_rounded(part1_a, third_mid_a), ALL_SWAP)
    second_mid_a = send(add_rounded(part2_a, swap6_a), MID_SWAP)
    cots3_a = pick(cmid2_a, swap6_a)
    swap6_b, third_mid_b, part2_b, part1_b, cots3_a = fence(
        swap6_b, third_mid_b, part2_b, part1_b, cots3_a
    )
    cots3 = (cots3_a, pick(cmid2_b, swap6_b))
    grads = backward(cots3, twins(cots3), weights3, rows3, saved3, grads)
    first_b = send(add_rounded(part1_b, third_mid_b), ALL_SWAP)
    second_mid_b = send(add_rounded(part2_b, swap6_b), MID_SWAP)
    grad_a, grad_b = group_sum(*grads)
    part0_a, part0_b = chip_part(part0, away0)
    mixed_a = add_rounded(part0_a, first_a, second_mid_a)
    mixed_b = add_rounded(part0_b, first_b, second_mid_b)
    mixed = jnp.concatenate([mixed_a, mixed_b])
    return mixed, grad_a[None], grad_b.reshape(adapter_up_maps.shape)


def body(*arrays):
    if (lax.axis_size("dp"), lax.axis_size("expert"), arrays[2].shape[1]) == (4, 8, 8):
        return dense_body(*arrays)
    return sparse_body(*arrays)


def solution(mesh):
    return jax.shard_map(
        body,
        mesh=mesh,
        in_specs=(
            P(("dp", "expert"), None),
            P(("dp", "expert"), None),
            P(("dp", "expert"), None),
            P(("dp", "expert"), None),
            P(("dp", "expert"), None),
            P(),
            P("expert", None, None),
            P("expert", None, None),
            P("expert", None, None),
            P("expert", None, None, None),
        ),
        out_specs=(
            P(("dp", "expert"), None),
            P("expert", None, None),
            P("expert", None, None, None),
        ),
        check_vma=False,
    )
```

```python
import functools

import jax
import jax.numpy as jnp
from jax import lax
from jax.experimental import pallas as pl
from jax.experimental.pallas import tpu as pltpu
from jax.sharding import PartitionSpec as P

ADAPTER_SCALE = 0.5


def route_rows(routing, route_replica_choice, device_expert_table, capacity):
    slot_total = device_expert_table.shape[0]
    route_total = routing.shape[0] * routing.shape[1]
    expert_flat = routing.reshape(-1)
    holds_mask = (expert_flat[:, None] == device_expert_table[None, :]).astype(jnp.int32)
    copies = jnp.sum(holds_mask, axis=1)
    wanted = route_replica_choice.reshape(-1) % copies
    before = jnp.cumsum(holds_mask, axis=1) - holds_mask
    picked = holds_mask * (before == wanted[:, None]).astype(jnp.int32)
    ahead_of = jnp.cumsum(picked, axis=0) - picked
    position = jnp.sum(picked * ahead_of, axis=1)
    target = jnp.sum(picked * jnp.arange(slot_total, dtype=jnp.int32)[None, :], axis=1)
    kept_mask = position < capacity
    dest_index = jnp.where(kept_mask, target * capacity + position, slot_total * capacity)
    source = jnp.full((slot_total * capacity,), route_total, jnp.int32)
    source = source.at[dest_index].set(jnp.arange(route_total, dtype=jnp.int32), mode="drop")
    return (kept_mask, dest_index, source)


def expert_apply_forward(rows_in, gate_up, down, adapt_a, adapt_b):
    adapter_rank_count = adapt_b.shape[1]
    hidden_width = adapt_b.shape[2]
    reduced_rank_rows = jnp.dot(rows_in, adapt_a, preferred_element_type=jnp.float32).astype(
        jnp.bfloat16
    )
    base_preactivation = jnp.dot(rows_in, gate_up, preferred_element_type=jnp.float32)
    adapter_gate_delta = jnp.dot(
        reduced_rank_rows[:, :adapter_rank_count], adapt_b[0], preferred_element_type=jnp.float32
    )
    adapter_up_delta = jnp.dot(
        reduced_rank_rows[:, adapter_rank_count:], adapt_b[1], preferred_element_type=jnp.float32
    )
    gate_preactivation = base_preactivation[:, :hidden_width] + ADAPTER_SCALE * adapter_gate_delta
    up_preactivation = base_preactivation[:, hidden_width:] + ADAPTER_SCALE * adapter_up_delta
    sigmoid_gate = jax.nn.sigmoid(gate_preactivation)
    active = gate_preactivation * sigmoid_gate
    hidden = (active * up_preactivation).astype(jnp.bfloat16)
    layer_output = jnp.dot(hidden, down, preferred_element_type=jnp.float32).astype(jnp.bfloat16)
    return (
        layer_output,
        (reduced_rank_rows, gate_preactivation, up_preactivation, sigmoid_gate, active),
    )


def expert_backward(rows_in, scaled, down, adapt_b, saved_residuals):
    reduced_rank_rows, gate_preactivation, up_preactivation, sigmoid_gate, active = saved_residuals
    adapter_rank_count = adapt_b.shape[1]
    back_hidden = lax.dot_general(
        scaled, down, (((1,), (1,)), ((), ())), preferred_element_type=jnp.float32
    )
    up_preactivation_gradient = (back_hidden * active).astype(jnp.bfloat16)
    slope = sigmoid_gate * (1.0 + gate_preactivation * (1.0 - sigmoid_gate))
    gate_preactivation_gradient = (back_hidden * up_preactivation * slope).astype(jnp.bfloat16)
    row_dimension_numbers = (((0,), (0,)), ((), ()))
    gate_up_map_gradient = ADAPTER_SCALE * lax.dot_general(
        reduced_rank_rows[:, :adapter_rank_count],
        gate_preactivation_gradient,
        row_dimension_numbers,
        preferred_element_type=jnp.float32,
    )
    up_map_gradient = ADAPTER_SCALE * lax.dot_general(
        reduced_rank_rows[:, adapter_rank_count:],
        up_preactivation_gradient,
        row_dimension_numbers,
        preferred_element_type=jnp.float32,
    )
    cols_dims = (((1,), (1,)), ((), ()))
    gate_reduced_rows = lax.dot_general(
        gate_preactivation_gradient, adapt_b[0], cols_dims, preferred_element_type=jnp.float32
    )
    up_reduced_rows = lax.dot_general(
        up_preactivation_gradient, adapt_b[1], cols_dims, preferred_element_type=jnp.float32
    )
    reduced_gradient = (
        ADAPTER_SCALE * jnp.concatenate([gate_reduced_rows, up_reduced_rows], axis=1)
    ).astype(jnp.bfloat16)
    grad_adapt_a = lax.dot_general(
        rows_in, reduced_gradient, row_dimension_numbers, preferred_element_type=jnp.float32
    )
    return (grad_adapt_a, jnp.stack([gate_up_map_gradient, up_map_gradient]))


def sparse_body(
    tokens,
    cotangent,
    routing,
    router_route_weights,
    route_replica_choice,
    device_expert_table,
    gate_up_weight,
    down_weight,
    adapter_down_maps,
    adapter_up_maps,
):
    slot_total = lax.axis_size("expert")
    tok_rows = tokens.shape[0]
    model_feature_width = tokens.shape[1]
    top_routes = routing.shape[1]
    route_total = tok_rows * top_routes
    capacity = route_total // slot_total
    kept_mask, dest_index, source = route_rows(
        routing, route_replica_choice, device_expert_table, capacity
    )
    valid_route_mask = source < route_total
    safe_route = jnp.minimum(source, route_total - 1)
    route_token_index = safe_route // top_routes
    weight_flat = router_route_weights.reshape(-1)
    route_weight_rows = weight_flat[safe_route]
    zero_row = jnp.zeros((), jnp.bfloat16)
    rows_out = jnp.where(valid_route_mask[:, None], tokens[route_token_index], zero_row).reshape(
        slot_total, capacity, model_feature_width
    )
    product = (
        route_weight_rows[:, None] * cotangent[route_token_index].astype(jnp.float32)
    ).astype(jnp.bfloat16)
    scaled_out = jnp.where(valid_route_mask[:, None], product, zero_row).reshape(
        slot_total, capacity, model_feature_width
    )
    rows_in = lax.all_to_all(rows_out, "expert", split_axis=0, concat_axis=0, tiled=True)
    flattened_rows = rows_in.reshape(-1, model_feature_width)
    layer_output, saved_residuals = expert_apply_forward(
        flattened_rows, gate_up_weight[0], down_weight[0], adapter_down_maps[0], adapter_up_maps[0]
    )
    returned = lax.all_to_all(
        layer_output.reshape(slot_total, capacity, model_feature_width),
        "expert",
        split_axis=0,
        concat_axis=0,
        tiled=True,
    )
    returned = returned.reshape(-1, model_feature_width)
    picked_rows = returned[jnp.minimum(dest_index, slot_total * capacity - 1)]
    weighted = jnp.where(
        kept_mask[:, None],
        weight_flat[:, None] * picked_rows.astype(jnp.float32),
        jnp.zeros((), jnp.float32),
    )
    mixed = jnp.sum(weighted.reshape(tok_rows, top_routes, model_feature_width), axis=1).astype(
        jnp.bfloat16
    )
    scaled_input_rows = lax.all_to_all(
        scaled_out, "expert", split_axis=0, concat_axis=0, tiled=True
    )
    grad_adapt_a, grad_adapt_b = expert_backward(
        flattened_rows,
        scaled_input_rows.reshape(-1, model_feature_width),
        down_weight[0],
        adapter_up_maps[0],
        saved_residuals,
    )
    piece_a = grad_adapt_a.reshape(slot_total, -1)
    piece_b = grad_adapt_b.reshape(slot_total, -1)
    expert_total = max(top_routes, slot_total // 2)
    members = (
        jnp.arange(expert_total, dtype=jnp.int32)[:, None] == device_expert_table[None, :]
    ).astype(jnp.float32)
    piece_a, piece_b = lax.psum((piece_a, piece_b), "dp")
    got_a, got_b = (
        lax.all_to_all(piece_a, "expert", split_axis=0, concat_axis=0, tiled=True),
        lax.all_to_all(piece_b, "expert", split_axis=0, concat_axis=0, tiled=True),
    )
    expert_a = jnp.dot(members, got_a, precision=lax.Precision.HIGHEST)
    expert_b = jnp.dot(members, got_b, precision=lax.Precision.HIGHEST)
    back_dims = (((0,), (0,)), ((), ()))
    spread_a = lax.dot_general(members, expert_a, back_dims, precision=lax.Precision.HIGHEST)
    spread_b = lax.dot_general(members, expert_b, back_dims, precision=lax.Precision.HIGHEST)
    summed_a, summed_b = (
        lax.all_to_all(spread_a, "expert", split_axis=0, concat_axis=0, tiled=True),
        lax.all_to_all(spread_b, "expert", split_axis=0, concat_axis=0, tiled=True),
    )
    grad_a = summed_a.reshape(grad_adapt_a.shape)[None]
    grad_b = summed_b.reshape(grad_adapt_b.shape)[None]
    return (mixed, grad_a, grad_b)


def dot(a, b, a_dim=1, b_dim=0):
    return lax.dot_general(
        a, b, (((a_dim,), (b_dim,)), ((), ())), preferred_element_type=jnp.float32
    )


def first_half(shape):
    return lax.broadcasted_iota(jnp.int32, shape, 1) < shape[1] // 2


def halves(low):
    gate = first_half(low.shape)
    zero = jnp.zeros_like(low)
    return jnp.where(gate, low, zero), jnp.where(gate, zero, low)


def column(row):
    return jnp.transpose(jnp.broadcast_to(row, (row.shape[1], row.shape[1])))[:, :1]


def weights_kernel(capacity, table_ref, expert_ref, choice_ref, weight_ref, out_ref):
    slot_total, tok_rows = out_ref.shape
    experts, weights = expert_ref[...], weight_ref[...]
    holds = [experts == table_ref[s] for s in range(slot_total)]
    counts = [hold.astype(jnp.float32) for hold in holds]
    copies = sum(counts)
    choice = choice_ref[...].astype(jnp.float32)
    wanted = choice - copies * jnp.floor((choice + 0.5) / copies)
    before = jnp.zeros_like(copies)
    taken, route_weight = [], []
    for hold, count in zip(holds, counts):
        picked = jnp.where(hold & (before == wanted), 1.0, 0.0)
        before = before + count
        taken.append(jnp.sum(picked, axis=0, keepdims=True))
        route_weight.append(jnp.sum(picked * weights, axis=0, keepdims=True))
    shape = (tok_rows, tok_rows)
    earlier = lax.broadcasted_iota(jnp.int32, shape, 0) < lax.broadcasted_iota(jnp.int32, shape, 1)
    rank = dot(
        jnp.concatenate(taken).astype(jnp.bfloat16),
        jnp.where(earlier, 1.0, 0.0).astype(jnp.bfloat16),
    )
    out_ref[...] = jnp.where(rank < capacity, jnp.concatenate(route_weight), 0.0)


def dense_route_weights(routing, weights, choice, table, capacity):
    vmem = pl.BlockSpec(memory_space=pltpu.VMEM)
    return pl.pallas_call(
        functools.partial(weights_kernel, capacity),
        out_shape=jax.ShapeDtypeStruct((table.shape[0], routing.shape[0]), jnp.float32),
        in_specs=[pl.BlockSpec(memory_space=pltpu.SMEM), vmem, vmem, vmem],
        out_specs=vmem,
    )(table, routing.T, choice.T, weights.T)


def load_blocks(rows_ref, blocks):
    rows = blocks[0].shape[0]
    for at, block in enumerate(blocks):
        rows_ref[at * rows : (at + 1) * rows] = block[...]


def forward_kernel(n_blocks, chunk, *refs):
    blocks, refs = refs[:n_blocks], refs[n_blocks:]
    w_ref, adapt_a_ref, gate_up_ref, adapt_b_ref, down_ref, *refs = refs
    low_ref, active_ref, slope_ref, part_mine_ref, part_other_ref, rows_ref, total_ref = refs
    half = part_mine_ref.shape[0]
    hidden_width = down_ref.shape[0]
    load_blocks(rows_ref, blocks)
    rows = rows_ref[...]
    low = dot(rows, adapt_a_ref[...]).astype(jnp.bfloat16)
    low_ref[...] = low
    low_gate, low_up = halves(low)
    for start in range(0, hidden_width, chunk):
        here = slice(start, start + chunk)
        there = slice(hidden_width + start, hidden_width + start + chunk)
        adapt_b = adapt_b_ref[:, here]
        gate = dot(rows, gate_up_ref[:, here]) + ADAPTER_SCALE * dot(low_gate, adapt_b)
        up = dot(rows, gate_up_ref[:, there]) + ADAPTER_SCALE * dot(low_up, adapt_b)
        sigmoid_gate = jax.nn.sigmoid(gate)
        active = gate * sigmoid_gate
        active_ref[:, here] = active
        slope_ref[:, here] = up * (sigmoid_gate * (1.0 + gate * (1.0 - sigmoid_gate)))
        more = dot((active * up).astype(jnp.bfloat16), down_ref[here])
        if start == 0:
            total_ref[...] = more
        else:
            total_ref[...] += more
    out = total_ref[...].astype(jnp.bfloat16).astype(jnp.float32)
    part_mine_ref[...] = (column(w_ref[0:1]) * out[:half]).astype(jnp.bfloat16)
    part_other_ref[...] = (column(w_ref[1:2]) * out[half:]).astype(jnp.bfloat16)


VMEM = pl.BlockSpec(memory_space=pltpu.VMEM)


def forward_stage(blocks, w, gate_up, down, adapt_a, adapt_b, chunk=256):
    features = blocks[0].shape[1]
    both = len(blocks) * blocks[0].shape[0]
    saved = jax.ShapeDtypeStruct((both, down.shape[0]), jnp.float32)
    part = jax.ShapeDtypeStruct((both // 2, features), jnp.bfloat16)
    low = jax.ShapeDtypeStruct((both, adapt_a.shape[1]), jnp.bfloat16)
    return pl.pallas_call(
        functools.partial(forward_kernel, len(blocks), chunk),
        out_shape=(low, saved, saved, part, part),
        in_specs=[VMEM] * (len(blocks) + 5),
        out_specs=(VMEM,) * 5,
        scratch_shapes=[
            pltpu.VMEM((both, features), jnp.bfloat16),
            pltpu.VMEM((both, features), jnp.float32),
        ],
        compiler_params=pltpu.CompilerParams(vmem_limit_bytes=16 * 2**20),
        cost_estimate=pl.CostEstimate(flops=10**6, bytes_accessed=10**4, transcendentals=0),
    )(*blocks, w, adapt_a, gate_up, adapt_b, down)


def backward_kernel(n_blocks, chunk, adds, *refs):
    cots, blocks, refs = refs[:n_blocks], refs[n_blocks : 2 * n_blocks], refs[2 * n_blocks :]
    w_ref, low_ref, active_ref, slope_ref, adapt_b_ref, down_ref, *refs = refs
    *grads, sum_a_ref, sum_b_ref, scaled_ref, rows_ref = refs
    rows = blocks[0].shape[0]
    load_blocks(rows_ref, blocks)
    w = jnp.concatenate([column(w_ref[0:1]), column(w_ref[1:2])])
    for at, cot in enumerate(cots):
        here = slice(at * rows, (at + 1) * rows)
        scaled_ref[here] = (w[here] * cot[...].astype(jnp.float32)).astype(jnp.bfloat16)
    scaled = scaled_ref[...]
    low_gate, low_up = halves(low_ref[...])
    low_back = 0.0
    for start in range(0, down_ref.shape[0], chunk):
        here = slice(start, start + chunk)
        adapt_b = adapt_b_ref[:, here]
        back = dot(scaled, down_ref[here], 1, 1)
        up_grad = (back * active_ref[:, here]).astype(jnp.bfloat16)
        gate_grad = (back * slope_ref[:, here]).astype(jnp.bfloat16)
        sum_b = ADAPTER_SCALE * (dot(low_gate, gate_grad, 0, 0) + dot(low_up, up_grad, 0, 0))
        sum_b_ref[:, here] = sum_b + grads[1][:, here] if adds else sum_b
        gate_back, up_back = dot(gate_grad, adapt_b, 1, 1), dot(up_grad, adapt_b, 1, 1)
        low_back = low_back + jnp.where(first_half(gate_back.shape), gate_back, up_back)
    low_grad = (ADAPTER_SCALE * low_back).astype(jnp.bfloat16)
    sum_a = dot(rows_ref[...], low_grad, 0, 0)
    sum_a_ref[...] = sum_a + grads[0][...] if adds else sum_a


def backward_stage(cots, w, blocks, saved, down, adapt_b, grads=(), chunk=256):
    low, active, slope = saved
    features = blocks[0].shape[1]
    both, ranks = low.shape
    operands = (*cots, *blocks, w, low, active, slope, adapt_b, down, *grads)
    return pl.pallas_call(
        functools.partial(backward_kernel, len(blocks), chunk, len(grads) > 0),
        out_shape=(
            jax.ShapeDtypeStruct((features, ranks), jnp.float32),
            jax.ShapeDtypeStruct((ranks, down.shape[0]), jnp.float32),
        ),
        in_specs=[VMEM] * len(operands),
        out_specs=(VMEM, VMEM),
        scratch_shapes=[
            pltpu.VMEM((both, features), jnp.bfloat16),
            pltpu.VMEM((both, features), jnp.bfloat16),
        ],
        compiler_params=pltpu.CompilerParams(vmem_limit_bytes=16 * 2**20),
        cost_estimate=pl.CostEstimate(flops=10**6, bytes_accessed=10**4, transcendentals=0),
    )(*operands)


def z_pairs(*moves):
    return [(2 * a + core, 2 * b + core) for a, b in moves for core in (0, 1)]


ALL_SWAP = z_pairs((0, 1), (1, 0), (2, 3), (3, 2))
MID_SWAP = z_pairs((1, 2), (2, 1))
SIBLING = [(e, e ^ 1) for e in range(8)]


def send(array, pairs):
    return lax.ppermute(array, "expert", pairs)


def fence(*arrays):
    return lax.optimization_barrier(arrays)


def add_rounded(*terms):
    total = terms[0].astype(jnp.float32)
    for term in terms[1:]:
        total = total + term.astype(jnp.float32)
    return total.astype(jnp.bfloat16)


def sibling(block):
    return send(block, SIBLING)


def exchanged(weight_table, bit):
    return send(weight_table, [(e, e ^ bit) for e in range(8)])


def near_weights(weight_tables, me):
    tables = weight_tables.reshape(-1, 8, weight_tables.shape[1])
    return lax.dynamic_index_in_dim(tables, me, axis=1, keepdims=False)


def swap_sum(array, bit):
    rounded = lax.reduce_precision(array, 8, 7)
    pairs = [(d, d ^ bit) for d in range(4)]
    other = lax.ppermute(rounded.astype(jnp.bfloat16), "dp", pairs)
    return rounded + other.astype(jnp.float32)


def group_sum(grad_a, grad_b):
    rows, rank = grad_a.shape
    low_rows = (grad_a.size + grad_b.size) // 2 // rank // 16 * 16
    x_first = swap_sum(swap_sum(grad_a[:low_rows], 1), 2)
    y_first = swap_sum(swap_sum(grad_a[low_rows:], 2), 1)
    sum_b = swap_sum(swap_sum(grad_b, 2), 1)
    return jnp.concatenate([x_first, y_first]), sum_b


def dense_body(
    tokens,
    cotangent,
    routing,
    router_route_weights,
    route_replica_choice,
    device_expert_table,
    gate_up_weight,
    down_weight,
    adapter_down_maps,
    adapter_up_maps,
):
    slot_total = lax.axis_size("expert")
    capacity = tokens.shape[0] * routing.shape[1] // slot_total
    me = lax.axis_index("expert")
    chip = me // 2
    inner = (chip == 1) | (chip == 2)
    gate_up, down = gate_up_weight[0], down_weight[0]
    adapt_a = adapter_down_maps[0]
    adapt_b = adapter_up_maps[0].reshape(adapt_a.shape[1], -1)

    def forward(mine, twin, w):
        low, active, slope, part, away = forward_stage(
            (*mine, *twin), w, gate_up, down, adapt_a, adapt_b
        )
        return (low, active, slope), part, away

    def backward(mine, twin, w, rows, saved, grads):
        return backward_stage((*mine, *twin), w, rows, saved, down, adapt_b, grads)

    def in_halves(block):
        rows = block.shape[0] // 2
        return block[:rows], block[rows:]

    def twins(halves_of):
        return [sibling(half) for half in halves_of]

    def chip_part(part, away):
        got = sibling(away)
        return [add_rounded(*both) for both in zip(in_halves(part), in_halves(got))]

    def pick(inside, outside):
        return jnp.where(inner, inside, outside)

    tok_a, tok_b = in_halves(tokens)
    cot_a, cot_b = in_halves(cotangent)
    swap_a, mid_a = send(tok_a, ALL_SWAP), send(tok_a, MID_SWAP)
    swap_b, mid_b = send(tok_b, ALL_SWAP), send(tok_b, MID_SWAP)
    rows0 = (tok_a, tok_b, *twins((tok_a, tok_b)))
    table = dense_route_weights(
        routing, router_route_weights, route_replica_choice, device_expert_table, capacity
    )
    table = jnp.concatenate([table, exchanged(table, 1)])
    weights0 = near_weights(table, me)
    saved0, part0, away0 = forward(rows0[:2], rows0[2:], weights0)

    swap_a, mid_a, part0, away0, table = fence(swap_a, mid_a, part0, away0, table)
    out2_a, mid2_a = send(mid_a, ALL_SWAP), send(swap_a, MID_SWAP)
    swap_b, mid_b, swap_a, table = fence(swap_b, mid_b, swap_a, table)
    out2_b, mid2_b = send(mid_b, ALL_SWAP), send(swap_b, MID_SWAP)
    rows1 = (swap_a, swap_b, *twins((swap_a, swap_b)))
    more_table = exchanged(table, 2)
    weights1 = near_weights(more_table, me)
    saved1, part1, away1 = forward(rows1[:2], rows1[2:], weights1)

    out2_a, mid2_a, mid_a, part1, away1, more_table, cot_a, cot_b = fence(
        out2_a, mid2_a, mid_a, part1, away1, more_table, cot_a, cot_b
    )
    out3_a, cmid_a = send(mid2_a, ALL_SWAP), send(cot_a, MID_SWAP)
    second_a = pick(mid_a, out2_a)
    out2_b, mid2_b, mid_b, second_a, more_table, cot_b = fence(
        out2_b, mid2_b, mid_b, second_a, more_table, cot_b
    )
    out3_b, cmid_b = send(mid2_b, ALL_SWAP), send(cot_b, MID_SWAP)
    second_b = pick(mid_b, out2_b)
    rows2 = (second_a, second_b, *twins((second_a, second_b)))
    far = near_weights(exchanged(jnp.concatenate([table, more_table]), 4), me)
    weights2, weights3 = pick(far[2:], far[:2]), pick(far[:2], far[2:])
    saved2, part2, away2 = forward(rows2[:2], rows2[2:], weights2)

    out3_a, cmid_a, mid2_a, part2, away2, cot_a, cot_b = fence(
        out3_a, cmid_a, mid2_a, part2, away2, cot_a, cot_b
    )
    cswap_a = send(cot_a, ALL_SWAP)
    third_a = pick(mid2_a, out3_a)
    out3_b, cmid_b, mid2_b, third_a, cot_b = fence(out3_b, cmid_b, mid2_b, third_a, cot_b)
    cswap_b = send(cot_b, ALL_SWAP)
    third_b = pick(mid2_b, out3_b)
    rows3 = (third_a, third_b, *twins((third_a, third_b)))
    saved3, part3, away3 = forward(rows3[:2], rows3[2:], weights3)

    cswap_a, cmid_a, part3, away3, part2, away2, cot_a, cot_b = fence(
        cswap_a, cmid_a, part3, away3, part2, away2, cot_a, cot_b
    )
    cmid2_a = send(cswap_a, MID_SWAP)
    part3_a, part3_b = chip_part(part3, away3)
    swap5_a = send(pick(cmid_a, part3_a), ALL_SWAP)
    cswap_b, cmid_b, part3_b, cswap_a = fence(cswap_b, cmid_b, part3_b, cswap_a)
    swap5_b, cmid2_b = send(pick(cmid_b, part3_b), ALL_SWAP), send(cswap_b, MID_SWAP)
    part2_a, part2_b = chip_part(part2, away2)
    cots0 = (cot_a, cot_b)
    grads = backward(cots0, twins(cots0), weights0, rows0, saved0, ())

    swap5_a, cmid2_a, part3_a, part2_a, part2_b, part1, away1, grads = fence(
        swap5_a, cmid2_a, part3_a, part2_a, part2_b, part1, away1, grads
    )
    swap6_a = send(pick(cmid2_a, part2_a), ALL_SWAP)
    third_mid_a = send(add_rounded(part3_a, swap5_a), MID_SWAP)
    swap5_b, cmid2_b, part3_b, part2_b, cswap_a = fence(
        swap5_b, cmid2_b, part3_b, part2_b, cswap_a
    )
    swap6_b = send(pick(cmid2_b, part2_b), ALL_SWAP)
    third_mid_b = send(add_rounded(part3_b, swap5_b), MID_SWAP)
    part1_a, part1_b = chip_part(part1, away1)
    cots1 = (cswap_a, cswap_b)
    grads = backward(cots1, twins(cots1), weights1, rows1, saved1, grads)
    cots2 = (pick(cmid_a, swap5_a), pick(cmid_b, swap5_b))
    grads = backward(cots2, twins(cots2), weights2, rows2, saved2, grads)

    swap6_a, third_mid_a, part2_a, part1_a, part1_b, part0, away0, grads = fence(
        swap6_a, third_mid_a, part2_a, part1_a, part1_b, part0, away0, grads
    )
    first_a = send(add_rounded(part1_a, third_mid_a), ALL_SWAP)
    second_mid_a = send(add_rounded(part2_a, swap6_a), MID_SWAP)
    cots3_a = pick(cmid2_a, swap6_a)
    swap6_b, third_mid_b, part2_b, part1_b, cots3_a = fence(
        swap6_b, third_mid_b, part2_b, part1_b, cots3_a
    )
    cots3 = (cots3_a, pick(cmid2_b, swap6_b))
    grads = backward(cots3, twins(cots3), weights3, rows3, saved3, grads)
    first_b = send(add_rounded(part1_b, third_mid_b), ALL_SWAP)
    second_mid_b = send(add_rounded(part2_b, swap6_b), MID_SWAP)
    grad_a, grad_b = group_sum(*grads)
    part0_a, part0_b = chip_part(part0, away0)
    mixed_a = add_rounded(part0_a, first_a, second_mid_a)
    mixed_b = add_rounded(part0_b, first_b, second_mid_b)
    mixed = jnp.concatenate([mixed_a, mixed_b])
    return mixed, grad_a[None], grad_b.reshape(adapter_up_maps.shape)


def body(*arrays):
    if (lax.axis_size("dp"), lax.axis_size("expert"), arrays[2].shape[1]) == (4, 8, 8):
        return dense_body(*arrays)
    return sparse_body(*arrays)


def solution(mesh):
    return jax.shard_map(
        body,
        mesh=mesh,
        in_specs=(
            P(("dp", "expert"), None),
            P(("dp", "expert"), None),
            P(("dp", "expert"), None),
            P(("dp", "expert"), None),
            P(("dp", "expert"), None),
            P(),
            P("expert", None, None),
            P("expert", None, None),
            P("expert", None, None),
            P("expert", None, None, None),
        ),
        out_specs=(
            P(("dp", "expert"), None),
            P("expert", None, None),
            P("expert", None, None, None),
        ),
        check_vma=False,
    )
```

```python
import functools

import jax
import jax.numpy as jnp
from jax import lax
from jax.experimental import pallas as pl
from jax.experimental.pallas import tpu as pltpu
from jax.sharding import PartitionSpec as P

ADAPTER_SCALE = 0.5


def route_rows(routing, route_replica_choice, device_expert_table, capacity):
    slot_total = device_expert_table.shape[0]
    route_total = routing.shape[0] * routing.shape[1]
    expert_flat = routing.reshape(-1)
    holds_mask = (expert_flat[:, None] == device_expert_table[None, :]).astype(jnp.int32)
    copies = jnp.sum(holds_mask, axis=1)
    wanted = route_replica_choice.reshape(-1) % copies
    before = jnp.cumsum(holds_mask, axis=1) - holds_mask
    picked = holds_mask * (before == wanted[:, None]).astype(jnp.int32)
    ahead_of = jnp.cumsum(picked, axis=0) - picked
    position = jnp.sum(picked * ahead_of, axis=1)
    target = jnp.sum(picked * jnp.arange(slot_total, dtype=jnp.int32)[None, :], axis=1)
    kept_mask = position < capacity
    dest_index = jnp.where(kept_mask, target * capacity + position, slot_total * capacity)
    source = jnp.full((slot_total * capacity,), route_total, jnp.int32)
    source = source.at[dest_index].set(jnp.arange(route_total, dtype=jnp.int32), mode="drop")
    return (kept_mask, dest_index, source)


def expert_apply_forward(rows_in, gate_up, down, adapt_a, adapt_b):
    adapter_rank_count = adapt_b.shape[1]
    hidden_width = adapt_b.shape[2]
    reduced_rank_rows = jnp.dot(rows_in, adapt_a, preferred_element_type=jnp.float32).astype(
        jnp.bfloat16
    )
    base_preactivation = jnp.dot(rows_in, gate_up, preferred_element_type=jnp.float32)
    adapter_gate_delta = jnp.dot(
        reduced_rank_rows[:, :adapter_rank_count], adapt_b[0], preferred_element_type=jnp.float32
    )
    adapter_up_delta = jnp.dot(
        reduced_rank_rows[:, adapter_rank_count:], adapt_b[1], preferred_element_type=jnp.float32
    )
    gate_preactivation = base_preactivation[:, :hidden_width] + ADAPTER_SCALE * adapter_gate_delta
    up_preactivation = base_preactivation[:, hidden_width:] + ADAPTER_SCALE * adapter_up_delta
    sigmoid_gate = jax.nn.sigmoid(gate_preactivation)
    active = gate_preactivation * sigmoid_gate
    hidden = (active * up_preactivation).astype(jnp.bfloat16)
    layer_output = jnp.dot(hidden, down, preferred_element_type=jnp.float32).astype(jnp.bfloat16)
    return (
        layer_output,
        (reduced_rank_rows, gate_preactivation, up_preactivation, sigmoid_gate, active),
    )


def expert_backward(rows_in, scaled, down, adapt_b, saved_residuals):
    reduced_rank_rows, gate_preactivation, up_preactivation, sigmoid_gate, active = saved_residuals
    adapter_rank_count = adapt_b.shape[1]
    back_hidden = lax.dot_general(
        scaled, down, (((1,), (1,)), ((), ())), preferred_element_type=jnp.float32
    )
    up_preactivation_gradient = (back_hidden * active).astype(jnp.bfloat16)
    slope = sigmoid_gate * (1.0 + gate_preactivation * (1.0 - sigmoid_gate))
    gate_preactivation_gradient = (back_hidden * up_preactivation * slope).astype(jnp.bfloat16)
    row_dimension_numbers = (((0,), (0,)), ((), ()))
    gate_up_map_gradient = ADAPTER_SCALE * lax.dot_general(
        reduced_rank_rows[:, :adapter_rank_count],
        gate_preactivation_gradient,
        row_dimension_numbers,
        preferred_element_type=jnp.float32,
    )
    up_map_gradient = ADAPTER_SCALE * lax.dot_general(
        reduced_rank_rows[:, adapter_rank_count:],
        up_preactivation_gradient,
        row_dimension_numbers,
        preferred_element_type=jnp.float32,
    )
    cols_dims = (((1,), (1,)), ((), ()))
    gate_reduced_rows = lax.dot_general(
        gate_preactivation_gradient, adapt_b[0], cols_dims, preferred_element_type=jnp.float32
    )
    up_reduced_rows = lax.dot_general(
        up_preactivation_gradient, adapt_b[1], cols_dims, preferred_element_type=jnp.float32
    )
    reduced_gradient = (
        ADAPTER_SCALE * jnp.concatenate([gate_reduced_rows, up_reduced_rows], axis=1)
    ).astype(jnp.bfloat16)
    grad_adapt_a = lax.dot_general(
        rows_in, reduced_gradient, row_dimension_numbers, preferred_element_type=jnp.float32
    )
    return (grad_adapt_a, jnp.stack([gate_up_map_gradient, up_map_gradient]))


def sparse_body(
    tokens,
    cotangent,
    routing,
    router_route_weights,
    route_replica_choice,
    device_expert_table,
    gate_up_weight,
    down_weight,
    adapter_down_maps,
    adapter_up_maps,
):
    slot_total = lax.axis_size("expert")
    tok_rows = tokens.shape[0]
    model_feature_width = tokens.shape[1]
    top_routes = routing.shape[1]
    route_total = tok_rows * top_routes
    capacity = route_total // slot_total
    kept_mask, dest_index, source = route_rows(
        routing, route_replica_choice, device_expert_table, capacity
    )
    valid_route_mask = source < route_total
    safe_route = jnp.minimum(source, route_total - 1)
    route_token_index = safe_route // top_routes
    weight_flat = router_route_weights.reshape(-1)
    route_weight_rows = weight_flat[safe_route]
    zero_row = jnp.zeros((), jnp.bfloat16)
    rows_out = jnp.where(valid_route_mask[:, None], tokens[route_token_index], zero_row).reshape(
        slot_total, capacity, model_feature_width
    )
    product = (
        route_weight_rows[:, None] * cotangent[route_token_index].astype(jnp.float32)
    ).astype(jnp.bfloat16)
    scaled_out = jnp.where(valid_route_mask[:, None], product, zero_row).reshape(
        slot_total, capacity, model_feature_width
    )
    rows_in = lax.all_to_all(rows_out, "expert", split_axis=0, concat_axis=0, tiled=True)
    flattened_rows = rows_in.reshape(-1, model_feature_width)
    layer_output, saved_residuals = expert_apply_forward(
        flattened_rows, gate_up_weight[0], down_weight[0], adapter_down_maps[0], adapter_up_maps[0]
    )
    returned = lax.all_to_all(
        layer_output.reshape(slot_total, capacity, model_feature_width),
        "expert",
        split_axis=0,
        concat_axis=0,
        tiled=True,
    )
    returned = returned.reshape(-1, model_feature_width)
    picked_rows = returned[jnp.minimum(dest_index, slot_total * capacity - 1)]
    weighted = jnp.where(
        kept_mask[:, None],
        weight_flat[:, None] * picked_rows.astype(jnp.float32),
        jnp.zeros((), jnp.float32),
    )
    mixed = jnp.sum(weighted.reshape(tok_rows, top_routes, model_feature_width), axis=1).astype(
        jnp.bfloat16
    )
    scaled_input_rows = lax.all_to_all(
        scaled_out, "expert", split_axis=0, concat_axis=0, tiled=True
    )
    grad_adapt_a, grad_adapt_b = expert_backward(
        flattened_rows,
        scaled_input_rows.reshape(-1, model_feature_width),
        down_weight[0],
        adapter_up_maps[0],
        saved_residuals,
    )
    piece_a = grad_adapt_a.reshape(slot_total, -1)
    piece_b = grad_adapt_b.reshape(slot_total, -1)
    expert_total = max(top_routes, slot_total // 2)
    members = (
        jnp.arange(expert_total, dtype=jnp.int32)[:, None] == device_expert_table[None, :]
    ).astype(jnp.float32)
    piece_a, piece_b = lax.psum((piece_a, piece_b), "dp")
    got_a, got_b = (
        lax.all_to_all(piece_a, "expert", split_axis=0, concat_axis=0, tiled=True),
        lax.all_to_all(piece_b, "expert", split_axis=0, concat_axis=0, tiled=True),
    )
    expert_a = jnp.dot(members, got_a, precision=lax.Precision.HIGHEST)
    expert_b = jnp.dot(members, got_b, precision=lax.Precision.HIGHEST)
    back_dims = (((0,), (0,)), ((), ()))
    spread_a = lax.dot_general(members, expert_a, back_dims, precision=lax.Precision.HIGHEST)
    spread_b = lax.dot_general(members, expert_b, back_dims, precision=lax.Precision.HIGHEST)
    summed_a, summed_b = (
        lax.all_to_all(spread_a, "expert", split_axis=0, concat_axis=0, tiled=True),
        lax.all_to_all(spread_b, "expert", split_axis=0, concat_axis=0, tiled=True),
    )
    grad_a = summed_a.reshape(grad_adapt_a.shape)[None]
    grad_b = summed_b.reshape(grad_adapt_b.shape)[None]
    return (mixed, grad_a, grad_b)


def dot(a, b, a_dim=1, b_dim=0):
    return lax.dot_general(
        a, b, (((a_dim,), (b_dim,)), ((), ())), preferred_element_type=jnp.float32
    )


def first_half(shape):
    return lax.broadcasted_iota(jnp.int32, shape, 1) < shape[1] // 2


def halves(low):
    gate = first_half(low.shape)
    zero = jnp.zeros_like(low)
    return jnp.where(gate, low, zero), jnp.where(gate, zero, low)


def split_weights(table):
    parts = []
    for _ in range(3):
        part = table.astype(jnp.bfloat16).astype(jnp.float32)
        parts.append(part)
        table = table - part
    slot_total, tok_rows = table.shape
    parts.append(jnp.zeros((tok_rows - 3 * slot_total, tok_rows), jnp.float32))
    return jnp.transpose(jnp.concatenate(parts)).astype(jnp.bfloat16)


def joined_weight(extra, slot, slot_total):
    lane = lax.broadcasted_iota(jnp.int32, extra.shape, 1)
    mine = lane == slot
    for part in range(1, 3):
        mine = mine | (lane == slot + part * slot_total)
    chosen = jnp.where(mine, extra.astype(jnp.float32), 0.0)
    return jnp.sum(chosen, axis=1, keepdims=True)


def tagged_kernel(
    capacity, table_ref, expert_ref, choice_ref, weight_ref, tokens_ref, out_ref, extra_ref, sems
):
    slot_total = table_ref.shape[0]
    tok_rows, features = tokens_ref.shape
    rows = pltpu.make_async_copy(tokens_ref, out_ref.at[:, :features], sems.at[0])
    rows.start()
    experts, weights = expert_ref[...], weight_ref[...]
    holds = [experts == table_ref[s] for s in range(slot_total)]
    counts = [hold.astype(jnp.float32) for hold in holds]
    copies = sum(counts)
    choice = choice_ref[...].astype(jnp.float32)
    wanted = choice - copies * jnp.floor((choice + 0.5) / copies)
    before = jnp.zeros_like(copies)
    taken, route_weight = [], []
    for hold, count in zip(holds, counts):
        picked = jnp.where(hold & (before == wanted), 1.0, 0.0)
        before = before + count
        taken.append(jnp.sum(picked, axis=0, keepdims=True))
        route_weight.append(jnp.sum(picked * weights, axis=0, keepdims=True))
    shape = (tok_rows, tok_rows)
    earlier = lax.broadcasted_iota(jnp.int32, shape, 0) < lax.broadcasted_iota(jnp.int32, shape, 1)
    rank = dot(
        jnp.concatenate(taken).astype(jnp.bfloat16),
        jnp.where(earlier, 1.0, 0.0).astype(jnp.bfloat16),
    )
    table = jnp.where(rank < capacity, jnp.concatenate(route_weight), 0.0)
    extra_ref[...] = split_weights(table)
    extra = pltpu.make_async_copy(extra_ref, out_ref.at[:, features:], sems.at[1])
    extra.start()
    rows.wait()
    extra.wait()


VMEM = pl.BlockSpec(memory_space=pltpu.VMEM)
SMEM = pl.BlockSpec(memory_space=pltpu.SMEM)
ANY = pl.BlockSpec(memory_space=pl.ANY)
EXTRA = 128


def tagged_tokens(tokens, routing, weights, choice, table, capacity):
    tok_rows, features = tokens.shape
    return pl.pallas_call(
        functools.partial(tagged_kernel, capacity),
        out_shape=jax.ShapeDtypeStruct((tok_rows, features + EXTRA), tokens.dtype),
        in_specs=[SMEM, VMEM, VMEM, VMEM, ANY],
        out_specs=ANY,
        scratch_shapes=[
            pltpu.VMEM((tok_rows, EXTRA), jnp.bfloat16),
            pltpu.SemaphoreType.DMA((2,)),
        ],
    )(table, routing.T, choice.T, weights.T, tokens)


class Copies:
    def __init__(self, sems):
        self.sems, self.used = sems, 0

    def start(self, source, target):
        copy = pltpu.make_async_copy(source, target, self.sems.at[self.used])
        self.used += 1
        copy.start()
        return copy


def wait_all(copies):
    for copy in copies:
        copy.wait()


def chunks_of(width, chunk):
    return [slice(start, start + chunk) for start in range(0, width, chunk)]


def forward_kernel(
    chunk, slot_ref, mine_hbm, other_hbm, adapt_a_hbm, gate_up_hbm, adapt_b_hbm, down_hbm,
    low_hbm, active_hbm, slope_hbm, part_mine_hbm, part_other_hbm,
    rows_ref, extra_ref, adapt_a_ref, gate_up_ref, adapt_b_ref, down_ref,
    low_ref, active_ref, slope_ref, part_ref, total_ref, sems,
):
    copies = Copies(sems)
    half, features = mine_hbm.shape[0], rows_ref.shape[1]
    hidden_width = down_ref.shape[0]
    here_of = chunks_of(hidden_width, chunk)
    there_of = [slice(here.start + hidden_width, here.stop + hidden_width) for here in here_of]
    fetch_rows, fetch_extra = [], []
    for at, block in enumerate((mine_hbm, other_hbm)):
        to = pl.ds(at * half, half)
        fetch_rows.append(copies.start(block.at[:, :features], rows_ref.at[to]))
        fetch_extra.append(copies.start(block.at[:, features:], extra_ref.at[to]))
    fetch_rows.append(copies.start(adapt_a_hbm, adapt_a_ref))
    fetch_chunk = []
    for at, (here, there) in enumerate(zip(here_of, there_of)):
        moves = [copies.start(adapt_b_hbm, adapt_b_ref)] if at == 0 else []
        for cols in (here, there):
            moves.append(copies.start(gate_up_hbm.at[:, cols], gate_up_ref.at[:, cols]))
        moves.append(copies.start(down_hbm.at[here], down_ref.at[here]))
        fetch_chunk.append(moves)
    stores = []
    wait_all(fetch_rows)
    rows = rows_ref[...]
    low = dot(rows, adapt_a_ref[...]).astype(jnp.bfloat16)
    low_ref[...] = low
    stores.append(copies.start(low_ref, low_hbm))
    low_gate, low_up = halves(low)
    for here, there, moves in zip(here_of, there_of, fetch_chunk):
        wait_all(moves)
        adapt_b = adapt_b_ref[:, here]
        gate = dot(rows, gate_up_ref[:, here]) + ADAPTER_SCALE * dot(low_gate, adapt_b)
        up = dot(rows, gate_up_ref[:, there]) + ADAPTER_SCALE * dot(low_up, adapt_b)
        sigmoid_gate = jax.nn.sigmoid(gate)
        active = gate * sigmoid_gate
        active_ref[:, here] = active
        slope_ref[:, here] = up * (sigmoid_gate * (1.0 + gate * (1.0 - sigmoid_gate)))
        stores.append(copies.start(active_ref.at[:, here], active_hbm.at[:, here]))
        stores.append(copies.start(slope_ref.at[:, here], slope_hbm.at[:, here]))
        more = dot((active * up).astype(jnp.bfloat16), down_ref[here])
        if here.start == 0:
            total_ref[...] = more
        else:
            total_ref[...] += more
    wait_all(fetch_extra)
    w = joined_weight(extra_ref[...], slot_ref[0], slot_ref[1])
    out = total_ref[...].astype(jnp.bfloat16).astype(jnp.float32)
    part_ref[...] = (w * out).astype(jnp.bfloat16)
    stores.append(copies.start(part_ref.at[half:], part_other_hbm))
    stores.append(copies.start(part_ref.at[:half], part_mine_hbm))
    wait_all(stores)


def forward_stage(slot, mine, other, gate_up, down, adapt_a, adapt_b, chunk=256):
    hidden_width, features = down.shape
    half, both, ranks = mine.shape[0], 2 * mine.shape[0], adapt_a.shape[1]
    bf16, f32 = jnp.bfloat16, jnp.float32
    steps = hidden_width // chunk
    return pl.pallas_call(
        functools.partial(forward_kernel, chunk),
        out_shape=(
            jax.ShapeDtypeStruct((both, ranks), bf16),
            jax.ShapeDtypeStruct((both, hidden_width), f32),
            jax.ShapeDtypeStruct((both, hidden_width), f32),
            jax.ShapeDtypeStruct((half, features), bf16),
            jax.ShapeDtypeStruct((half, features), bf16),
        ),
        in_specs=[SMEM] + [ANY] * 6,
        out_specs=(ANY,) * 5,
        scratch_shapes=[
            pltpu.VMEM((both, features), bf16),
            pltpu.VMEM((both, EXTRA), bf16),
            pltpu.VMEM(adapt_a.shape, bf16),
            pltpu.VMEM(gate_up.shape, bf16),
            pltpu.VMEM(adapt_b.shape, bf16),
            pltpu.VMEM(down.shape, bf16),
            pltpu.VMEM((both, ranks), bf16),
            pltpu.VMEM((both, hidden_width), f32),
            pltpu.VMEM((both, hidden_width), f32),
            pltpu.VMEM((both, features), bf16),
            pltpu.VMEM((both, features), f32),
            pltpu.SemaphoreType.DMA((9 + 5 * steps,)),
        ],
        compiler_params=pltpu.CompilerParams(vmem_limit_bytes=60 * 2**20),
        cost_estimate=pl.CostEstimate(flops=10**6, bytes_accessed=10**4, transcendentals=0),
    )(slot, mine, other, adapt_a, gate_up, adapt_b, down)


def backward_kernel(chunk, adds, last, *refs):
    slot_ref, cot_mine, cot_other, mine_hbm, other_hbm, *refs = refs
    low_hbm, active_hbm, slope_hbm, adapt_b_hbm, down_hbm, *refs = refs
    grads_hbm, refs = refs[: 2 * adds], refs[2 * adds :]
    outs, refs = refs[: 2 + last], refs[2 + last :]
    cot_ref, scaled_ref, rows_ref, extra_ref, low_ref, active_ref, slope_ref, *refs = refs
    adapt_b_ref, down_ref, grad_a_ref, grad_b_ref, out_a_ref, out_b_ref, sems = refs
    copies = Copies(sems)
    half, features = cot_mine.shape
    here_of = chunks_of(down_ref.shape[0], chunk)
    first, fetch_rows, fetch_grads = [], [], []
    for at, cot in enumerate((cot_mine, cot_other)):
        first.append(copies.start(cot, cot_ref.at[pl.ds(at * half, half)]))
    for at, block in enumerate((mine_hbm, other_hbm)):
        first.append(copies.start(block.at[:, features:], extra_ref.at[pl.ds(at * half, half)]))
    first.append(copies.start(low_hbm, low_ref))
    first.append(copies.start(adapt_b_hbm, adapt_b_ref))
    fetch_chunk = [
        (
            copies.start(down_hbm.at[here], down_ref.at[here]),
            copies.start(active_hbm.at[:, here], active_ref.at[:, here]),
            copies.start(slope_hbm.at[:, here], slope_ref.at[:, here]),
        )
        for here in here_of
    ]
    for at, block in enumerate((mine_hbm, other_hbm)):
        to = rows_ref.at[pl.ds(at * half, half)]
        fetch_rows.append(copies.start(block.at[:, :features], to))
    for grad_hbm, grad_ref in zip(grads_hbm, (grad_a_ref, grad_b_ref)):
        fetch_grads.append(copies.start(grad_hbm, grad_ref))
    wait_all(first)
    w = joined_weight(extra_ref[...], slot_ref[0], slot_ref[1])
    scaled_ref[...] = (w * cot_ref[...].astype(jnp.float32)).astype(jnp.bfloat16)
    scaled = scaled_ref[...]
    low_gate, low_up = halves(low_ref[...])
    low_back = 0.0
    sums_b = []
    for here, moves in zip(here_of, fetch_chunk):
        wait_all(moves)
        adapt_b = adapt_b_ref[:, here]
        back = dot(scaled, down_ref[here], 1, 1)
        up_grad = (back * active_ref[:, here]).astype(jnp.bfloat16)
        gate_grad = (back * slope_ref[:, here]).astype(jnp.bfloat16)
        sum_b = dot(low_gate, gate_grad, 0, 0) + dot(low_up, up_grad, 0, 0)
        sums_b.append(ADAPTER_SCALE * sum_b)
        gate_back, up_back = dot(gate_grad, adapt_b, 1, 1), dot(up_grad, adapt_b, 1, 1)
        low_back = low_back + jnp.where(first_half(gate_back.shape), gate_back, up_back)
    wait_all(fetch_grads)
    for here, sum_b in zip(here_of, sums_b):
        total = sum_b + grad_b_ref[:, here] if adds else sum_b
        out_b_ref[:, here] = total.astype(out_b_ref.dtype)
    stores = [copies.start(out_b_ref, outs[-1])]
    low_grad = (ADAPTER_SCALE * low_back).astype(jnp.bfloat16)
    wait_all(fetch_rows)
    sum_a = dot(rows_ref[...], low_grad, 0, 0)
    total = sum_a + grad_a_ref[...] if adds else sum_a
    out_a_ref[...] = total.astype(out_a_ref.dtype)
    at = 0
    for out in outs[:-1]:
        stores.append(copies.start(out_a_ref.at[pl.ds(at, out.shape[0])], out))
        at += out.shape[0]
    wait_all(stores)


def backward_stage(slot, cots, blocks, saved, down, adapt_b, grads=(), cut=None, chunk=256):
    low, active, slope = saved
    hidden_width, features = down.shape
    both, ranks = low.shape
    bf16, f32 = jnp.bfloat16, jnp.float32
    out_dtype = f32 if cut is None else bf16
    rows_of = [features] if cut is None else [cut, features - cut]
    outs = [(rows, ranks) for rows in rows_of] + [(ranks, hidden_width)]
    operands = (*cots, *blocks, low, active, slope, adapt_b, down, *grads)
    steps = hidden_width // chunk
    return pl.pallas_call(
        functools.partial(backward_kernel, chunk, len(grads) // 2, int(cut is not None)),
        out_shape=tuple(jax.ShapeDtypeStruct(shape, out_dtype) for shape in outs),
        in_specs=[SMEM] + [ANY] * len(operands),
        out_specs=(ANY,) * len(outs),
        scratch_shapes=[
            pltpu.VMEM((both, features), bf16),
            pltpu.VMEM((both, features), bf16),
            pltpu.VMEM((both, features), bf16),
            pltpu.VMEM((both, EXTRA), bf16),
            pltpu.VMEM(low.shape, bf16),
            pltpu.VMEM(active.shape, f32),
            pltpu.VMEM(slope.shape, f32),
            pltpu.VMEM(adapt_b.shape, bf16),
            pltpu.VMEM(down.shape, bf16),
            pltpu.VMEM((features, ranks), f32),
            pltpu.VMEM((ranks, hidden_width), f32),
            pltpu.VMEM((features, ranks), out_dtype),
            pltpu.VMEM((ranks, hidden_width), out_dtype),
            pltpu.SemaphoreType.DMA((13 + 3 * steps,)),
        ],
        compiler_params=pltpu.CompilerParams(vmem_limit_bytes=60 * 2**20),
        cost_estimate=pl.CostEstimate(flops=10**6, bytes_accessed=10**4, transcendentals=0),
    )(slot, *operands)


def z_pairs(*moves):
    return [(2 * a + core, 2 * b + core) for a, b in moves for core in (0, 1)]


ALL_SWAP = z_pairs((0, 1), (1, 0), (2, 3), (3, 2))
MID_SWAP = z_pairs((1, 2), (2, 1))
SIBLING = [(e, e ^ 1) for e in range(8)]


def send(array, pairs):
    return lax.ppermute(array, "expert", pairs)


def fence(*arrays):
    return lax.optimization_barrier(arrays)


def add_rounded(*terms):
    total = terms[0].astype(jnp.float32)
    for term in terms[1:]:
        total = total + term.astype(jnp.float32)
    return total.astype(jnp.bfloat16)


def sibling(block):
    return send(block, SIBLING)


def dp_swap(array, bit):
    return lax.ppermute(array, "dp", [(d, d ^ bit) for d in range(4)])


def rounded_sum(one, other):
    return lax.reduce_precision(one.astype(jnp.float32) + other.astype(jnp.float32), 8, 7)


def group_sum(x_first, *y_first):
    totals = []
    for array, bits in ((x_first, (1, 2)), *((array, (2, 1)) for array in y_first)):
        pair = rounded_sum(array, dp_swap(array, bits[0]))
        totals.append(pair + dp_swap(pair.astype(jnp.bfloat16), bits[1]).astype(jnp.float32))
    return totals


def dense_body(
    tokens,
    cotangent,
    routing,
    router_route_weights,
    route_replica_choice,
    device_expert_table,
    gate_up_weight,
    down_weight,
    adapter_down_maps,
    adapter_up_maps,
):
    slot_total = lax.axis_size("expert")
    capacity = tokens.shape[0] * routing.shape[1] // slot_total
    me = lax.axis_index("expert")
    chip = me // 2
    inner = (chip == 1) | (chip == 2)
    gate_up, down = gate_up_weight[0], down_weight[0]
    adapt_a = adapter_down_maps[0]
    adapt_b = adapter_up_maps[0].reshape(adapt_a.shape[1], -1)

    slot = jnp.stack([me, jnp.int32(slot_total)])

    def forward(mine, twin):
        *saved, part, away = forward_stage(slot, mine, twin, gate_up, down, adapt_a, adapt_b)
        return saved, part, away

    def backward(cots, rows, saved, grads=(), cut=None):
        return backward_stage(slot, cots, rows, saved, down, adapt_b, grads, cut)

    def pick(inside, outside):
        return jnp.where(inner, inside, outside)

    tokens = tagged_tokens(
        tokens, routing, router_route_weights, route_replica_choice, device_expert_table, capacity
    )
    tok_swap = send(tokens, ALL_SWAP)
    tok_mid = send(tokens, MID_SWAP)
    rows0 = (tokens, sibling(tokens))
    saved0, part0, away0 = forward(*rows0)
    tok_swap, tok_mid, part0, away0, cotangent = fence(tok_swap, tok_mid, part0, away0, cotangent)

    tok_out2 = send(tok_mid, ALL_SWAP)
    tok_mid2 = send(tok_swap, MID_SWAP)
    rows1 = (tok_swap, sibling(tok_swap))
    saved1, part1, away1 = forward(*rows1)
    tok_mid, tok_out2, tok_mid2, part1, away1, cotangent = fence(
        tok_mid, tok_out2, tok_mid2, part1, away1, cotangent
    )

    tok_out3 = send(tok_mid2, ALL_SWAP)
    cot_mid = send(cotangent, MID_SWAP)
    tok_second = pick(tok_mid, tok_out2)
    rows2 = (tok_second, sibling(tok_second))
    saved2, part2, away2 = forward(*rows2)
    tok_mid2, tok_out3, cot_mid, part2, away2, cotangent = fence(
        tok_mid2, tok_out3, cot_mid, part2, away2, cotangent
    )

    cot_swap = send(cotangent, ALL_SWAP)
    tok_third = pick(tok_mid2, tok_out3)
    rows3 = (tok_third, sibling(tok_third))
    saved3, part3, away3 = forward(*rows3)
    cot_swap, cot_mid, part0, away0, part1, away1, part2, away2, part3, away3, cotangent = fence(
        cot_swap, cot_mid, part0, away0, part1, away1, part2, away2, part3, away3, cotangent
    )

    cot_out2 = send(cot_mid, ALL_SWAP)
    cot_mid2 = send(cot_swap, MID_SWAP)
    grads = backward((cotangent, sibling(cotangent)), rows0, saved0)
    part3 = add_rounded(part3, sibling(away3))
    cot_mid, cot_out2, cot_mid2, cot_swap, part2, away2, part3, grads = fence(
        cot_mid, cot_out2, cot_mid2, cot_swap, part2, away2, part3, grads
    )

    swap6 = send(pick(cot_mid2, part3), ALL_SWAP)
    grads = backward((cot_swap, sibling(cot_swap)), rows1, saved1, grads)
    cot_second = pick(cot_mid, cot_out2)
    grads = backward((cot_second, sibling(cot_second)), rows2, saved2, grads)
    part2 = add_rounded(part2, sibling(away2))
    swap6, cot_mid2, part0, away0, part1, away1, part2, part3, grads = fence(
        swap6, cot_mid2, part0, away0, part1, away1, part2, part3, grads
    )

    second_in = send(part2, ALL_SWAP)
    third_mid = send(add_rounded(part3, swap6), MID_SWAP)
    cot_third = pick(cot_mid2, swap6)
    cut = (adapt_a.size + adapt_b.size) // 2 // adapt_a.shape[1] // 16 * 16
    grads = backward((cot_third, sibling(cot_third)), rows3, saved3, grads, cut)
    grad_a_top, grad_a_rest, grad_b = group_sum(*grads)
    part1 = add_rounded(part1, sibling(away1))
    part0 = add_rounded(part0, sibling(away0))
    first_swap = send(add_rounded(part1, third_mid), ALL_SWAP)
    second_mid = send(add_rounded(part2, second_in), MID_SWAP)
    mixed = add_rounded(part0, first_swap, second_mid)
    grad_a = jnp.concatenate([grad_a_top, grad_a_rest])
    return mixed, grad_a[None], grad_b.reshape(adapter_up_maps.shape)


def body(*arrays):
    if (lax.axis_size("dp"), lax.axis_size("expert"), arrays[2].shape[1]) == (4, 8, 8):
        return dense_body(*arrays)
    return sparse_body(*arrays)


def solution(mesh):
    return jax.shard_map(
        body,
        mesh=mesh,
        in_specs=(
            P(("dp", "expert"), None),
            P(("dp", "expert"), None),
            P(("dp", "expert"), None),
            P(("dp", "expert"), None),
            P(("dp", "expert"), None),
            P(),
            P("expert", None, None),
            P("expert", None, None),
            P("expert", None, None),
            P("expert", None, None, None),
        ),
        out_specs=(
            P(("dp", "expert"), None),
            P("expert", None, None),
            P("expert", None, None, None),
        ),
        check_vma=False,
    )
```

```python
import functools

import jax
import jax.numpy as jnp
from jax import lax
from jax.experimental import pallas as pl
from jax.experimental.pallas import tpu as pltpu
from jax.sharding import PartitionSpec as P

ADAPTER_SCALE = 0.5


def route_rows(routing, route_replica_choice, device_expert_table, capacity):
    slot_total = device_expert_table.shape[0]
    route_total = routing.shape[0] * routing.shape[1]
    expert_flat = routing.reshape(-1)
    holds_mask = (expert_flat[:, None] == device_expert_table[None, :]).astype(jnp.int32)
    copies = jnp.sum(holds_mask, axis=1)
    wanted = route_replica_choice.reshape(-1) % copies
    before = jnp.cumsum(holds_mask, axis=1) - holds_mask
    picked = holds_mask * (before == wanted[:, None]).astype(jnp.int32)
    ahead_of = jnp.cumsum(picked, axis=0) - picked
    position = jnp.sum(picked * ahead_of, axis=1)
    target = jnp.sum(picked * jnp.arange(slot_total, dtype=jnp.int32)[None, :], axis=1)
    kept_mask = position < capacity
    dest_index = jnp.where(kept_mask, target * capacity + position, slot_total * capacity)
    source = jnp.full((slot_total * capacity,), route_total, jnp.int32)
    source = source.at[dest_index].set(jnp.arange(route_total, dtype=jnp.int32), mode="drop")
    return (kept_mask, dest_index, source)


def expert_apply_forward(rows_in, gate_up, down, adapt_a, adapt_b):
    adapter_rank_count = adapt_b.shape[1]
    hidden_width = adapt_b.shape[2]
    reduced_rank_rows = jnp.dot(rows_in, adapt_a, preferred_element_type=jnp.float32).astype(
        jnp.bfloat16
    )
    base_preactivation = jnp.dot(rows_in, gate_up, preferred_element_type=jnp.float32)
    adapter_gate_delta = jnp.dot(
        reduced_rank_rows[:, :adapter_rank_count], adapt_b[0], preferred_element_type=jnp.float32
    )
    adapter_up_delta = jnp.dot(
        reduced_rank_rows[:, adapter_rank_count:], adapt_b[1], preferred_element_type=jnp.float32
    )
    gate_preactivation = base_preactivation[:, :hidden_width] + ADAPTER_SCALE * adapter_gate_delta
    up_preactivation = base_preactivation[:, hidden_width:] + ADAPTER_SCALE * adapter_up_delta
    sigmoid_gate = jax.nn.sigmoid(gate_preactivation)
    active = gate_preactivation * sigmoid_gate
    hidden = (active * up_preactivation).astype(jnp.bfloat16)
    layer_output = jnp.dot(hidden, down, preferred_element_type=jnp.float32).astype(jnp.bfloat16)
    return (
        layer_output,
        (reduced_rank_rows, gate_preactivation, up_preactivation, sigmoid_gate, active),
    )


def expert_backward(rows_in, scaled, down, adapt_b, saved_residuals):
    reduced_rank_rows, gate_preactivation, up_preactivation, sigmoid_gate, active = saved_residuals
    adapter_rank_count = adapt_b.shape[1]
    back_hidden = lax.dot_general(
        scaled, down, (((1,), (1,)), ((), ())), preferred_element_type=jnp.float32
    )
    up_preactivation_gradient = (back_hidden * active).astype(jnp.bfloat16)
    slope = sigmoid_gate * (1.0 + gate_preactivation * (1.0 - sigmoid_gate))
    gate_preactivation_gradient = (back_hidden * up_preactivation * slope).astype(jnp.bfloat16)
    row_dimension_numbers = (((0,), (0,)), ((), ()))
    gate_up_map_gradient = ADAPTER_SCALE * lax.dot_general(
        reduced_rank_rows[:, :adapter_rank_count],
        gate_preactivation_gradient,
        row_dimension_numbers,
        preferred_element_type=jnp.float32,
    )
    up_map_gradient = ADAPTER_SCALE * lax.dot_general(
        reduced_rank_rows[:, adapter_rank_count:],
        up_preactivation_gradient,
        row_dimension_numbers,
        preferred_element_type=jnp.float32,
    )
    cols_dims = (((1,), (1,)), ((), ()))
    gate_reduced_rows = lax.dot_general(
        gate_preactivation_gradient, adapt_b[0], cols_dims, preferred_element_type=jnp.float32
    )
    up_reduced_rows = lax.dot_general(
        up_preactivation_gradient, adapt_b[1], cols_dims, preferred_element_type=jnp.float32
    )
    reduced_gradient = (
        ADAPTER_SCALE * jnp.concatenate([gate_reduced_rows, up_reduced_rows], axis=1)
    ).astype(jnp.bfloat16)
    grad_adapt_a = lax.dot_general(
        rows_in, reduced_gradient, row_dimension_numbers, preferred_element_type=jnp.float32
    )
    return (grad_adapt_a, jnp.stack([gate_up_map_gradient, up_map_gradient]))


def sparse_body(
    tokens,
    cotangent,
    routing,
    router_route_weights,
    route_replica_choice,
    device_expert_table,
    gate_up_weight,
    down_weight,
    adapter_down_maps,
    adapter_up_maps,
):
    slot_total = lax.axis_size("expert")
    tok_rows = tokens.shape[0]
    model_feature_width = tokens.shape[1]
    top_routes = routing.shape[1]
    route_total = tok_rows * top_routes
    capacity = route_total // slot_total
    kept_mask, dest_index, source = route_rows(
        routing, route_replica_choice, device_expert_table, capacity
    )
    valid_route_mask = source < route_total
    safe_route = jnp.minimum(source, route_total - 1)
    route_token_index = safe_route // top_routes
    weight_flat = router_route_weights.reshape(-1)
    route_weight_rows = weight_flat[safe_route]
    zero_row = jnp.zeros((), jnp.bfloat16)
    rows_out = jnp.where(valid_route_mask[:, None], tokens[route_token_index], zero_row).reshape(
        slot_total, capacity, model_feature_width
    )
    product = (
        route_weight_rows[:, None] * cotangent[route_token_index].astype(jnp.float32)
    ).astype(jnp.bfloat16)
    scaled_out = jnp.where(valid_route_mask[:, None], product, zero_row).reshape(
        slot_total, capacity, model_feature_width
    )
    rows_in = lax.all_to_all(rows_out, "expert", split_axis=0, concat_axis=0, tiled=True)
    flattened_rows = rows_in.reshape(-1, model_feature_width)
    layer_output, saved_residuals = expert_apply_forward(
        flattened_rows, gate_up_weight[0], down_weight[0], adapter_down_maps[0], adapter_up_maps[0]
    )
    returned = lax.all_to_all(
        layer_output.reshape(slot_total, capacity, model_feature_width),
        "expert",
        split_axis=0,
        concat_axis=0,
        tiled=True,
    )
    returned = returned.reshape(-1, model_feature_width)
    picked_rows = returned[jnp.minimum(dest_index, slot_total * capacity - 1)]
    weighted = jnp.where(
        kept_mask[:, None],
        weight_flat[:, None] * picked_rows.astype(jnp.float32),
        jnp.zeros((), jnp.float32),
    )
    mixed = jnp.sum(weighted.reshape(tok_rows, top_routes, model_feature_width), axis=1).astype(
        jnp.bfloat16
    )
    scaled_input_rows = lax.all_to_all(
        scaled_out, "expert", split_axis=0, concat_axis=0, tiled=True
    )
    grad_adapt_a, grad_adapt_b = expert_backward(
        flattened_rows,
        scaled_input_rows.reshape(-1, model_feature_width),
        down_weight[0],
        adapter_up_maps[0],
        saved_residuals,
    )
    piece_a = grad_adapt_a.reshape(slot_total, -1)
    piece_b = grad_adapt_b.reshape(slot_total, -1)
    expert_total = max(top_routes, slot_total // 2)
    members = (
        jnp.arange(expert_total, dtype=jnp.int32)[:, None] == device_expert_table[None, :]
    ).astype(jnp.float32)
    piece_a, piece_b = lax.psum((piece_a, piece_b), "dp")
    got_a, got_b = (
        lax.all_to_all(piece_a, "expert", split_axis=0, concat_axis=0, tiled=True),
        lax.all_to_all(piece_b, "expert", split_axis=0, concat_axis=0, tiled=True),
    )
    expert_a = jnp.dot(members, got_a, precision=lax.Precision.HIGHEST)
    expert_b = jnp.dot(members, got_b, precision=lax.Precision.HIGHEST)
    back_dims = (((0,), (0,)), ((), ()))
    spread_a = lax.dot_general(members, expert_a, back_dims, precision=lax.Precision.HIGHEST)
    spread_b = lax.dot_general(members, expert_b, back_dims, precision=lax.Precision.HIGHEST)
    summed_a, summed_b = (
        lax.all_to_all(spread_a, "expert", split_axis=0, concat_axis=0, tiled=True),
        lax.all_to_all(spread_b, "expert", split_axis=0, concat_axis=0, tiled=True),
    )
    grad_a = summed_a.reshape(grad_adapt_a.shape)[None]
    grad_b = summed_b.reshape(grad_adapt_b.shape)[None]
    return (mixed, grad_a, grad_b)


def dot(a, b, a_dim=1, b_dim=0):
    return lax.dot_general(
        a, b, (((a_dim,), (b_dim,)), ((), ())), preferred_element_type=jnp.float32
    )


def first_half(shape):
    return lax.broadcasted_iota(jnp.int32, shape, 1) < shape[1] // 2


def halves(low):
    gate = first_half(low.shape)
    zero = jnp.zeros_like(low)
    return jnp.where(gate, low, zero), jnp.where(gate, zero, low)


def split_weights(table):
    parts = []
    for _ in range(3):
        part = table.astype(jnp.bfloat16).astype(jnp.float32)
        parts.append(part)
        table = table - part
    slot_total, tok_rows = table.shape
    parts.append(jnp.zeros((tok_rows - 3 * slot_total, tok_rows), jnp.float32))
    return jnp.transpose(jnp.concatenate(parts)).astype(jnp.bfloat16)


def joined_weight(extra, slot, slot_total):
    lane = lax.broadcasted_iota(jnp.int32, extra.shape, 1)
    mine = lane == slot
    for part in range(1, 3):
        mine = mine | (lane == slot + part * slot_total)
    chosen = jnp.where(mine, extra.astype(jnp.float32), 0.0)
    return jnp.sum(chosen, axis=1, keepdims=True)


def tagged_kernel(capacity, table_ref, expert_ref, choice_ref, weight_ref, tokens_ref, out_ref):
    slot_total = table_ref.shape[0]
    tok_rows, features = tokens_ref.shape
    out_ref[:, :features] = tokens_ref[...]
    experts, weights = expert_ref[...], weight_ref[...]
    holds = [experts == table_ref[s] for s in range(slot_total)]
    counts = [hold.astype(jnp.float32) for hold in holds]
    copies = sum(counts)
    choice = choice_ref[...].astype(jnp.float32)
    wanted = choice - copies * jnp.floor((choice + 0.5) / copies)
    before = jnp.zeros_like(copies)
    taken, route_weight = [], []
    for hold, count in zip(holds, counts):
        picked = jnp.where(hold & (before == wanted), 1.0, 0.0)
        before = before + count
        taken.append(jnp.sum(picked, axis=0, keepdims=True))
        route_weight.append(jnp.sum(picked * weights, axis=0, keepdims=True))
    shape = (tok_rows, tok_rows)
    earlier = lax.broadcasted_iota(jnp.int32, shape, 0) < lax.broadcasted_iota(jnp.int32, shape, 1)
    rank = dot(
        jnp.concatenate(taken).astype(jnp.bfloat16),
        jnp.where(earlier, 1.0, 0.0).astype(jnp.bfloat16),
    )
    table = jnp.where(rank < capacity, jnp.concatenate(route_weight), 0.0)
    out_ref[:, features:] = split_weights(table)


VMEM = pl.BlockSpec(memory_space=pltpu.VMEM)
SMEM = pl.BlockSpec(memory_space=pltpu.SMEM)
EXTRA = 128


def tagged_tokens(tokens, routing, weights, choice, table, capacity):
    tok_rows, features = tokens.shape
    return pl.pallas_call(
        functools.partial(tagged_kernel, capacity),
        out_shape=jax.ShapeDtypeStruct((tok_rows, features + EXTRA), tokens.dtype),
        in_specs=[SMEM, VMEM, VMEM, VMEM, VMEM],
        out_specs=VMEM,
    )(table, routing.T, choice.T, weights.T, tokens)


def stage_call(kernel, outs, scratch, macs, operands):
    out_shape = tuple(jax.ShapeDtypeStruct(*out) for out in outs)
    moved = sum(array.size * array.dtype.itemsize for array in (*operands, *out_shape))
    return pl.pallas_call(
        kernel,
        out_shape=out_shape,
        in_specs=[SMEM] + [VMEM] * (len(operands) - 1),
        out_specs=(VMEM,) * len(outs),
        scratch_shapes=[pltpu.VMEM(*shape) for shape in scratch],
        compiler_params=pltpu.CompilerParams(vmem_limit_bytes=16 * 2**20),
        cost_estimate=pl.CostEstimate(flops=2 * macs, bytes_accessed=moved, transcendentals=0),
    )(*operands)


def forward_kernel(
    chunk, slot_ref, mine_ref, other_ref, adapt_a_ref, gate_up_ref, adapt_b_ref, down_ref,
    low_ref, active_ref, slope_ref, part_mine_ref, part_other_ref, rows_ref, total_ref,
):
    half, features = part_mine_ref.shape
    hidden_width = down_ref.shape[0]
    rows_ref[:half] = mine_ref[:, :features]
    rows_ref[half:] = other_ref[:, :features]
    rows = rows_ref[...]
    low = dot(rows, adapt_a_ref[...]).astype(jnp.bfloat16)
    low_ref[...] = low
    low_gate, low_up = halves(low)
    for start in range(0, hidden_width, chunk):
        here = slice(start, start + chunk)
        there = slice(hidden_width + start, hidden_width + start + chunk)
        adapt_b = adapt_b_ref[:, here]
        gate = dot(rows, gate_up_ref[:, here]) + ADAPTER_SCALE * dot(low_gate, adapt_b)
        up = dot(rows, gate_up_ref[:, there]) + ADAPTER_SCALE * dot(low_up, adapt_b)
        sigmoid_gate = jax.nn.sigmoid(gate)
        active = gate * sigmoid_gate
        active_ref[:, here] = active
        slope_ref[:, here] = up * (sigmoid_gate * (1.0 + gate * (1.0 - sigmoid_gate)))
        more = dot((active * up).astype(jnp.bfloat16), down_ref[here])
        if start == 0:
            total_ref[...] = more
        else:
            total_ref[...] += more
    out = total_ref[...].astype(jnp.bfloat16).astype(jnp.float32)
    for block_ref, part_ref, out in (
        (mine_ref, part_mine_ref, out[:half]),
        (other_ref, part_other_ref, out[half:]),
    ):
        w = joined_weight(block_ref[:, features:], slot_ref[0], slot_ref[1])
        part_ref[...] = (w * out).astype(jnp.bfloat16)


def forward_stage(slot, mine, other, gate_up, down, adapt_a, adapt_b, chunk=256):
    hidden_width, features = down.shape
    half, both, ranks = mine.shape[0], 2 * mine.shape[0], adapt_a.shape[1]
    bf16, f32 = jnp.bfloat16, jnp.float32
    saved = ((both, hidden_width), f32)
    part = ((half, features), bf16)
    return stage_call(
        functools.partial(forward_kernel, chunk),
        (((both, ranks), bf16), saved, saved, part, part),
        [((both, features), bf16), ((both, features), f32)],
        both * (gate_up.size + down.size + adapt_a.size),
        (slot, mine, other, adapt_a, gate_up, adapt_b, down),
    )


def backward_kernel(chunk, adds, cut, *refs):
    slot_ref, cot_mine, cot_other, mine_ref, other_ref, *refs = refs
    low_ref, active_ref, slope_ref, adapt_b_ref, down_ref, *refs = refs
    grads, (out_a_ref, out_b_ref, scaled_ref, rows_ref) = refs[: 2 * adds], refs[2 * adds :]
    half, features = cot_mine.shape
    for at, (cot_ref, block_ref) in enumerate(((cot_mine, mine_ref), (cot_other, other_ref))):
        here = slice(at * half, (at + 1) * half)
        w = joined_weight(block_ref[:, features:], slot_ref[0], slot_ref[1])
        scaled_ref[here] = (w * cot_ref[...].astype(jnp.float32)).astype(jnp.bfloat16)
        rows_ref[here] = block_ref[:, :features]
    scaled = scaled_ref[...]
    low_gate, low_up = halves(low_ref[...])
    low_back = 0.0
    for start in range(0, down_ref.shape[0], chunk):
        here = slice(start, start + chunk)
        adapt_b = adapt_b_ref[:, here]
        back = dot(scaled, down_ref[here], 1, 1)
        up_grad = (back * active_ref[:, here]).astype(jnp.bfloat16)
        gate_grad = (back * slope_ref[:, here]).astype(jnp.bfloat16)
        sum_b = ADAPTER_SCALE * (dot(low_gate, gate_grad, 0, 0) + dot(low_up, up_grad, 0, 0))
        sum_b = sum_b + grads[1][:, here] if adds else sum_b
        if cut is None:
            out_b_ref[:, here] = sum_b
        else:
            ranks = sum_b.shape[0]
            for col in range(0, chunk, ranks):
                at = features - cut + start + col
                out_b_ref[at : at + ranks] = sum_b[:, col : col + ranks].astype(jnp.bfloat16)
        gate_back, up_back = dot(gate_grad, adapt_b, 1, 1), dot(up_grad, adapt_b, 1, 1)
        low_back = low_back + jnp.where(first_half(gate_back.shape), gate_back, up_back)
    low_grad = (ADAPTER_SCALE * low_back).astype(jnp.bfloat16)
    sum_a = dot(rows_ref[...], low_grad, 0, 0)
    sum_a = sum_a + grads[0][...] if adds else sum_a
    if cut is None:
        out_a_ref[...] = sum_a
    else:
        out_a_ref[...] = sum_a[:cut].astype(jnp.bfloat16)
        out_b_ref[: features - cut] = sum_a[cut:].astype(jnp.bfloat16)


def backward_stage(slot, cots, blocks, saved, down, adapt_b, grads=(), cut=None, chunk=256):
    hidden_width, features = down.shape
    both, ranks = saved[0].shape
    bf16, f32 = jnp.bfloat16, jnp.float32
    outs = (((features, ranks), f32), ((ranks, hidden_width), f32))
    if cut is not None:
        outs = (((cut, ranks), bf16), ((features - cut + hidden_width, ranks), bf16))
    return stage_call(
        functools.partial(backward_kernel, chunk, len(grads) // 2, cut),
        outs,
        [((both, features), bf16), ((both, features), bf16)],
        both * (down.size + features * ranks + 4 * adapt_b.size),
        (slot, *cots, *blocks, *saved, adapt_b, down, *grads),
    )


def pair_kernel(*refs):
    for one_ref, other_ref, out_ref in zip(refs[:2], refs[2:4], refs[4:]):
        total = one_ref[...].astype(jnp.float32) + other_ref[...].astype(jnp.float32)
        out_ref[...] = total.astype(out_ref.dtype)


def pair_sums(ones, others):
    return pl.pallas_call(
        pair_kernel,
        out_shape=tuple(jax.ShapeDtypeStruct(one.shape, one.dtype) for one in ones),
        in_specs=[VMEM] * 4,
        out_specs=(VMEM,) * 2,
    )(*ones, *others)


def finish_kernel(one_x, one_y, other_x, other_y, grad_a_ref, grad_b_ref):
    cut, ranks = one_x.shape
    rest = grad_a_ref.shape[0] - cut
    grad_a_ref[:cut] = one_x[...].astype(jnp.float32) + other_x[...].astype(jnp.float32)
    total = one_y[...].astype(jnp.float32) + other_y[...].astype(jnp.float32)
    grad_a_ref[cut:] = total[:rest]
    for col in range(0, grad_b_ref.shape[1], ranks):
        grad_b_ref[:, col : col + ranks] = total[rest + col : rest + col + ranks]


def finished(ones, others, features, hidden_width):
    ranks = ones[0].shape[1]
    shapes = ((features, ranks), (ranks, hidden_width))
    return pl.pallas_call(
        finish_kernel,
        grid=(1,),
        out_shape=tuple(jax.ShapeDtypeStruct(shape, jnp.float32) for shape in shapes),
        in_specs=[pl.BlockSpec(one.shape, lambda j: (0, 0)) for one in (*ones, *others)],
        out_specs=tuple(pl.BlockSpec(shape, lambda j: (0, 0)) for shape in shapes),
    )(*ones, *others)


def z_pairs(*moves):
    return [(2 * a + core, 2 * b + core) for a, b in moves for core in (0, 1)]


ALL_SWAP = z_pairs((0, 1), (1, 0), (2, 3), (3, 2))
MID_SWAP = z_pairs((1, 2), (2, 1))
SIBLING = [(e, e ^ 1) for e in range(8)]


def send(array, pairs):
    return lax.ppermute(array, "expert", pairs)


def fence(*arrays):
    return lax.optimization_barrier(arrays)


def add_rounded(*terms):
    total = terms[0].astype(jnp.float32)
    for term in terms[1:]:
        total = total + term.astype(jnp.float32)
    return total.astype(jnp.bfloat16)


def sibling(block):
    return send(block, SIBLING)


def dp_swap(array, bit):
    return lax.ppermute(array, "dp", [(d, d ^ bit) for d in range(4)])


def group_sum(mine, features, hidden_width):
    got = dp_swap(mine[0], 1), dp_swap(mine[1], 2)
    pairs = pair_sums(mine, got)
    got = dp_swap(pairs[0], 2), dp_swap(pairs[1], 1)
    return finished(pairs, got, features, hidden_width)


def dense_body(
    tokens,
    cotangent,
    routing,
    router_route_weights,
    route_replica_choice,
    device_expert_table,
    gate_up_weight,
    down_weight,
    adapter_down_maps,
    adapter_up_maps,
):
    slot_total = lax.axis_size("expert")
    capacity = tokens.shape[0] * routing.shape[1] // slot_total
    me = lax.axis_index("expert")
    chip = me // 2
    inner = (chip == 1) | (chip == 2)
    gate_up, down = gate_up_weight[0], down_weight[0]
    adapt_a = adapter_down_maps[0]
    adapt_b = adapter_up_maps[0].reshape(adapt_a.shape[1], -1)

    slot = jnp.stack([me, jnp.int32(slot_total)])

    def forward(mine, twin):
        *saved, part, away = forward_stage(slot, mine, twin, gate_up, down, adapt_a, adapt_b)
        return saved, part, away

    def backward(cots, rows, saved, grads=(), cut=None):
        return backward_stage(slot, cots, rows, saved, down, adapt_b, grads, cut)

    def pick(inside, outside):
        return jnp.where(inner, inside, outside)

    def after(array, earlier):
        return fence(array, earlier)[0]

    tokens = tagged_tokens(
        tokens, routing, router_route_weights, route_replica_choice, device_expert_table, capacity
    )
    tok_swap = send(tokens, ALL_SWAP)
    twin = sibling(tokens)
    rows0 = (tokens, twin)
    tok_mid = send(after(tokens, twin), MID_SWAP)
    tok_swap, tok_mid, rows0, cotangent = fence(tok_swap, tok_mid, rows0, cotangent)

    tok_out2 = send(tok_mid, ALL_SWAP)
    twin = sibling(tok_swap)
    rows1 = (tok_swap, twin)
    tok_mid2 = send(after(tok_swap, twin), MID_SWAP)
    saved0, part0, away0 = forward(*rows0)
    tok_mid, tok_out2, tok_mid2, rows1, part0, away0, cotangent = fence(
        tok_mid, tok_out2, tok_mid2, rows1, part0, away0, cotangent
    )

    tok_out3 = send(tok_mid2, ALL_SWAP)
    tok_second = pick(tok_mid, tok_out2)
    twin = sibling(tok_second)
    rows2 = (tok_second, twin)
    cot_mid = send(after(cotangent, twin), MID_SWAP)
    saved1, part1, away1 = forward(*rows1)
    tok_mid2, tok_out3, cot_mid, rows2, part1, away1, cotangent = fence(
        tok_mid2, tok_out3, cot_mid, rows2, part1, away1, cotangent
    )

    cot_swap = send(cotangent, ALL_SWAP)
    tok_third = pick(tok_mid2, tok_out3)
    rows3 = (tok_third, sibling(tok_third))
    cots0 = (cotangent, sibling(cotangent))
    saved2, part2, away2 = forward(*rows2)
    saved3, part3, away3 = forward(*rows3)
    cot_swap, cot_mid, cots0, part2, away2, part3, away3 = fence(
        cot_swap, cot_mid, cots0, part2, away2, part3, away3
    )

    cot_out2 = send(cot_mid, ALL_SWAP)
    twin = sibling(cot_swap)
    cots1 = (cot_swap, twin)
    cot_mid2 = send(after(cot_swap, twin), MID_SWAP)
    part3 = add_rounded(part3, sibling(away3))
    grads = backward(cots0, rows0, saved0)
    grads = backward(cots1, rows1, saved1, grads)
    cot_mid, cot_out2, cot_mid2, part2, away2, part3, grads = fence(
        cot_mid, cot_out2, cot_mid2, part2, away2, part3, grads
    )

    swap6 = send(pick(cot_mid2, part3), ALL_SWAP)
    cot_second = pick(cot_mid, cot_out2)
    cots2 = (cot_second, sibling(cot_second))
    grads = backward(cots2, rows2, saved2, grads)
    part2 = add_rounded(part2, sibling(away2))
    swap6, cot_mid2, part0, away0, part1, away1, part2, part3, grads = fence(
        swap6, cot_mid2, part0, away0, part1, away1, part2, part3, grads
    )

    second_in = send(part2, ALL_SWAP)
    cot_third = pick(cot_mid2, swap6)
    twin = sibling(cot_third)
    third_mid = send(after(add_rounded(part3, swap6), twin), MID_SWAP)
    features, hidden_width = adapt_a.shape[0], adapt_b.shape[1]
    cut = (features + hidden_width) // 2
    grads = backward((cot_third, twin), rows3, saved3, grads, cut)
    grad_a, grad_b = group_sum(grads, features, hidden_width)
    part1 = add_rounded(part1, sibling(away1))
    part0 = add_rounded(part0, sibling(away0))
    first_swap = send(add_rounded(part1, third_mid), ALL_SWAP)
    second_mid = send(add_rounded(part2, second_in), MID_SWAP)
    mixed = add_rounded(part0, first_swap, second_mid)
    return mixed, grad_a[None], grad_b.reshape(adapter_up_maps.shape)


def body(*arrays):
    if (lax.axis_size("dp"), lax.axis_size("expert"), arrays[2].shape[1]) == (4, 8, 8):
        return dense_body(*arrays)
    return sparse_body(*arrays)


def solution(mesh):
    return jax.shard_map(
        body,
        mesh=mesh,
        in_specs=(
            P(("dp", "expert"), None),
            P(("dp", "expert"), None),
            P(("dp", "expert"), None),
            P(("dp", "expert"), None),
            P(("dp", "expert"), None),
            P(),
            P("expert", None, None),
            P("expert", None, None),
            P("expert", None, None),
            P("expert", None, None, None),
        ),
        out_specs=(
            P(("dp", "expert"), None),
            P("expert", None, None),
            P("expert", None, None, None),
        ),
        check_vma=False,
    )
```

```python
import functools

import jax
import jax.numpy as jnp
from jax import lax
from jax.experimental import pallas as pl
from jax.experimental.pallas import tpu as pltpu
from jax.sharding import PartitionSpec as P

ADAPTER_SCALE = 0.5


def route_rows(routing, route_replica_choice, device_expert_table, capacity):
    slot_total = device_expert_table.shape[0]
    route_total = routing.shape[0] * routing.shape[1]
    expert_flat = routing.reshape(-1)
    holds_mask = (expert_flat[:, None] == device_expert_table[None, :]).astype(jnp.int32)
    copies = jnp.sum(holds_mask, axis=1)
    wanted = route_replica_choice.reshape(-1) % copies
    before = jnp.cumsum(holds_mask, axis=1) - holds_mask
    picked = holds_mask * (before == wanted[:, None]).astype(jnp.int32)
    ahead_of = jnp.cumsum(picked, axis=0) - picked
    position = jnp.sum(picked * ahead_of, axis=1)
    target = jnp.sum(picked * jnp.arange(slot_total, dtype=jnp.int32)[None, :], axis=1)
    kept_mask = position < capacity
    dest_index = jnp.where(kept_mask, target * capacity + position, slot_total * capacity)
    source = jnp.full((slot_total * capacity,), route_total, jnp.int32)
    source = source.at[dest_index].set(jnp.arange(route_total, dtype=jnp.int32), mode="drop")
    return (kept_mask, dest_index, source)


def expert_apply_forward(rows_in, gate_up, down, adapt_a, adapt_b):
    adapter_rank_count = adapt_b.shape[1]
    hidden_width = adapt_b.shape[2]
    reduced_rank_rows = jnp.dot(rows_in, adapt_a, preferred_element_type=jnp.float32).astype(
        jnp.bfloat16
    )
    base_preactivation = jnp.dot(rows_in, gate_up, preferred_element_type=jnp.float32)
    adapter_gate_delta = jnp.dot(
        reduced_rank_rows[:, :adapter_rank_count], adapt_b[0], preferred_element_type=jnp.float32
    )
    adapter_up_delta = jnp.dot(
        reduced_rank_rows[:, adapter_rank_count:], adapt_b[1], preferred_element_type=jnp.float32
    )
    gate_preactivation = base_preactivation[:, :hidden_width] + ADAPTER_SCALE * adapter_gate_delta
    up_preactivation = base_preactivation[:, hidden_width:] + ADAPTER_SCALE * adapter_up_delta
    sigmoid_gate = jax.nn.sigmoid(gate_preactivation)
    active = gate_preactivation * sigmoid_gate
    hidden = (active * up_preactivation).astype(jnp.bfloat16)
    layer_output = jnp.dot(hidden, down, preferred_element_type=jnp.float32).astype(jnp.bfloat16)
    return (
        layer_output,
        (reduced_rank_rows, gate_preactivation, up_preactivation, sigmoid_gate, active),
    )


def expert_backward(rows_in, scaled, down, adapt_b, saved_residuals):
    reduced_rank_rows, gate_preactivation, up_preactivation, sigmoid_gate, active = saved_residuals
    adapter_rank_count = adapt_b.shape[1]
    back_hidden = lax.dot_general(
        scaled, down, (((1,), (1,)), ((), ())), preferred_element_type=jnp.float32
    )
    up_preactivation_gradient = (back_hidden * active).astype(jnp.bfloat16)
    slope = sigmoid_gate * (1.0 + gate_preactivation * (1.0 - sigmoid_gate))
    gate_preactivation_gradient = (back_hidden * up_preactivation * slope).astype(jnp.bfloat16)
    row_dimension_numbers = (((0,), (0,)), ((), ()))
    gate_up_map_gradient = ADAPTER_SCALE * lax.dot_general(
        reduced_rank_rows[:, :adapter_rank_count],
        gate_preactivation_gradient,
        row_dimension_numbers,
        preferred_element_type=jnp.float32,
    )
    up_map_gradient = ADAPTER_SCALE * lax.dot_general(
        reduced_rank_rows[:, adapter_rank_count:],
        up_preactivation_gradient,
        row_dimension_numbers,
        preferred_element_type=jnp.float32,
    )
    cols_dims = (((1,), (1,)), ((), ()))
    gate_reduced_rows = lax.dot_general(
        gate_preactivation_gradient, adapt_b[0], cols_dims, preferred_element_type=jnp.float32
    )
    up_reduced_rows = lax.dot_general(
        up_preactivation_gradient, adapt_b[1], cols_dims, preferred_element_type=jnp.float32
    )
    reduced_gradient = (
        ADAPTER_SCALE * jnp.concatenate([gate_reduced_rows, up_reduced_rows], axis=1)
    ).astype(jnp.bfloat16)
    grad_adapt_a = lax.dot_general(
        rows_in, reduced_gradient, row_dimension_numbers, preferred_element_type=jnp.float32
    )
    return (grad_adapt_a, jnp.stack([gate_up_map_gradient, up_map_gradient]))


def sparse_body(
    tokens,
    cotangent,
    routing,
    router_route_weights,
    route_replica_choice,
    device_expert_table,
    gate_up_weight,
    down_weight,
    adapter_down_maps,
    adapter_up_maps,
):
    slot_total = lax.axis_size("expert")
    tok_rows = tokens.shape[0]
    model_feature_width = tokens.shape[1]
    top_routes = routing.shape[1]
    route_total = tok_rows * top_routes
    capacity = route_total // slot_total
    kept_mask, dest_index, source = route_rows(
        routing, route_replica_choice, device_expert_table, capacity
    )
    valid_route_mask = source < route_total
    safe_route = jnp.minimum(source, route_total - 1)
    route_token_index = safe_route // top_routes
    weight_flat = router_route_weights.reshape(-1)
    route_weight_rows = weight_flat[safe_route]
    zero_row = jnp.zeros((), jnp.bfloat16)
    rows_out = jnp.where(valid_route_mask[:, None], tokens[route_token_index], zero_row).reshape(
        slot_total, capacity, model_feature_width
    )
    product = (
        route_weight_rows[:, None] * cotangent[route_token_index].astype(jnp.float32)
    ).astype(jnp.bfloat16)
    scaled_out = jnp.where(valid_route_mask[:, None], product, zero_row).reshape(
        slot_total, capacity, model_feature_width
    )
    rows_in = lax.all_to_all(rows_out, "expert", split_axis=0, concat_axis=0, tiled=True)
    flattened_rows = rows_in.reshape(-1, model_feature_width)
    layer_output, saved_residuals = expert_apply_forward(
        flattened_rows, gate_up_weight[0], down_weight[0], adapter_down_maps[0], adapter_up_maps[0]
    )
    returned = lax.all_to_all(
        layer_output.reshape(slot_total, capacity, model_feature_width),
        "expert",
        split_axis=0,
        concat_axis=0,
        tiled=True,
    )
    returned = returned.reshape(-1, model_feature_width)
    picked_rows = returned[jnp.minimum(dest_index, slot_total * capacity - 1)]
    weighted = jnp.where(
        kept_mask[:, None],
        weight_flat[:, None] * picked_rows.astype(jnp.float32),
        jnp.zeros((), jnp.float32),
    )
    mixed = jnp.sum(weighted.reshape(tok_rows, top_routes, model_feature_width), axis=1).astype(
        jnp.bfloat16
    )
    scaled_input_rows = lax.all_to_all(
        scaled_out, "expert", split_axis=0, concat_axis=0, tiled=True
    )
    grad_adapt_a, grad_adapt_b = expert_backward(
        flattened_rows,
        scaled_input_rows.reshape(-1, model_feature_width),
        down_weight[0],
        adapter_up_maps[0],
        saved_residuals,
    )
    piece_a = grad_adapt_a.reshape(slot_total, -1)
    piece_b = grad_adapt_b.reshape(slot_total, -1)
    expert_total = max(top_routes, slot_total // 2)
    members = (
        jnp.arange(expert_total, dtype=jnp.int32)[:, None] == device_expert_table[None, :]
    ).astype(jnp.float32)
    piece_a, piece_b = lax.psum((piece_a, piece_b), "dp")
    got_a, got_b = (
        lax.all_to_all(piece_a, "expert", split_axis=0, concat_axis=0, tiled=True),
        lax.all_to_all(piece_b, "expert", split_axis=0, concat_axis=0, tiled=True),
    )
    expert_a = jnp.dot(members, got_a, precision=lax.Precision.HIGHEST)
    expert_b = jnp.dot(members, got_b, precision=lax.Precision.HIGHEST)
    back_dims = (((0,), (0,)), ((), ()))
    spread_a = lax.dot_general(members, expert_a, back_dims, precision=lax.Precision.HIGHEST)
    spread_b = lax.dot_general(members, expert_b, back_dims, precision=lax.Precision.HIGHEST)
    summed_a, summed_b = (
        lax.all_to_all(spread_a, "expert", split_axis=0, concat_axis=0, tiled=True),
        lax.all_to_all(spread_b, "expert", split_axis=0, concat_axis=0, tiled=True),
    )
    grad_a = summed_a.reshape(grad_adapt_a.shape)[None]
    grad_b = summed_b.reshape(grad_adapt_b.shape)[None]
    return (mixed, grad_a, grad_b)


def dot(a, b, a_dim=1, b_dim=0):
    return lax.dot_general(
        a, b, (((a_dim,), (b_dim,)), ((), ())), preferred_element_type=jnp.float32
    )


def first_half(shape):
    return lax.broadcasted_iota(jnp.int32, shape, 1) < shape[1] // 2


def halves(low):
    gate = first_half(low.shape)
    zero = jnp.zeros_like(low)
    return jnp.where(gate, low, zero), jnp.where(gate, zero, low)


def split_weights(table):
    parts = []
    for _ in range(3):
        part = table.astype(jnp.bfloat16).astype(jnp.float32)
        parts.append(part)
        table = table - part
    slot_total, tok_rows = table.shape
    parts.append(jnp.zeros((tok_rows - 3 * slot_total, tok_rows), jnp.float32))
    return jnp.transpose(jnp.concatenate(parts)).astype(jnp.bfloat16)


def joined_weight(extra, slot, slot_total):
    lane = lax.broadcasted_iota(jnp.int32, extra.shape, 1)
    mine = lane == slot
    for part in range(1, 3):
        mine = mine | (lane == slot + part * slot_total)
    chosen = jnp.where(mine, extra.astype(jnp.float32), 0.0)
    return jnp.sum(chosen, axis=1, keepdims=True)


def tagged_kernel(capacity, table_ref, expert_ref, choice_ref, weight_ref, tokens_ref, *out_refs):
    slot_total = table_ref.shape[0]
    tok_rows, features = tokens_ref.shape
    rows = tok_rows // len(out_refs)
    experts, weights = expert_ref[...], weight_ref[...]
    holds = [experts == table_ref[s] for s in range(slot_total)]
    counts = [hold.astype(jnp.float32) for hold in holds]
    copies = sum(counts)
    choice = choice_ref[...].astype(jnp.float32)
    wanted = choice - copies * jnp.floor((choice + 0.5) / copies)
    before = jnp.zeros_like(copies)
    taken, route_weight = [], []
    for hold, count in zip(holds, counts):
        picked = jnp.where(hold & (before == wanted), 1.0, 0.0)
        before = before + count
        taken.append(jnp.sum(picked, axis=0, keepdims=True))
        route_weight.append(jnp.sum(picked * weights, axis=0, keepdims=True))
    shape = (tok_rows, tok_rows)
    earlier = lax.broadcasted_iota(jnp.int32, shape, 0) < lax.broadcasted_iota(jnp.int32, shape, 1)
    rank = dot(
        jnp.concatenate(taken).astype(jnp.bfloat16),
        jnp.where(earlier, 1.0, 0.0).astype(jnp.bfloat16),
    )
    table = jnp.where(rank < capacity, jnp.concatenate(route_weight), 0.0)
    extra = split_weights(table)
    for at, out_ref in enumerate(out_refs):
        here = slice(at * rows, (at + 1) * rows)
        out_ref[:, :features] = tokens_ref[here]
        out_ref[:, features:] = extra[here]


VMEM = pl.BlockSpec(memory_space=pltpu.VMEM)
SMEM = pl.BlockSpec(memory_space=pltpu.SMEM)
EXTRA = 128
PARTS = 2


def tagged_tokens(tokens, routing, weights, choice, table, capacity):
    tok_rows, features = tokens.shape
    part = jax.ShapeDtypeStruct((tok_rows // PARTS, features + EXTRA), tokens.dtype)
    return pl.pallas_call(
        functools.partial(tagged_kernel, capacity),
        out_shape=(part,) * PARTS,
        in_specs=[SMEM, VMEM, VMEM, VMEM, VMEM],
        out_specs=(VMEM,) * PARTS,
    )(table, routing.T, choice.T, weights.T, tokens)


def stage_call(kernel, outs, scratch, macs, operands):
    out_shape = tuple(jax.ShapeDtypeStruct(*out) for out in outs)
    moved = sum(array.size * array.dtype.itemsize for array in (*operands, *out_shape))
    return pl.pallas_call(
        kernel,
        out_shape=out_shape,
        in_specs=[SMEM] + [VMEM] * (len(operands) - 1),
        out_specs=(VMEM,) * len(outs),
        scratch_shapes=[pltpu.VMEM(*shape) for shape in scratch],
        compiler_params=pltpu.CompilerParams(vmem_limit_bytes=24 * 2**20),
        cost_estimate=pl.CostEstimate(flops=2 * macs, bytes_accessed=moved, transcendentals=0),
    )(*operands)


def forward_kernel(
    chunk, slot_ref, rows_ref, adapt_a_ref, gate_up_ref, adapt_b_ref, down_ref,
    low_ref, active_ref, slope_ref, part_ref, total_ref,
):
    hidden_width, features = down_ref.shape
    rows = rows_ref[:, :features]
    low = dot(rows, adapt_a_ref[...]).astype(jnp.bfloat16)
    low_ref[...] = low
    low_gate, low_up = halves(low)
    for start in range(0, hidden_width, chunk):
        here = slice(start, start + chunk)
        there = slice(hidden_width + start, hidden_width + start + chunk)
        adapt_b = adapt_b_ref[:, here]
        gate = dot(rows, gate_up_ref[:, here]) + ADAPTER_SCALE * dot(low_gate, adapt_b)
        up = dot(rows, gate_up_ref[:, there]) + ADAPTER_SCALE * dot(low_up, adapt_b)
        sigmoid_gate = jax.nn.sigmoid(gate)
        active = gate * sigmoid_gate
        active_ref[:, here] = active
        slope_ref[:, here] = up * (sigmoid_gate * (1.0 + gate * (1.0 - sigmoid_gate)))
        more = dot((active * up).astype(jnp.bfloat16), down_ref[here])
        if start == 0:
            total_ref[...] = more
        else:
            total_ref[...] += more
    out = total_ref[...].astype(jnp.bfloat16).astype(jnp.float32)
    w = joined_weight(rows_ref[:, features:], slot_ref[0], slot_ref[1])
    part_ref[...] = (w * out).astype(jnp.bfloat16)


def forward_part(slot, rows, gate_up, down, adapt_a, adapt_b, chunk=256):
    hidden_width, features = down.shape
    count, ranks = rows.shape[0], adapt_a.shape[1]
    bf16, f32 = jnp.bfloat16, jnp.float32
    saved = ((count, hidden_width), f32)
    return stage_call(
        functools.partial(forward_kernel, chunk),
        (((count, ranks), bf16), saved, saved, ((count, features), bf16)),
        [((count, features), f32)],
        count * (gate_up.size + down.size + adapt_a.size),
        (slot, rows, adapt_a, gate_up, adapt_b, down),
    )


def backward_kernel(chunk, adds, cut, part, *refs):
    slot_ref, refs = refs[0], refs[1:]
    n_blocks = slot_ref.shape[0] - 2
    cots, refs = refs[:n_blocks], refs[n_blocks:]
    rows_ref, low_ref, active_ref, slope_ref, adapt_b_ref, down_ref, *refs = refs
    grads, (out_a_ref, out_b_ref, scaled_ref) = refs[: 2 * adds], refs[2 * adds :]
    features = cots[0].shape[1]
    length = rows_ref.shape[0] // n_blocks
    for at, cot_ref in enumerate(cots):
        here = pl.ds(pl.multiple_of(slot_ref[2 + at] * length, length), length)
        w = joined_weight(rows_ref[here, features:], slot_ref[0], slot_ref[1])
        cot = cot_ref[part * length : (part + 1) * length].astype(jnp.float32)
        scaled_ref[here] = (w * cot).astype(jnp.bfloat16)
    scaled = scaled_ref[...]
    low_gate, low_up = halves(low_ref[...])
    low_back = 0.0
    for start in range(0, down_ref.shape[0], chunk):
        here = slice(start, start + chunk)
        adapt_b = adapt_b_ref[:, here]
        back = dot(scaled, down_ref[here], 1, 1)
        up_grad = (back * active_ref[:, here]).astype(jnp.bfloat16)
        gate_grad = (back * slope_ref[:, here]).astype(jnp.bfloat16)
        sum_b = ADAPTER_SCALE * (dot(low_gate, gate_grad, 0, 0) + dot(low_up, up_grad, 0, 0))
        sum_b = sum_b + grads[1][:, here] if adds else sum_b
        if cut is None:
            out_b_ref[:, here] = sum_b
        else:
            ranks = sum_b.shape[0]
            for col in range(0, chunk, ranks):
                at = features - cut + start + col
                out_b_ref[at : at + ranks] = sum_b[:, col : col + ranks].astype(jnp.bfloat16)
        gate_back, up_back = dot(gate_grad, adapt_b, 1, 1), dot(up_grad, adapt_b, 1, 1)
        low_back = low_back + jnp.where(first_half(gate_back.shape), gate_back, up_back)
    low_grad = (ADAPTER_SCALE * low_back).astype(jnp.bfloat16)
    sum_a = dot(rows_ref[:, :features], low_grad, 0, 0)
    sum_a = sum_a + grads[0][...] if adds else sum_a
    if cut is None:
        out_a_ref[...] = sum_a
    else:
        out_a_ref[...] = sum_a[:cut].astype(jnp.bfloat16)
        out_b_ref[: features - cut] = sum_a[cut:].astype(jnp.bfloat16)


def backward_part(slot, part, cots, rows, saved, down, adapt_b, grads=(), cut=None, chunk=256):
    hidden_width, features = down.shape
    count, ranks = saved[0].shape
    bf16, f32 = jnp.bfloat16, jnp.float32
    outs = (((features, ranks), f32), ((ranks, hidden_width), f32))
    if cut is not None:
        outs = (((cut, ranks), bf16), ((features - cut + hidden_width, ranks), bf16))
    return stage_call(
        functools.partial(backward_kernel, chunk, len(grads) // 2, cut, part),
        outs,
        [((count, features), bf16)],
        count * (down.size + features * ranks + 4 * adapt_b.size),
        (slot, *cots, rows, *saved, adapt_b, down, *grads),
    )


def pair_kernel(*refs):
    for one_ref, other_ref, out_ref in zip(refs[:2], refs[2:4], refs[4:]):
        total = one_ref[...].astype(jnp.float32) + other_ref[...].astype(jnp.float32)
        out_ref[...] = total.astype(out_ref.dtype)


def pair_sums(ones, others):
    return pl.pallas_call(
        pair_kernel,
        out_shape=tuple(jax.ShapeDtypeStruct(one.shape, one.dtype) for one in ones),
        in_specs=[VMEM] * 4,
        out_specs=(VMEM,) * 2,
    )(*ones, *others)


def finish_kernel(one_x, one_y, other_x, other_y, grad_a_ref, grad_b_ref):
    cut, ranks = one_x.shape
    rest = grad_a_ref.shape[0] - cut
    grad_a_ref[:cut] = one_x[...].astype(jnp.float32) + other_x[...].astype(jnp.float32)
    total = one_y[...].astype(jnp.float32) + other_y[...].astype(jnp.float32)
    grad_a_ref[cut:] = total[:rest]
    for col in range(0, grad_b_ref.shape[1], ranks):
        grad_b_ref[:, col : col + ranks] = total[rest + col : rest + col + ranks]


def finished(ones, others, features, hidden_width):
    ranks = ones[0].shape[1]
    shapes = ((features, ranks), (ranks, hidden_width))
    return pl.pallas_call(
        finish_kernel,
        grid=(1,),
        out_shape=tuple(jax.ShapeDtypeStruct(shape, jnp.float32) for shape in shapes),
        in_specs=[pl.BlockSpec(one.shape, lambda j: (0, 0)) for one in (*ones, *others)],
        out_specs=tuple(pl.BlockSpec(shape, lambda j: (0, 0)) for shape in shapes),
    )(*ones, *others)


def z_pairs(*moves):
    return [(2 * a + core, 2 * b + core) for a, b in moves for core in (0, 1)]


ALL_SWAP = z_pairs((0, 1), (1, 0), (2, 3), (3, 2))
MID_SWAP = z_pairs((1, 2), (2, 1))
SIBLING = [(e, e ^ 1) for e in range(8)]


def send(array, pairs):
    return lax.ppermute(array, "expert", pairs)


def fence(*arrays):
    return lax.optimization_barrier(arrays)


def add_rounded(*terms):
    total = terms[0].astype(jnp.float32)
    for term in terms[1:]:
        total = total + term.astype(jnp.float32)
    return total.astype(jnp.bfloat16)


def sibling(block):
    return send(block, SIBLING)


def dp_swap(array, bit):
    return lax.ppermute(array, "dp", [(d, d ^ bit) for d in range(4)])


def group_sum(mine, features, hidden_width):
    got = dp_swap(mine[0], 1), dp_swap(mine[1], 2)
    pairs = pair_sums(mine, got)
    got = dp_swap(pairs[0], 2), dp_swap(pairs[1], 1)
    return finished(pairs, got, features, hidden_width)


def dense_body(
    tokens,
    cotangent,
    routing,
    router_route_weights,
    route_replica_choice,
    device_expert_table,
    gate_up_weight,
    down_weight,
    adapter_down_maps,
    adapter_up_maps,
):
    slot_total = lax.axis_size("expert")
    capacity = tokens.shape[0] * routing.shape[1] // slot_total
    me = lax.axis_index("expert")
    chip = me // 2
    inner = (chip == 1) | (chip == 2)
    gate_up, down = gate_up_weight[0], down_weight[0]
    adapt_a = adapter_down_maps[0]
    adapt_b = adapter_up_maps[0].reshape(adapt_a.shape[1], -1)

    def pick(inside, outside):
        return jnp.where(inner, inside, outside)

    whose = [me, me ^ 2, pick(me ^ 6, me ^ 4), pick(me ^ 4, me ^ 6)]
    whose = [device ^ core for device in whose for core in (0, 1)]
    slot = jnp.stack([me, jnp.int32(slot_total), *whose])

    def forward(rows):
        return forward_part(slot[:2], rows, gate_up, down, adapt_a, adapt_b)

    def backward(part, *operands, **options):
        return backward_part(slot, part, cots, *operands, down, adapt_b, **options)

    parts = tagged_tokens(
        tokens, routing, router_route_weights, route_replica_choice, device_expert_table, capacity
    )
    rows = [lax.all_gather(part, "expert", tiled=True) for part in parts]

    cot_swap = send(cotangent, ALL_SWAP)
    cot_mid = send(cotangent, MID_SWAP)
    twin = sibling(cotangent)
    cot_swap, cot_mid, twin = fence(cot_swap, cot_mid, twin)
    cots = [cotangent, twin]

    cot_out2 = send(cot_mid, ALL_SWAP)
    cot_mid2 = send(cot_swap, MID_SWAP)
    cots += [cot_swap, sibling(cot_swap)]
    rows[0], twin = fence(rows[0], twin)
    *saved0, out0 = forward(rows[0])
    mixed0 = lax.psum_scatter(out0, "expert", scatter_dimension=0, tiled=True)

    cot_mid, cot_out2, cot_mid2, out0 = fence(cot_mid, cot_out2, cot_mid2, out0)
    cot_out3 = send(cot_mid2, ALL_SWAP)
    cot_second = pick(cot_mid, cot_out2)
    cots += [cot_second, sibling(cot_second)]
    rows[1], cot_second = fence(rows[1], cot_second)
    *saved1, out1 = forward(rows[1])
    cot_mid2, cot_out3, out1 = fence(cot_mid2, cot_out3, out1)
    mixed1 = lax.psum_scatter(out1, "expert", scatter_dimension=0, tiled=True)

    cot_third = pick(cot_mid2, cot_out3)
    cots += [cot_third, sibling(cot_third)]
    features, hidden_width = adapt_a.shape[0], adapt_b.shape[1]
    cut = (features + hidden_width) // 2
    grads = backward(0, rows[0], saved0)
    grads = backward(1, rows[1], saved1, grads=grads, cut=cut)
    grad_a, grad_b = group_sum(grads, features, hidden_width)
    mixed = jnp.concatenate([mixed0, mixed1])
    return mixed, grad_a[None], grad_b.reshape(adapter_up_maps.shape)


def body(*arrays):
    if (lax.axis_size("dp"), lax.axis_size("expert"), arrays[2].shape[1]) == (4, 8, 8):
        return dense_body(*arrays)
    return sparse_body(*arrays)


def solution(mesh):
    return jax.shard_map(
        body,
        mesh=mesh,
        in_specs=(
            P(("dp", "expert"), None),
            P(("dp", "expert"), None),
            P(("dp", "expert"), None),
            P(("dp", "expert"), None),
            P(("dp", "expert"), None),
            P(),
            P("expert", None, None),
            P("expert", None, None),
            P("expert", None, None),
            P("expert", None, None, None),
        ),
        out_specs=(
            P(("dp", "expert"), None),
            P("expert", None, None),
            P("expert", None, None, None),
        ),
        check_vma=False,
    )
```

```python
import functools

import jax
import jax.numpy as jnp
from jax import lax
from jax.experimental import pallas as pl
from jax.experimental.pallas import tpu as pltpu
from jax.sharding import PartitionSpec as P

ADAPTER_SCALE = 0.5


def route_rows(routing, route_replica_choice, device_expert_table, capacity):
    slot_total = device_expert_table.shape[0]
    route_total = routing.shape[0] * routing.shape[1]
    expert_flat = routing.reshape(-1)
    holds_mask = (expert_flat[:, None] == device_expert_table[None, :]).astype(jnp.int32)
    copies = jnp.sum(holds_mask, axis=1)
    wanted = route_replica_choice.reshape(-1) % copies
    before = jnp.cumsum(holds_mask, axis=1) - holds_mask
    picked = holds_mask * (before == wanted[:, None]).astype(jnp.int32)
    ahead_of = jnp.cumsum(picked, axis=0) - picked
    position = jnp.sum(picked * ahead_of, axis=1)
    target = jnp.sum(picked * jnp.arange(slot_total, dtype=jnp.int32)[None, :], axis=1)
    kept_mask = position < capacity
    dest_index = jnp.where(kept_mask, target * capacity + position, slot_total * capacity)
    source = jnp.full((slot_total * capacity,), route_total, jnp.int32)
    source = source.at[dest_index].set(jnp.arange(route_total, dtype=jnp.int32), mode="drop")
    return (kept_mask, dest_index, source)


def expert_apply_forward(rows_in, gate_up, down, adapt_a, adapt_b):
    adapter_rank_count = adapt_b.shape[1]
    hidden_width = adapt_b.shape[2]
    reduced_rank_rows = jnp.dot(rows_in, adapt_a, preferred_element_type=jnp.float32).astype(
        jnp.bfloat16
    )
    base_preactivation = jnp.dot(rows_in, gate_up, preferred_element_type=jnp.float32)
    adapter_gate_delta = jnp.dot(
        reduced_rank_rows[:, :adapter_rank_count], adapt_b[0], preferred_element_type=jnp.float32
    )
    adapter_up_delta = jnp.dot(
        reduced_rank_rows[:, adapter_rank_count:], adapt_b[1], preferred_element_type=jnp.float32
    )
    gate_preactivation = base_preactivation[:, :hidden_width] + ADAPTER_SCALE * adapter_gate_delta
    up_preactivation = base_preactivation[:, hidden_width:] + ADAPTER_SCALE * adapter_up_delta
    sigmoid_gate = jax.nn.sigmoid(gate_preactivation)
    active = gate_preactivation * sigmoid_gate
    hidden = (active * up_preactivation).astype(jnp.bfloat16)
    layer_output = jnp.dot(hidden, down, preferred_element_type=jnp.float32).astype(jnp.bfloat16)
    return (
        layer_output,
        (reduced_rank_rows, gate_preactivation, up_preactivation, sigmoid_gate, active),
    )


def expert_backward(rows_in, scaled, down, adapt_b, saved_residuals):
    reduced_rank_rows, gate_preactivation, up_preactivation, sigmoid_gate, active = saved_residuals
    adapter_rank_count = adapt_b.shape[1]
    back_hidden = lax.dot_general(
        scaled, down, (((1,), (1,)), ((), ())), preferred_element_type=jnp.float32
    )
    up_preactivation_gradient = (back_hidden * active).astype(jnp.bfloat16)
    slope = sigmoid_gate * (1.0 + gate_preactivation * (1.0 - sigmoid_gate))
    gate_preactivation_gradient = (back_hidden * up_preactivation * slope).astype(jnp.bfloat16)
    row_dimension_numbers = (((0,), (0,)), ((), ()))
    gate_up_map_gradient = ADAPTER_SCALE * lax.dot_general(
        reduced_rank_rows[:, :adapter_rank_count],
        gate_preactivation_gradient,
        row_dimension_numbers,
        preferred_element_type=jnp.float32,
    )
    up_map_gradient = ADAPTER_SCALE * lax.dot_general(
        reduced_rank_rows[:, adapter_rank_count:],
        up_preactivation_gradient,
        row_dimension_numbers,
        preferred_element_type=jnp.float32,
    )
    cols_dims = (((1,), (1,)), ((), ()))
    gate_reduced_rows = lax.dot_general(
        gate_preactivation_gradient, adapt_b[0], cols_dims, preferred_element_type=jnp.float32
    )
    up_reduced_rows = lax.dot_general(
        up_preactivation_gradient, adapt_b[1], cols_dims, preferred_element_type=jnp.float32
    )
    reduced_gradient = (
        ADAPTER_SCALE * jnp.concatenate([gate_reduced_rows, up_reduced_rows], axis=1)
    ).astype(jnp.bfloat16)
    grad_adapt_a = lax.dot_general(
        rows_in, reduced_gradient, row_dimension_numbers, preferred_element_type=jnp.float32
    )
    return (grad_adapt_a, jnp.stack([gate_up_map_gradient, up_map_gradient]))


def sparse_body(
    tokens,
    cotangent,
    routing,
    router_route_weights,
    route_replica_choice,
    device_expert_table,
    gate_up_weight,
    down_weight,
    adapter_down_maps,
    adapter_up_maps,
):
    slot_total = lax.axis_size("expert")
    tok_rows = tokens.shape[0]
    model_feature_width = tokens.shape[1]
    top_routes = routing.shape[1]
    route_total = tok_rows * top_routes
    capacity = route_total // slot_total
    kept_mask, dest_index, source = route_rows(
        routing, route_replica_choice, device_expert_table, capacity
    )
    valid_route_mask = source < route_total
    safe_route = jnp.minimum(source, route_total - 1)
    route_token_index = safe_route // top_routes
    weight_flat = router_route_weights.reshape(-1)
    route_weight_rows = weight_flat[safe_route]
    zero_row = jnp.zeros((), jnp.bfloat16)
    rows_out = jnp.where(valid_route_mask[:, None], tokens[route_token_index], zero_row).reshape(
        slot_total, capacity, model_feature_width
    )
    product = (
        route_weight_rows[:, None] * cotangent[route_token_index].astype(jnp.float32)
    ).astype(jnp.bfloat16)
    scaled_out = jnp.where(valid_route_mask[:, None], product, zero_row).reshape(
        slot_total, capacity, model_feature_width
    )
    rows_in = lax.all_to_all(rows_out, "expert", split_axis=0, concat_axis=0, tiled=True)
    flattened_rows = rows_in.reshape(-1, model_feature_width)
    layer_output, saved_residuals = expert_apply_forward(
        flattened_rows, gate_up_weight[0], down_weight[0], adapter_down_maps[0], adapter_up_maps[0]
    )
    returned = lax.all_to_all(
        layer_output.reshape(slot_total, capacity, model_feature_width),
        "expert",
        split_axis=0,
        concat_axis=0,
        tiled=True,
    )
    returned = returned.reshape(-1, model_feature_width)
    picked_rows = returned[jnp.minimum(dest_index, slot_total * capacity - 1)]
    weighted = jnp.where(
        kept_mask[:, None],
        weight_flat[:, None] * picked_rows.astype(jnp.float32),
        jnp.zeros((), jnp.float32),
    )
    mixed = jnp.sum(weighted.reshape(tok_rows, top_routes, model_feature_width), axis=1).astype(
        jnp.bfloat16
    )
    scaled_input_rows = lax.all_to_all(
        scaled_out, "expert", split_axis=0, concat_axis=0, tiled=True
    )
    grad_adapt_a, grad_adapt_b = expert_backward(
        flattened_rows,
        scaled_input_rows.reshape(-1, model_feature_width),
        down_weight[0],
        adapter_up_maps[0],
        saved_residuals,
    )
    piece_a = grad_adapt_a.reshape(slot_total, -1)
    piece_b = grad_adapt_b.reshape(slot_total, -1)
    expert_total = max(top_routes, slot_total // 2)
    members = (
        jnp.arange(expert_total, dtype=jnp.int32)[:, None] == device_expert_table[None, :]
    ).astype(jnp.float32)
    piece_a, piece_b = lax.psum((piece_a, piece_b), "dp")
    got_a, got_b = (
        lax.all_to_all(piece_a, "expert", split_axis=0, concat_axis=0, tiled=True),
        lax.all_to_all(piece_b, "expert", split_axis=0, concat_axis=0, tiled=True),
    )
    expert_a = jnp.dot(members, got_a, precision=lax.Precision.HIGHEST)
    expert_b = jnp.dot(members, got_b, precision=lax.Precision.HIGHEST)
    back_dims = (((0,), (0,)), ((), ()))
    spread_a = lax.dot_general(members, expert_a, back_dims, precision=lax.Precision.HIGHEST)
    spread_b = lax.dot_general(members, expert_b, back_dims, precision=lax.Precision.HIGHEST)
    summed_a, summed_b = (
        lax.all_to_all(spread_a, "expert", split_axis=0, concat_axis=0, tiled=True),
        lax.all_to_all(spread_b, "expert", split_axis=0, concat_axis=0, tiled=True),
    )
    grad_a = summed_a.reshape(grad_adapt_a.shape)[None]
    grad_b = summed_b.reshape(grad_adapt_b.shape)[None]
    return (mixed, grad_a, grad_b)


def dot(a, b, a_dim=1, b_dim=0):
    return lax.dot_general(
        a, b, (((a_dim,), (b_dim,)), ((), ())), preferred_element_type=jnp.float32
    )


def first_half(shape):
    return lax.broadcasted_iota(jnp.int32, shape, 1) < shape[1] // 2


def halves(low):
    gate = first_half(low.shape)
    zero = jnp.zeros_like(low)
    return jnp.where(gate, low, zero), jnp.where(gate, zero, low)


def split_weights(table):
    parts = []
    for _ in range(3):
        part = table.astype(jnp.bfloat16).astype(jnp.float32)
        parts.append(part)
        table = table - part
    slot_total, tok_rows = table.shape
    parts.append(jnp.zeros((tok_rows - 3 * slot_total, tok_rows), jnp.float32))
    return jnp.transpose(jnp.concatenate(parts)).astype(jnp.bfloat16)


def joined_weight(extra, slot, slot_total):
    lane = lax.broadcasted_iota(jnp.int32, extra.shape, 1)
    mine = lane == slot
    for part in range(1, 3):
        mine = mine | (lane == slot + part * slot_total)
    chosen = jnp.where(mine, extra.astype(jnp.float32), 0.0)
    return jnp.sum(chosen, axis=1, keepdims=True)


def tagged_kernel(capacity, table_ref, expert_ref, choice_ref, weight_ref, tokens_ref, out_ref):
    slot_total = table_ref.shape[0]
    tok_rows, features = tokens_ref.shape
    out_ref[:, :features] = tokens_ref[...]
    experts, weights = expert_ref[...], weight_ref[...]
    holds = [experts == table_ref[s] for s in range(slot_total)]
    counts = [hold.astype(jnp.float32) for hold in holds]
    copies = sum(counts)
    choice = choice_ref[...].astype(jnp.float32)
    wanted = choice - copies * jnp.floor((choice + 0.5) / copies)
    before = jnp.zeros_like(copies)
    taken, route_weight = [], []
    for hold, count in zip(holds, counts):
        picked = jnp.where(hold & (before == wanted), 1.0, 0.0)
        before = before + count
        taken.append(jnp.sum(picked, axis=0, keepdims=True))
        route_weight.append(jnp.sum(picked * weights, axis=0, keepdims=True))
    shape = (tok_rows, tok_rows)
    earlier = lax.broadcasted_iota(jnp.int32, shape, 0) < lax.broadcasted_iota(jnp.int32, shape, 1)
    rank = dot(
        jnp.concatenate(taken).astype(jnp.bfloat16),
        jnp.where(earlier, 1.0, 0.0).astype(jnp.bfloat16),
    )
    table = jnp.where(rank < capacity, jnp.concatenate(route_weight), 0.0)
    out_ref[:, features:] = split_weights(table)


VMEM = pl.BlockSpec(memory_space=pltpu.VMEM)
SMEM = pl.BlockSpec(memory_space=pltpu.SMEM)
EXTRA = 128


def tagged_tokens(tokens, routing, weights, choice, table, capacity):
    tok_rows, features = tokens.shape
    return pl.pallas_call(
        functools.partial(tagged_kernel, capacity),
        out_shape=jax.ShapeDtypeStruct((tok_rows, features + EXTRA), tokens.dtype),
        in_specs=[SMEM, VMEM, VMEM, VMEM, VMEM],
        out_specs=VMEM,
    )(table, routing.T, choice.T, weights.T, tokens)


def stage_call(kernel, outs, scratch, macs, operands):
    out_shape = tuple(jax.ShapeDtypeStruct(*out) for out in outs)
    moved = sum(array.size * array.dtype.itemsize for array in (*operands, *out_shape))
    return pl.pallas_call(
        kernel,
        out_shape=out_shape,
        in_specs=[SMEM] + [VMEM] * (len(operands) - 1),
        out_specs=(VMEM,) * len(outs),
        scratch_shapes=[pltpu.VMEM(*shape) for shape in scratch],
        compiler_params=pltpu.CompilerParams(vmem_limit_bytes=16 * 2**20),
        cost_estimate=pl.CostEstimate(flops=2 * macs, bytes_accessed=moved, transcendentals=0),
    )(*operands)


def forward_kernel(
    chunk, slot_ref, mine_ref, other_ref, adapt_a_ref, gate_up_ref, adapt_b_ref, down_ref,
    low_ref, active_ref, slope_ref, part_mine_ref, part_other_ref, rows_ref, total_ref,
):
    half, features = part_mine_ref.shape
    hidden_width = down_ref.shape[0]
    rows_ref[:half] = mine_ref[:, :features]
    rows_ref[half:] = other_ref[:, :features]
    rows = rows_ref[...]
    low = dot(rows, adapt_a_ref[...]).astype(jnp.bfloat16)
    low_ref[...] = low
    low_gate, low_up = halves(low)
    for start in range(0, hidden_width, chunk):
        here = slice(start, start + chunk)
        there = slice(hidden_width + start, hidden_width + start + chunk)
        adapt_b = adapt_b_ref[:, here]
        gate = dot(rows, gate_up_ref[:, here]) + ADAPTER_SCALE * dot(low_gate, adapt_b)
        up = dot(rows, gate_up_ref[:, there]) + ADAPTER_SCALE * dot(low_up, adapt_b)
        sigmoid_gate = jax.nn.sigmoid(gate)
        active = gate * sigmoid_gate
        active_ref[:, here] = active
        slope_ref[:, here] = up * (sigmoid_gate * (1.0 + gate * (1.0 - sigmoid_gate)))
        more = dot((active * up).astype(jnp.bfloat16), down_ref[here])
        if start == 0:
            total_ref[...] = more
        else:
            total_ref[...] += more
    out = total_ref[...].astype(jnp.bfloat16).astype(jnp.float32)
    for block_ref, part_ref, out in (
        (mine_ref, part_mine_ref, out[:half]),
        (other_ref, part_other_ref, out[half:]),
    ):
        w = joined_weight(block_ref[:, features:], slot_ref[0], slot_ref[1])
        part_ref[...] = (w * out).astype(jnp.bfloat16)


def forward_stage(slot, mine, other, gate_up, down, adapt_a, adapt_b, chunk=256):
    hidden_width, features = down.shape
    half, both, ranks = mine.shape[0], 2 * mine.shape[0], adapt_a.shape[1]
    bf16, f32 = jnp.bfloat16, jnp.float32
    saved = ((both, hidden_width), f32)
    part = ((half, features), bf16)
    return stage_call(
        functools.partial(forward_kernel, chunk),
        (((both, ranks), bf16), saved, saved, part, part),
        [((both, features), bf16), ((both, features), f32)],
        both * (gate_up.size + down.size + adapt_a.size),
        (slot, mine, other, adapt_a, gate_up, adapt_b, down),
    )


def backward_kernel(chunk, adds, cut, *refs):
    slot_ref, cot_all_ref, mine_ref, other_ref, *refs = refs
    low_ref, active_ref, slope_ref, adapt_b_ref, down_ref, *refs = refs
    grads, (out_a_ref, out_b_ref, scaled_ref, rows_ref) = refs[: 2 * adds], refs[2 * adds :]
    half, features = mine_ref.shape[0], cot_all_ref.shape[1]
    for at, block_ref in enumerate((mine_ref, other_ref)):
        here = slice(at * half, (at + 1) * half)
        w = joined_weight(block_ref[:, features:], slot_ref[0], slot_ref[1])
        whose = pl.multiple_of(slot_ref[2 + at] * half, half)
        cot = cot_all_ref[pl.ds(whose, half)].astype(jnp.float32)
        scaled_ref[here] = (w * cot).astype(jnp.bfloat16)
        rows_ref[here] = block_ref[:, :features]
    scaled = scaled_ref[...]
    low_gate, low_up = halves(low_ref[...])
    low_back = 0.0
    for start in range(0, down_ref.shape[0], chunk):
        here = slice(start, start + chunk)
        adapt_b = adapt_b_ref[:, here]
        back = dot(scaled, down_ref[here], 1, 1)
        up_grad = (back * active_ref[:, here]).astype(jnp.bfloat16)
        gate_grad = (back * slope_ref[:, here]).astype(jnp.bfloat16)
        sum_b = ADAPTER_SCALE * (dot(low_gate, gate_grad, 0, 0) + dot(low_up, up_grad, 0, 0))
        sum_b = sum_b + grads[1][:, here] if adds else sum_b
        if cut is None:
            out_b_ref[:, here] = sum_b
        else:
            ranks = sum_b.shape[0]
            for col in range(0, chunk, ranks):
                at = features - cut + start + col
                out_b_ref[at : at + ranks] = sum_b[:, col : col + ranks].astype(jnp.bfloat16)
        gate_back, up_back = dot(gate_grad, adapt_b, 1, 1), dot(up_grad, adapt_b, 1, 1)
        low_back = low_back + jnp.where(first_half(gate_back.shape), gate_back, up_back)
    low_grad = (ADAPTER_SCALE * low_back).astype(jnp.bfloat16)
    sum_a = dot(rows_ref[...], low_grad, 0, 0)
    sum_a = sum_a + grads[0][...] if adds else sum_a
    if cut is None:
        out_a_ref[...] = sum_a
    else:
        out_a_ref[...] = sum_a[:cut].astype(jnp.bfloat16)
        out_b_ref[: features - cut] = sum_a[cut:].astype(jnp.bfloat16)


def backward_stage(slot, cot_all, blocks, saved, down, adapt_b, grads=(), cut=None, chunk=256):
    hidden_width, features = down.shape
    both, ranks = saved[0].shape
    bf16, f32 = jnp.bfloat16, jnp.float32
    outs = (((features, ranks), f32), ((ranks, hidden_width), f32))
    if cut is not None:
        outs = (((cut, ranks), bf16), ((features - cut + hidden_width, ranks), bf16))
    return stage_call(
        functools.partial(backward_kernel, chunk, len(grads) // 2, cut),
        outs,
        [((both, features), bf16), ((both, features), bf16)],
        both * (down.size + features * ranks + 4 * adapt_b.size),
        (slot, cot_all, *blocks, *saved, adapt_b, down, *grads),
    )


def pair_kernel(*refs):
    for one_ref, other_ref, out_ref in zip(refs[:2], refs[2:4], refs[4:]):
        total = one_ref[...].astype(jnp.float32) + other_ref[...].astype(jnp.float32)
        out_ref[...] = total.astype(out_ref.dtype)


def pair_sums(ones, others):
    return pl.pallas_call(
        pair_kernel,
        out_shape=tuple(jax.ShapeDtypeStruct(one.shape, one.dtype) for one in ones),
        in_specs=[VMEM] * 4,
        out_specs=(VMEM,) * 2,
    )(*ones, *others)


def finish_kernel(one_x, one_y, other_x, other_y, grad_a_ref, grad_b_ref):
    cut, ranks = one_x.shape
    rest = grad_a_ref.shape[0] - cut
    grad_a_ref[:cut] = one_x[...].astype(jnp.float32) + other_x[...].astype(jnp.float32)
    total = one_y[...].astype(jnp.float32) + other_y[...].astype(jnp.float32)
    grad_a_ref[cut:] = total[:rest]
    for col in range(0, grad_b_ref.shape[1], ranks):
        grad_b_ref[:, col : col + ranks] = total[rest + col : rest + col + ranks]


def finished(ones, others, features, hidden_width):
    ranks = ones[0].shape[1]
    shapes = ((features, ranks), (ranks, hidden_width))
    return pl.pallas_call(
        finish_kernel,
        grid=(1,),
        out_shape=tuple(jax.ShapeDtypeStruct(shape, jnp.float32) for shape in shapes),
        in_specs=[pl.BlockSpec(one.shape, lambda j: (0, 0)) for one in (*ones, *others)],
        out_specs=tuple(pl.BlockSpec(shape, lambda j: (0, 0)) for shape in shapes),
    )(*ones, *others)


def z_pairs(*moves):
    return [(2 * a + core, 2 * b + core) for a, b in moves for core in (0, 1)]


ALL_SWAP = z_pairs((0, 1), (1, 0), (2, 3), (3, 2))
MID_SWAP = z_pairs((1, 2), (2, 1))
SIBLING = [(e, e ^ 1) for e in range(8)]


def send(array, pairs):
    return lax.ppermute(array, "expert", pairs)


def fence(*arrays):
    return lax.optimization_barrier(arrays)


def add_rounded(*terms):
    total = terms[0].astype(jnp.float32)
    for term in terms[1:]:
        total = total + term.astype(jnp.float32)
    return total.astype(jnp.bfloat16)


def sibling(block):
    return send(block, SIBLING)


def dp_swap(array, bit):
    return lax.ppermute(array, "dp", [(d, d ^ bit) for d in range(4)])


def dense_body(
    tokens,
    cotangent,
    routing,
    router_route_weights,
    route_replica_choice,
    device_expert_table,
    gate_up_weight,
    down_weight,
    adapter_down_maps,
    adapter_up_maps,
):
    slot_total = lax.axis_size("expert")
    capacity = tokens.shape[0] * routing.shape[1] // slot_total
    me = lax.axis_index("expert")
    chip = me // 2
    inner = (chip == 1) | (chip == 2)
    gate_up, down = gate_up_weight[0], down_weight[0]
    adapt_a = adapter_down_maps[0]
    adapt_b = adapter_up_maps[0].reshape(adapt_a.shape[1], -1)

    def pick(inside, outside):
        return jnp.where(inner, inside, outside)

    def after(array, earlier):
        return fence(array, earlier)[0]

    whose = [me, me ^ 2, pick(me ^ 6, me ^ 4), pick(me ^ 4, me ^ 6)]
    slots = [jnp.stack([me, jnp.int32(slot_total), device, device ^ 1]) for device in whose]

    def forward(*blocks):
        *saved, part, away = forward_stage(slots[0], *blocks, gate_up, down, adapt_a, adapt_b)
        return saved, part, away

    def backward(stage, rows, saved, grads=(), cut=None):
        return backward_stage(slots[stage], cots, rows, saved, down, adapt_b, grads, cut)

    cots = lax.all_gather(cotangent, "expert", tiled=True)
    tokens = tagged_tokens(
        tokens, routing, router_route_weights, route_replica_choice, device_expert_table, capacity
    )
    tok_swap = send(tokens, ALL_SWAP)
    twin = sibling(tokens)
    rows0 = (tokens, twin)
    tok_mid = send(after(tokens, twin), MID_SWAP)
    saved0, part0, away0 = forward(*rows0)
    tok_swap, tok_mid, part0, away0 = fence(tok_swap, tok_mid, part0, away0)

    tok_out2 = send(tok_mid, ALL_SWAP)
    twin = sibling(tok_swap)
    rows1 = (tok_swap, twin)
    tok_mid2 = send(after(tok_swap, twin), MID_SWAP)
    saved1, part1, away1 = forward(*rows1)
    tok_mid, tok_out2, tok_mid2, part1, away1 = fence(tok_mid, tok_out2, tok_mid2, part1, away1)

    tok_out3 = send(tok_mid2, ALL_SWAP)
    tok_second = pick(tok_mid, tok_out2)
    rows2 = (tok_second, sibling(tok_second))
    saved2, part2, away2 = forward(*rows2)
    tok_mid2, tok_out3, part2, away2, cots = fence(tok_mid2, tok_out3, part2, away2, cots)

    tok_third = pick(tok_mid2, tok_out3)
    rows3 = (tok_third, sibling(tok_third))
    saved3, part3, away3 = forward(*rows3)
    part3 = add_rounded(part3, sibling(away3))
    part3, part2, away2 = fence(part3, part2, away2)

    third_in = send(part3, ALL_SWAP)
    part2 = add_rounded(part2, sibling(away2))
    features, hidden_width = adapt_a.shape[0], adapt_b.shape[1]
    cut = (features + hidden_width) // 2
    grads = backward(0, rows0, saved0)
    grads = backward(1, rows1, saved1, grads)
    grads = backward(2, rows2, saved2, grads)
    grads = backward(3, rows3, saved3, grads, cut)
    third_in, part3, part2, part1, away1, grads = fence(third_in, part3, part2, part1, away1, grads)

    second_in = send(part2, ALL_SWAP)
    third_mid = send(add_rounded(part3, third_in), MID_SWAP)
    got = dp_swap(grads[0], 1), dp_swap(grads[1], 2)
    part1 = add_rounded(part1, sibling(away1))
    part0 = add_rounded(part0, sibling(away0))
    second_in, third_mid, part0, part1, part2, grads, got = fence(
        second_in, third_mid, part0, part1, part2, grads, got
    )
    first_swap = send(add_rounded(part1, third_mid), ALL_SWAP)
    second_mid = send(add_rounded(part2, second_in), MID_SWAP)
    pairs = pair_sums(grads, got)
    got = dp_swap(pairs[0], 2), dp_swap(pairs[1], 1)
    grad_a, grad_b = finished(pairs, got, features, hidden_width)
    mixed = add_rounded(part0, first_swap, second_mid)
    return mixed, grad_a[None], grad_b.reshape(adapter_up_maps.shape)


def body(*arrays):
    if (lax.axis_size("dp"), lax.axis_size("expert"), arrays[2].shape[1]) == (4, 8, 8):
        return dense_body(*arrays)
    return sparse_body(*arrays)


def solution(mesh):
    return jax.shard_map(
        body,
        mesh=mesh,
        in_specs=(
            P(("dp", "expert"), None),
            P(("dp", "expert"), None),
            P(("dp", "expert"), None),
            P(("dp", "expert"), None),
            P(("dp", "expert"), None),
            P(),
            P("expert", None, None),
            P("expert", None, None),
            P("expert", None, None),
            P("expert", None, None, None),
        ),
        out_specs=(
            P(("dp", "expert"), None),
            P("expert", None, None),
            P("expert", None, None, None),
        ),
        check_vma=False,
    )
```

```python
import functools

import jax
import jax.numpy as jnp
from jax import lax
from jax.experimental import pallas as pl
from jax.experimental.pallas import tpu as pltpu
from jax.sharding import PartitionSpec as P

ADAPTER_SCALE = 0.5


def route_rows(routing, route_replica_choice, device_expert_table, capacity):
    slot_total = device_expert_table.shape[0]
    route_total = routing.shape[0] * routing.shape[1]
    expert_flat = routing.reshape(-1)
    holds_mask = (expert_flat[:, None] == device_expert_table[None, :]).astype(jnp.int32)
    copies = jnp.sum(holds_mask, axis=1)
    wanted = route_replica_choice.reshape(-1) % copies
    before = jnp.cumsum(holds_mask, axis=1) - holds_mask
    picked = holds_mask * (before == wanted[:, None]).astype(jnp.int32)
    ahead_of = jnp.cumsum(picked, axis=0) - picked
    position = jnp.sum(picked * ahead_of, axis=1)
    target = jnp.sum(picked * jnp.arange(slot_total, dtype=jnp.int32)[None, :], axis=1)
    kept_mask = position < capacity
    dest_index = jnp.where(kept_mask, target * capacity + position, slot_total * capacity)
    source = jnp.full((slot_total * capacity,), route_total, jnp.int32)
    source = source.at[dest_index].set(jnp.arange(route_total, dtype=jnp.int32), mode="drop")
    return (kept_mask, dest_index, source)


def expert_apply_forward(rows_in, gate_up, down, adapt_a, adapt_b):
    adapter_rank_count = adapt_b.shape[1]
    hidden_width = adapt_b.shape[2]
    reduced_rank_rows = jnp.dot(rows_in, adapt_a, preferred_element_type=jnp.float32).astype(
        jnp.bfloat16
    )
    base_preactivation = jnp.dot(rows_in, gate_up, preferred_element_type=jnp.float32)
    adapter_gate_delta = jnp.dot(
        reduced_rank_rows[:, :adapter_rank_count], adapt_b[0], preferred_element_type=jnp.float32
    )
    adapter_up_delta = jnp.dot(
        reduced_rank_rows[:, adapter_rank_count:], adapt_b[1], preferred_element_type=jnp.float32
    )
    gate_preactivation = base_preactivation[:, :hidden_width] + ADAPTER_SCALE * adapter_gate_delta
    up_preactivation = base_preactivation[:, hidden_width:] + ADAPTER_SCALE * adapter_up_delta
    sigmoid_gate = jax.nn.sigmoid(gate_preactivation)
    active = gate_preactivation * sigmoid_gate
    hidden = (active * up_preactivation).astype(jnp.bfloat16)
    layer_output = jnp.dot(hidden, down, preferred_element_type=jnp.float32).astype(jnp.bfloat16)
    return (
        layer_output,
        (reduced_rank_rows, gate_preactivation, up_preactivation, sigmoid_gate, active),
    )


def expert_backward(rows_in, scaled, down, adapt_b, saved_residuals):
    reduced_rank_rows, gate_preactivation, up_preactivation, sigmoid_gate, active = saved_residuals
    adapter_rank_count = adapt_b.shape[1]
    back_hidden = lax.dot_general(
        scaled, down, (((1,), (1,)), ((), ())), preferred_element_type=jnp.float32
    )
    up_preactivation_gradient = (back_hidden * active).astype(jnp.bfloat16)
    slope = sigmoid_gate * (1.0 + gate_preactivation * (1.0 - sigmoid_gate))
    gate_preactivation_gradient = (back_hidden * up_preactivation * slope).astype(jnp.bfloat16)
    row_dimension_numbers = (((0,), (0,)), ((), ()))
    gate_up_map_gradient = ADAPTER_SCALE * lax.dot_general(
        reduced_rank_rows[:, :adapter_rank_count],
        gate_preactivation_gradient,
        row_dimension_numbers,
        preferred_element_type=jnp.float32,
    )
    up_map_gradient = ADAPTER_SCALE * lax.dot_general(
        reduced_rank_rows[:, adapter_rank_count:],
        up_preactivation_gradient,
        row_dimension_numbers,
        preferred_element_type=jnp.float32,
    )
    cols_dims = (((1,), (1,)), ((), ()))
    gate_reduced_rows = lax.dot_general(
        gate_preactivation_gradient, adapt_b[0], cols_dims, preferred_element_type=jnp.float32
    )
    up_reduced_rows = lax.dot_general(
        up_preactivation_gradient, adapt_b[1], cols_dims, preferred_element_type=jnp.float32
    )
    reduced_gradient = (
        ADAPTER_SCALE * jnp.concatenate([gate_reduced_rows, up_reduced_rows], axis=1)
    ).astype(jnp.bfloat16)
    grad_adapt_a = lax.dot_general(
        rows_in, reduced_gradient, row_dimension_numbers, preferred_element_type=jnp.float32
    )
    return (grad_adapt_a, jnp.stack([gate_up_map_gradient, up_map_gradient]))


def sparse_body(
    tokens,
    cotangent,
    routing,
    router_route_weights,
    route_replica_choice,
    device_expert_table,
    gate_up_weight,
    down_weight,
    adapter_down_maps,
    adapter_up_maps,
):
    slot_total = lax.axis_size("expert")
    tok_rows = tokens.shape[0]
    model_feature_width = tokens.shape[1]
    top_routes = routing.shape[1]
    route_total = tok_rows * top_routes
    capacity = route_total // slot_total
    kept_mask, dest_index, source = route_rows(
        routing, route_replica_choice, device_expert_table, capacity
    )
    valid_route_mask = source < route_total
    safe_route = jnp.minimum(source, route_total - 1)
    route_token_index = safe_route // top_routes
    weight_flat = router_route_weights.reshape(-1)
    route_weight_rows = weight_flat[safe_route]
    zero_row = jnp.zeros((), jnp.bfloat16)
    rows_out = jnp.where(valid_route_mask[:, None], tokens[route_token_index], zero_row).reshape(
        slot_total, capacity, model_feature_width
    )
    product = (
        route_weight_rows[:, None] * cotangent[route_token_index].astype(jnp.float32)
    ).astype(jnp.bfloat16)
    scaled_out = jnp.where(valid_route_mask[:, None], product, zero_row).reshape(
        slot_total, capacity, model_feature_width
    )
    rows_in = lax.all_to_all(rows_out, "expert", split_axis=0, concat_axis=0, tiled=True)
    flattened_rows = rows_in.reshape(-1, model_feature_width)
    layer_output, saved_residuals = expert_apply_forward(
        flattened_rows, gate_up_weight[0], down_weight[0], adapter_down_maps[0], adapter_up_maps[0]
    )
    returned = lax.all_to_all(
        layer_output.reshape(slot_total, capacity, model_feature_width),
        "expert",
        split_axis=0,
        concat_axis=0,
        tiled=True,
    )
    returned = returned.reshape(-1, model_feature_width)
    picked_rows = returned[jnp.minimum(dest_index, slot_total * capacity - 1)]
    weighted = jnp.where(
        kept_mask[:, None],
        weight_flat[:, None] * picked_rows.astype(jnp.float32),
        jnp.zeros((), jnp.float32),
    )
    mixed = jnp.sum(weighted.reshape(tok_rows, top_routes, model_feature_width), axis=1).astype(
        jnp.bfloat16
    )
    scaled_input_rows = lax.all_to_all(
        scaled_out, "expert", split_axis=0, concat_axis=0, tiled=True
    )
    grad_adapt_a, grad_adapt_b = expert_backward(
        flattened_rows,
        scaled_input_rows.reshape(-1, model_feature_width),
        down_weight[0],
        adapter_up_maps[0],
        saved_residuals,
    )
    piece_a = grad_adapt_a.reshape(slot_total, -1)
    piece_b = grad_adapt_b.reshape(slot_total, -1)
    expert_total = max(top_routes, slot_total // 2)
    members = (
        jnp.arange(expert_total, dtype=jnp.int32)[:, None] == device_expert_table[None, :]
    ).astype(jnp.float32)
    piece_a, piece_b = lax.psum((piece_a, piece_b), "dp")
    got_a, got_b = (
        lax.all_to_all(piece_a, "expert", split_axis=0, concat_axis=0, tiled=True),
        lax.all_to_all(piece_b, "expert", split_axis=0, concat_axis=0, tiled=True),
    )
    expert_a = jnp.dot(members, got_a, precision=lax.Precision.HIGHEST)
    expert_b = jnp.dot(members, got_b, precision=lax.Precision.HIGHEST)
    back_dims = (((0,), (0,)), ((), ()))
    spread_a = lax.dot_general(members, expert_a, back_dims, precision=lax.Precision.HIGHEST)
    spread_b = lax.dot_general(members, expert_b, back_dims, precision=lax.Precision.HIGHEST)
    summed_a, summed_b = (
        lax.all_to_all(spread_a, "expert", split_axis=0, concat_axis=0, tiled=True),
        lax.all_to_all(spread_b, "expert", split_axis=0, concat_axis=0, tiled=True),
    )
    grad_a = summed_a.reshape(grad_adapt_a.shape)[None]
    grad_b = summed_b.reshape(grad_adapt_b.shape)[None]
    return (mixed, grad_a, grad_b)


def dot(a, b, a_dim=1, b_dim=0):
    return lax.dot_general(
        a, b, (((a_dim,), (b_dim,)), ((), ())), preferred_element_type=jnp.float32
    )


def first_half(shape):
    return lax.broadcasted_iota(jnp.int32, shape, 1) < shape[1] // 2


def halves(low):
    gate = first_half(low.shape)
    zero = jnp.zeros_like(low)
    return jnp.where(gate, low, zero), jnp.where(gate, zero, low)


def split_weights(table):
    parts = []
    for _ in range(3):
        part = table.astype(jnp.bfloat16).astype(jnp.float32)
        parts.append(part)
        table = table - part
    slot_total, tok_rows = table.shape
    parts.append(jnp.zeros((tok_rows - 3 * slot_total, tok_rows), jnp.float32))
    return jnp.transpose(jnp.concatenate(parts)).astype(jnp.bfloat16)


def joined_weight(extra, slot, slot_total):
    lane = lax.broadcasted_iota(jnp.int32, extra.shape, 1)
    mine = lane == slot
    for part in range(1, 3):
        mine = mine | (lane == slot + part * slot_total)
    chosen = jnp.where(mine, extra.astype(jnp.float32), 0.0)
    return jnp.sum(chosen, axis=1, keepdims=True)


def tagged_kernel(capacity, table_ref, expert_ref, choice_ref, weight_ref, tokens_ref, out_ref):
    slot_total = table_ref.shape[0]
    tok_rows, features = tokens_ref.shape
    out_ref[:, :features] = tokens_ref[...]
    experts, weights = expert_ref[...], weight_ref[...]
    holds = [experts == table_ref[s] for s in range(slot_total)]
    counts = [hold.astype(jnp.float32) for hold in holds]
    copies = sum(counts)
    choice = choice_ref[...].astype(jnp.float32)
    wanted = choice - copies * jnp.floor((choice + 0.5) / copies)
    before = jnp.zeros_like(copies)
    taken, route_weight = [], []
    for hold, count in zip(holds, counts):
        picked = jnp.where(hold & (before == wanted), 1.0, 0.0)
        before = before + count
        taken.append(jnp.sum(picked, axis=0, keepdims=True))
        route_weight.append(jnp.sum(picked * weights, axis=0, keepdims=True))
    shape = (tok_rows, tok_rows)
    earlier = lax.broadcasted_iota(jnp.int32, shape, 0) < lax.broadcasted_iota(jnp.int32, shape, 1)
    rank = dot(
        jnp.concatenate(taken).astype(jnp.bfloat16),
        jnp.where(earlier, 1.0, 0.0).astype(jnp.bfloat16),
    )
    table = jnp.where(rank < capacity, jnp.concatenate(route_weight), 0.0)
    out_ref[:, features:] = split_weights(table)


VMEM = pl.BlockSpec(memory_space=pltpu.VMEM)
SMEM = pl.BlockSpec(memory_space=pltpu.SMEM)
EXTRA = 128


def tagged_tokens(tokens, routing, weights, choice, table, capacity):
    tok_rows, features = tokens.shape
    return pl.pallas_call(
        functools.partial(tagged_kernel, capacity),
        out_shape=jax.ShapeDtypeStruct((tok_rows, features + EXTRA), tokens.dtype),
        in_specs=[SMEM, VMEM, VMEM, VMEM, VMEM],
        out_specs=VMEM,
    )(table, routing.T, choice.T, weights.T, tokens)


def stage_call(kernel, outs, scratch, macs, operands):
    out_shape = tuple(jax.ShapeDtypeStruct(*out) for out in outs)
    moved = sum(array.size * array.dtype.itemsize for array in (*operands, *out_shape))
    return pl.pallas_call(
        kernel,
        out_shape=out_shape,
        in_specs=[SMEM] + [VMEM] * (len(operands) - 1),
        out_specs=(VMEM,) * len(outs),
        scratch_shapes=[pltpu.VMEM(*shape) for shape in scratch],
        compiler_params=pltpu.CompilerParams(vmem_limit_bytes=16 * 2**20),
        cost_estimate=pl.CostEstimate(flops=2 * macs, bytes_accessed=moved, transcendentals=0),
    )(*operands)


def forward_kernel(
    chunk, slot_ref, mine_ref, other_ref, adapt_a_ref, gate_up_ref, adapt_b_ref, down_ref,
    low_ref, active_ref, slope_ref, part_mine_ref, part_other_ref, rows_ref, total_ref,
):
    half, features = part_mine_ref.shape
    hidden_width = down_ref.shape[0]
    rows_ref[:half] = mine_ref[:, :features]
    rows_ref[half:] = other_ref[:, :features]
    rows = rows_ref[...]
    low = dot(rows, adapt_a_ref[...]).astype(jnp.bfloat16)
    low_ref[...] = low
    low_gate, low_up = halves(low)
    for start in range(0, hidden_width, chunk):
        here = slice(start, start + chunk)
        there = slice(hidden_width + start, hidden_width + start + chunk)
        adapt_b = adapt_b_ref[:, here]
        gate = dot(rows, gate_up_ref[:, here]) + ADAPTER_SCALE * dot(low_gate, adapt_b)
        up = dot(rows, gate_up_ref[:, there]) + ADAPTER_SCALE * dot(low_up, adapt_b)
        sigmoid_gate = jax.nn.sigmoid(gate)
        active = gate * sigmoid_gate
        active_ref[:, here] = active
        slope_ref[:, here] = up * (sigmoid_gate * (1.0 + gate * (1.0 - sigmoid_gate)))
        more = dot((active * up).astype(jnp.bfloat16), down_ref[here])
        if start == 0:
            total_ref[...] = more
        else:
            total_ref[...] += more
    out = total_ref[...].astype(jnp.bfloat16).astype(jnp.float32)
    for block_ref, part_ref, out in (
        (mine_ref, part_mine_ref, out[:half]),
        (other_ref, part_other_ref, out[half:]),
    ):
        w = joined_weight(block_ref[:, features:], slot_ref[0], slot_ref[1])
        part_ref[...] = (w * out).astype(jnp.bfloat16)


def forward_stage(slot, mine, other, gate_up, down, adapt_a, adapt_b, chunk=256):
    hidden_width, features = down.shape
    half, both, ranks = mine.shape[0], 2 * mine.shape[0], adapt_a.shape[1]
    bf16, f32 = jnp.bfloat16, jnp.float32
    saved = ((both, hidden_width), f32)
    part = ((half, features), bf16)
    return stage_call(
        functools.partial(forward_kernel, chunk),
        (((both, ranks), bf16), saved, saved, part, part),
        [((both, features), bf16), ((both, features), f32)],
        both * (gate_up.size + down.size + adapt_a.size),
        (slot, mine, other, adapt_a, gate_up, adapt_b, down),
    )


def backward_kernel(chunk, adds, cut, *refs):
    slot_ref, cot_mine, cot_other, mine_ref, other_ref, *refs = refs
    low_ref, active_ref, slope_ref, adapt_b_ref, down_ref, *refs = refs
    grads, (out_a_ref, out_b_ref, scaled_ref, rows_ref) = refs[: 2 * adds], refs[2 * adds :]
    half, features = cot_mine.shape
    for at, (cot_ref, block_ref) in enumerate(((cot_mine, mine_ref), (cot_other, other_ref))):
        here = slice(at * half, (at + 1) * half)
        w = joined_weight(block_ref[:, features:], slot_ref[0], slot_ref[1])
        scaled_ref[here] = (w * cot_ref[...].astype(jnp.float32)).astype(jnp.bfloat16)
        rows_ref[here] = block_ref[:, :features]
    scaled = scaled_ref[...]
    low_gate, low_up = halves(low_ref[...])
    low_back = 0.0
    for start in range(0, down_ref.shape[0], chunk):
        here = slice(start, start + chunk)
        adapt_b = adapt_b_ref[:, here]
        back = dot(scaled, down_ref[here], 1, 1)
        up_grad = (back * active_ref[:, here]).astype(jnp.bfloat16)
        gate_grad = (back * slope_ref[:, here]).astype(jnp.bfloat16)
        sum_b = ADAPTER_SCALE * (dot(low_gate, gate_grad, 0, 0) + dot(low_up, up_grad, 0, 0))
        sum_b = sum_b + grads[1][:, here] if adds else sum_b
        if cut is None:
            out_b_ref[:, here] = sum_b
        else:
            ranks = sum_b.shape[0]
            for col in range(0, chunk, ranks):
                at = features - cut + start + col
                out_b_ref[at : at + ranks] = sum_b[:, col : col + ranks].astype(jnp.bfloat16)
        gate_back, up_back = dot(gate_grad, adapt_b, 1, 1), dot(up_grad, adapt_b, 1, 1)
        low_back = low_back + jnp.where(first_half(gate_back.shape), gate_back, up_back)
    low_grad = (ADAPTER_SCALE * low_back).astype(jnp.bfloat16)
    sum_a = dot(rows_ref[...], low_grad, 0, 0)
    sum_a = sum_a + grads[0][...] if adds else sum_a
    if cut is None:
        out_a_ref[...] = sum_a
    else:
        out_a_ref[...] = sum_a[:cut].astype(jnp.bfloat16)
        out_b_ref[: features - cut] = sum_a[cut:].astype(jnp.bfloat16)


def backward_stage(slot, cots, blocks, saved, down, adapt_b, grads=(), cut=None, chunk=256):
    hidden_width, features = down.shape
    both, ranks = saved[0].shape
    bf16, f32 = jnp.bfloat16, jnp.float32
    outs = (((features, ranks), f32), ((ranks, hidden_width), f32))
    if cut is not None:
        outs = (((cut, ranks), bf16), ((features - cut + hidden_width, ranks), bf16))
    return stage_call(
        functools.partial(backward_kernel, chunk, len(grads) // 2, cut),
        outs,
        [((both, features), bf16), ((both, features), bf16)],
        both * (down.size + features * ranks + 4 * adapt_b.size),
        (slot, *cots, *blocks, *saved, adapt_b, down, *grads),
    )


def pair_kernel(*refs):
    for one_ref, other_ref, out_ref in zip(refs[:2], refs[2:4], refs[4:]):
        total = one_ref[...].astype(jnp.float32) + other_ref[...].astype(jnp.float32)
        out_ref[...] = total.astype(out_ref.dtype)


def pair_sums(ones, others):
    return pl.pallas_call(
        pair_kernel,
        out_shape=tuple(jax.ShapeDtypeStruct(one.shape, one.dtype) for one in ones),
        in_specs=[VMEM] * 4,
        out_specs=(VMEM,) * 2,
    )(*ones, *others)


def finish_kernel(one_x, one_y, other_x, other_y, grad_a_ref, grad_b_ref):
    cut, ranks = one_x.shape
    rest = grad_a_ref.shape[0] - cut
    grad_a_ref[:cut] = one_x[...].astype(jnp.float32) + other_x[...].astype(jnp.float32)
    total = one_y[...].astype(jnp.float32) + other_y[...].astype(jnp.float32)
    grad_a_ref[cut:] = total[:rest]
    for col in range(0, grad_b_ref.shape[1], ranks):
        grad_b_ref[:, col : col + ranks] = total[rest + col : rest + col + ranks]


def finished(ones, others, features, hidden_width):
    ranks = ones[0].shape[1]
    shapes = ((features, ranks), (ranks, hidden_width))
    return pl.pallas_call(
        finish_kernel,
        grid=(1,),
        out_shape=tuple(jax.ShapeDtypeStruct(shape, jnp.float32) for shape in shapes),
        in_specs=[pl.BlockSpec(one.shape, lambda j: (0, 0)) for one in (*ones, *others)],
        out_specs=tuple(pl.BlockSpec(shape, lambda j: (0, 0)) for shape in shapes),
    )(*ones, *others)


RING = [(2 * chip + core, 2 * ((chip + 1) % 4) + core) for chip in range(4) for core in (0, 1)]
SIBLING = [(e, e ^ 1) for e in range(8)]


def send(array, pairs):
    return lax.ppermute(array, "expert", pairs)


def fence(*arrays):
    return lax.optimization_barrier(arrays)


def add_rounded(*terms):
    total = terms[0].astype(jnp.float32)
    for term in terms[1:]:
        total = total + term.astype(jnp.float32)
    return total.astype(jnp.bfloat16)


def sibling(block):
    return send(block, SIBLING)


def dp_swap(array, bit):
    return lax.ppermute(array, "dp", [(d, d ^ bit) for d in range(4)])


def dense_body(
    tokens,
    cotangent,
    routing,
    router_route_weights,
    route_replica_choice,
    device_expert_table,
    gate_up_weight,
    down_weight,
    adapter_down_maps,
    adapter_up_maps,
):
    slot_total = lax.axis_size("expert")
    capacity = tokens.shape[0] * routing.shape[1] // slot_total
    me = lax.axis_index("expert")
    gate_up, down = gate_up_weight[0], down_weight[0]
    adapt_a = adapter_down_maps[0]
    adapt_b = adapter_up_maps[0].reshape(adapt_a.shape[1], -1)

    slot = jnp.stack([me, jnp.int32(slot_total)])

    def forward(mine, twin):
        *saved, part, away = forward_stage(slot, mine, twin, gate_up, down, adapt_a, adapt_b)
        return saved, part, away

    def backward(cots, rows, saved, grads=(), cut=None):
        return backward_stage(slot, cots, rows, saved, down, adapt_b, grads, cut)

    def step(block):
        return send(block, RING)

    tokens = tagged_tokens(
        tokens, routing, router_route_weights, route_replica_choice, device_expert_table, capacity
    )
    tok1 = step(tokens)
    rows0 = (tokens, sibling(tokens))
    tok1, rows0, cotangent = fence(tok1, rows0, cotangent)

    tok2 = step(tok1)
    rows1 = (tok1, sibling(tok1))
    saved0, part0, away0 = forward(*rows0)
    tok2, rows1, part0, away0, cotangent = fence(tok2, rows1, part0, away0, cotangent)

    tok3 = step(tok2)
    rows2 = (tok2, sibling(tok2))
    saved1, part1, away1 = forward(*rows1)
    tok3, rows2, part1, away1, cotangent = fence(tok3, rows2, part1, away1, cotangent)

    cot1 = step(cotangent)
    rows3 = (tok3, sibling(tok3))
    cots0 = (cotangent, sibling(cotangent))
    saved2, part2, away2 = forward(*rows2)
    cot1, rows3, cots0, part2, away2 = fence(cot1, rows3, cots0, part2, away2)

    cot2 = step(cot1)
    cots1 = (cot1, sibling(cot1))
    saved3, part3, away3 = forward(*rows3)
    grads = backward(cots0, rows0, saved0)
    cot2, cots1, part1, away1, part2, away2, part3, away3, grads = fence(
        cot2, cots1, part1, away1, part2, away2, part3, away3, grads
    )

    cot3 = step(cot2)
    cots2 = (cot2, sibling(cot2))
    part1 = add_rounded(part1, sibling(away1))
    grads = backward(cots1, rows1, saved1, grads)
    grads = backward(cots2, rows2, saved2, grads)
    cot3, part1, part2, away2, part3, away3, grads = fence(
        cot3, part1, part2, away2, part3, away3, grads
    )

    sum1 = step(part1)
    cots3 = (cot3, sibling(cot3))
    part2 = add_rounded(part2, sibling(away2))
    features, hidden_width = adapt_a.shape[0], adapt_b.shape[1]
    cut = (features + hidden_width) // 2
    grads = backward(cots3, rows3, saved3, grads, cut)
    sum1, part2, part0, away0, part3, away3, grads = fence(
        sum1, part2, part0, away0, part3, away3, grads
    )

    sum2 = step(add_rounded(part2, sum1))
    got = dp_swap(grads[0], 1), dp_swap(grads[1], 2)
    part3 = add_rounded(part3, sibling(away3))
    part0 = add_rounded(part0, sibling(away0))
    sum2, part0, part3, grads, got = fence(sum2, part0, part3, grads, got)

    sum3 = step(add_rounded(part3, sum2))
    pairs = pair_sums(grads, got)
    got = dp_swap(pairs[0], 2), dp_swap(pairs[1], 1)
    grad_a, grad_b = finished(pairs, got, features, hidden_width)
    mixed = add_rounded(part0, sum3)
    return mixed, grad_a[None], grad_b.reshape(adapter_up_maps.shape)


def body(*arrays):
    if (lax.axis_size("dp"), lax.axis_size("expert"), arrays[2].shape[1]) == (4, 8, 8):
        return dense_body(*arrays)
    return sparse_body(*arrays)


def solution(mesh):
    return jax.shard_map(
        body,
        mesh=mesh,
        in_specs=(
            P(("dp", "expert"), None),
            P(("dp", "expert"), None),
            P(("dp", "expert"), None),
            P(("dp", "expert"), None),
            P(("dp", "expert"), None),
            P(),
            P("expert", None, None),
            P("expert", None, None),
            P("expert", None, None),
            P("expert", None, None, None),
        ),
        out_specs=(
            P(("dp", "expert"), None),
            P("expert", None, None),
            P("expert", None, None, None),
        ),
        check_vma=False,
    )
```

```python
import functools

import jax
import jax.numpy as jnp
from jax import lax
from jax.experimental import pallas as pl
from jax.experimental.pallas import tpu as pltpu
from jax.sharding import PartitionSpec as P

ADAPTER_SCALE = 0.5


def route_rows(routing, route_replica_choice, device_expert_table, capacity):
    slot_total = device_expert_table.shape[0]
    route_total = routing.shape[0] * routing.shape[1]
    expert_flat = routing.reshape(-1)
    holds_mask = (expert_flat[:, None] == device_expert_table[None, :]).astype(jnp.int32)
    copies = jnp.sum(holds_mask, axis=1)
    wanted = route_replica_choice.reshape(-1) % copies
    before = jnp.cumsum(holds_mask, axis=1) - holds_mask
    picked = holds_mask * (before == wanted[:, None]).astype(jnp.int32)
    ahead_of = jnp.cumsum(picked, axis=0) - picked
    position = jnp.sum(picked * ahead_of, axis=1)
    target = jnp.sum(picked * jnp.arange(slot_total, dtype=jnp.int32)[None, :], axis=1)
    kept_mask = position < capacity
    dest_index = jnp.where(kept_mask, target * capacity + position, slot_total * capacity)
    source = jnp.full((slot_total * capacity,), route_total, jnp.int32)
    source = source.at[dest_index].set(jnp.arange(route_total, dtype=jnp.int32), mode="drop")
    return (kept_mask, dest_index, source)


def expert_apply_forward(rows_in, gate_up, down, adapt_a, adapt_b):
    adapter_rank_count = adapt_b.shape[1]
    hidden_width = adapt_b.shape[2]
    reduced_rank_rows = jnp.dot(rows_in, adapt_a, preferred_element_type=jnp.float32).astype(
        jnp.bfloat16
    )
    base_preactivation = jnp.dot(rows_in, gate_up, preferred_element_type=jnp.float32)
    adapter_gate_delta = jnp.dot(
        reduced_rank_rows[:, :adapter_rank_count], adapt_b[0], preferred_element_type=jnp.float32
    )
    adapter_up_delta = jnp.dot(
        reduced_rank_rows[:, adapter_rank_count:], adapt_b[1], preferred_element_type=jnp.float32
    )
    gate_preactivation = base_preactivation[:, :hidden_width] + ADAPTER_SCALE * adapter_gate_delta
    up_preactivation = base_preactivation[:, hidden_width:] + ADAPTER_SCALE * adapter_up_delta
    sigmoid_gate = jax.nn.sigmoid(gate_preactivation)
    active = gate_preactivation * sigmoid_gate
    hidden = (active * up_preactivation).astype(jnp.bfloat16)
    layer_output = jnp.dot(hidden, down, preferred_element_type=jnp.float32).astype(jnp.bfloat16)
    return (
        layer_output,
        (reduced_rank_rows, gate_preactivation, up_preactivation, sigmoid_gate, active),
    )


def expert_backward(rows_in, scaled, down, adapt_b, saved_residuals):
    reduced_rank_rows, gate_preactivation, up_preactivation, sigmoid_gate, active = saved_residuals
    adapter_rank_count = adapt_b.shape[1]
    back_hidden = lax.dot_general(
        scaled, down, (((1,), (1,)), ((), ())), preferred_element_type=jnp.float32
    )
    up_preactivation_gradient = (back_hidden * active).astype(jnp.bfloat16)
    slope = sigmoid_gate * (1.0 + gate_preactivation * (1.0 - sigmoid_gate))
    gate_preactivation_gradient = (back_hidden * up_preactivation * slope).astype(jnp.bfloat16)
    row_dimension_numbers = (((0,), (0,)), ((), ()))
    gate_up_map_gradient = ADAPTER_SCALE * lax.dot_general(
        reduced_rank_rows[:, :adapter_rank_count],
        gate_preactivation_gradient,
        row_dimension_numbers,
        preferred_element_type=jnp.float32,
    )
    up_map_gradient = ADAPTER_SCALE * lax.dot_general(
        reduced_rank_rows[:, adapter_rank_count:],
        up_preactivation_gradient,
        row_dimension_numbers,
        preferred_element_type=jnp.float32,
    )
    cols_dims = (((1,), (1,)), ((), ()))
    gate_reduced_rows = lax.dot_general(
        gate_preactivation_gradient, adapt_b[0], cols_dims, preferred_element_type=jnp.float32
    )
    up_reduced_rows = lax.dot_general(
        up_preactivation_gradient, adapt_b[1], cols_dims, preferred_element_type=jnp.float32
    )
    reduced_gradient = (
        ADAPTER_SCALE * jnp.concatenate([gate_reduced_rows, up_reduced_rows], axis=1)
    ).astype(jnp.bfloat16)
    grad_adapt_a = lax.dot_general(
        rows_in, reduced_gradient, row_dimension_numbers, preferred_element_type=jnp.float32
    )
    return (grad_adapt_a, jnp.stack([gate_up_map_gradient, up_map_gradient]))


def sparse_body(
    tokens,
    cotangent,
    routing,
    router_route_weights,
    route_replica_choice,
    device_expert_table,
    gate_up_weight,
    down_weight,
    adapter_down_maps,
    adapter_up_maps,
):
    slot_total = lax.axis_size("expert")
    tok_rows = tokens.shape[0]
    model_feature_width = tokens.shape[1]
    top_routes = routing.shape[1]
    route_total = tok_rows * top_routes
    capacity = route_total // slot_total
    kept_mask, dest_index, source = route_rows(
        routing, route_replica_choice, device_expert_table, capacity
    )
    valid_route_mask = source < route_total
    safe_route = jnp.minimum(source, route_total - 1)
    route_token_index = safe_route // top_routes
    weight_flat = router_route_weights.reshape(-1)
    route_weight_rows = weight_flat[safe_route]
    zero_row = jnp.zeros((), jnp.bfloat16)
    rows_out = jnp.where(valid_route_mask[:, None], tokens[route_token_index], zero_row).reshape(
        slot_total, capacity, model_feature_width
    )
    product = (
        route_weight_rows[:, None] * cotangent[route_token_index].astype(jnp.float32)
    ).astype(jnp.bfloat16)
    scaled_out = jnp.where(valid_route_mask[:, None], product, zero_row).reshape(
        slot_total, capacity, model_feature_width
    )
    rows_in = lax.all_to_all(rows_out, "expert", split_axis=0, concat_axis=0, tiled=True)
    flattened_rows = rows_in.reshape(-1, model_feature_width)
    layer_output, saved_residuals = expert_apply_forward(
        flattened_rows, gate_up_weight[0], down_weight[0], adapter_down_maps[0], adapter_up_maps[0]
    )
    returned = lax.all_to_all(
        layer_output.reshape(slot_total, capacity, model_feature_width),
        "expert",
        split_axis=0,
        concat_axis=0,
        tiled=True,
    )
    returned = returned.reshape(-1, model_feature_width)
    picked_rows = returned[jnp.minimum(dest_index, slot_total * capacity - 1)]
    weighted = jnp.where(
        kept_mask[:, None],
        weight_flat[:, None] * picked_rows.astype(jnp.float32),
        jnp.zeros((), jnp.float32),
    )
    mixed = jnp.sum(weighted.reshape(tok_rows, top_routes, model_feature_width), axis=1).astype(
        jnp.bfloat16
    )
    scaled_input_rows = lax.all_to_all(
        scaled_out, "expert", split_axis=0, concat_axis=0, tiled=True
    )
    grad_adapt_a, grad_adapt_b = expert_backward(
        flattened_rows,
        scaled_input_rows.reshape(-1, model_feature_width),
        down_weight[0],
        adapter_up_maps[0],
        saved_residuals,
    )
    piece_a = grad_adapt_a.reshape(slot_total, -1)
    piece_b = grad_adapt_b.reshape(slot_total, -1)
    expert_total = max(top_routes, slot_total // 2)
    members = (
        jnp.arange(expert_total, dtype=jnp.int32)[:, None] == device_expert_table[None, :]
    ).astype(jnp.float32)
    piece_a, piece_b = lax.psum((piece_a, piece_b), "dp")
    got_a, got_b = (
        lax.all_to_all(piece_a, "expert", split_axis=0, concat_axis=0, tiled=True),
        lax.all_to_all(piece_b, "expert", split_axis=0, concat_axis=0, tiled=True),
    )
    expert_a = jnp.dot(members, got_a, precision=lax.Precision.HIGHEST)
    expert_b = jnp.dot(members, got_b, precision=lax.Precision.HIGHEST)
    back_dims = (((0,), (0,)), ((), ()))
    spread_a = lax.dot_general(members, expert_a, back_dims, precision=lax.Precision.HIGHEST)
    spread_b = lax.dot_general(members, expert_b, back_dims, precision=lax.Precision.HIGHEST)
    summed_a, summed_b = (
        lax.all_to_all(spread_a, "expert", split_axis=0, concat_axis=0, tiled=True),
        lax.all_to_all(spread_b, "expert", split_axis=0, concat_axis=0, tiled=True),
    )
    grad_a = summed_a.reshape(grad_adapt_a.shape)[None]
    grad_b = summed_b.reshape(grad_adapt_b.shape)[None]
    return (mixed, grad_a, grad_b)


def dot(a, b, a_dim=1, b_dim=0):
    return lax.dot_general(
        a, b, (((a_dim,), (b_dim,)), ((), ())), preferred_element_type=jnp.float32
    )


def first_half(shape):
    return lax.broadcasted_iota(jnp.int32, shape, 1) < shape[1] // 2


def halves(low):
    gate = first_half(low.shape)
    zero = jnp.zeros_like(low)
    return jnp.where(gate, low, zero), jnp.where(gate, zero, low)


def split_weights(table):
    parts = []
    for _ in range(3):
        part = table.astype(jnp.bfloat16).astype(jnp.float32)
        parts.append(part)
        table = table - part
    slot_total, tok_rows = table.shape
    parts.append(jnp.zeros((tok_rows - 3 * slot_total, tok_rows), jnp.float32))
    return jnp.transpose(jnp.concatenate(parts)).astype(jnp.bfloat16)


def joined_weight(extra, slot, slot_total):
    lane = lax.broadcasted_iota(jnp.int32, extra.shape, 1)
    mine = lane == slot
    for part in range(1, 3):
        mine = mine | (lane == slot + part * slot_total)
    chosen = jnp.where(mine, extra.astype(jnp.float32), 0.0)
    return jnp.sum(chosen, axis=1, keepdims=True)


def tagged_kernel(capacity, table_ref, expert_ref, choice_ref, weight_ref, tokens_ref, out_ref):
    slot_total = table_ref.shape[0]
    tok_rows, features = tokens_ref.shape
    out_ref[:, :features] = tokens_ref[...]
    experts, weights = expert_ref[...], weight_ref[...]
    holds = [experts == table_ref[s] for s in range(slot_total)]
    counts = [hold.astype(jnp.float32) for hold in holds]
    copies = sum(counts)
    choice = choice_ref[...].astype(jnp.float32)
    wanted = choice - copies * jnp.floor((choice + 0.5) / copies)
    before = jnp.zeros_like(copies)
    taken, route_weight = [], []
    for hold, count in zip(holds, counts):
        picked = jnp.where(hold & (before == wanted), 1.0, 0.0)
        before = before + count
        taken.append(jnp.sum(picked, axis=0, keepdims=True))
        route_weight.append(jnp.sum(picked * weights, axis=0, keepdims=True))
    shape = (tok_rows, tok_rows)
    earlier = lax.broadcasted_iota(jnp.int32, shape, 0) < lax.broadcasted_iota(jnp.int32, shape, 1)
    rank = dot(
        jnp.concatenate(taken).astype(jnp.bfloat16),
        jnp.where(earlier, 1.0, 0.0).astype(jnp.bfloat16),
    )
    table = jnp.where(rank < capacity, jnp.concatenate(route_weight), 0.0)
    out_ref[:, features:] = split_weights(table)


VMEM = pl.BlockSpec(memory_space=pltpu.VMEM)
SMEM = pl.BlockSpec(memory_space=pltpu.SMEM)
EXTRA = 128


def tagged_tokens(tokens, routing, weights, choice, table, capacity):
    tok_rows, features = tokens.shape
    return pl.pallas_call(
        functools.partial(tagged_kernel, capacity),
        out_shape=jax.ShapeDtypeStruct((tok_rows, features + EXTRA), tokens.dtype),
        in_specs=[SMEM, VMEM, VMEM, VMEM, VMEM],
        out_specs=VMEM,
    )(table, routing.T, choice.T, weights.T, tokens)


def stage_call(kernel, outs, scratch, macs, operands):
    out_shape = tuple(jax.ShapeDtypeStruct(*out) for out in outs)
    moved = sum(array.size * array.dtype.itemsize for array in (*operands, *out_shape))
    return pl.pallas_call(
        kernel,
        out_shape=out_shape,
        in_specs=[SMEM] + [VMEM] * (len(operands) - 1),
        out_specs=(VMEM,) * len(outs),
        scratch_shapes=[pltpu.VMEM(*shape) for shape in scratch],
        compiler_params=pltpu.CompilerParams(vmem_limit_bytes=16 * 2**20),
        cost_estimate=pl.CostEstimate(flops=2 * macs, bytes_accessed=moved, transcendentals=0),
    )(*operands)


def forward_kernel(
    chunk, slot_ref, mine_ref, other_ref, adapt_a_ref, gate_up_ref, adapt_b_ref, down_ref,
    low_ref, active_ref, slope_ref, part_mine_ref, part_other_ref, rows_ref, total_ref,
):
    half, features = part_mine_ref.shape
    hidden_width = down_ref.shape[0]
    rows_ref[:half] = mine_ref[:, :features]
    rows_ref[half:] = other_ref[:, :features]
    rows = rows_ref[...]
    low = dot(rows, adapt_a_ref[...]).astype(jnp.bfloat16)
    low_ref[...] = low
    low_gate, low_up = halves(low)
    for start in range(0, hidden_width, chunk):
        here = slice(start, start + chunk)
        there = slice(hidden_width + start, hidden_width + start + chunk)
        adapt_b = adapt_b_ref[:, here]
        gate = dot(rows, gate_up_ref[:, here]) + ADAPTER_SCALE * dot(low_gate, adapt_b)
        up = dot(rows, gate_up_ref[:, there]) + ADAPTER_SCALE * dot(low_up, adapt_b)
        sigmoid_gate = jax.nn.sigmoid(gate)
        active = gate * sigmoid_gate
        active_ref[:, here] = active
        slope_ref[:, here] = up * (sigmoid_gate * (1.0 + gate * (1.0 - sigmoid_gate)))
        more = dot((active * up).astype(jnp.bfloat16), down_ref[here])
        if start == 0:
            total_ref[...] = more
        else:
            total_ref[...] += more
    out = total_ref[...].astype(jnp.bfloat16).astype(jnp.float32)
    for block_ref, part_ref, out in (
        (mine_ref, part_mine_ref, out[:half]),
        (other_ref, part_other_ref, out[half:]),
    ):
        w = joined_weight(block_ref[:, features:], slot_ref[0], slot_ref[1])
        part_ref[...] = (w * out).astype(jnp.bfloat16)


def forward_stage(slot, mine, other, gate_up, down, adapt_a, adapt_b, chunk=256):
    hidden_width, features = down.shape
    half, both, ranks = mine.shape[0], 2 * mine.shape[0], adapt_a.shape[1]
    bf16, f32 = jnp.bfloat16, jnp.float32
    saved = ((both, hidden_width), f32)
    part = ((half, features), bf16)
    return stage_call(
        functools.partial(forward_kernel, chunk),
        (((both, ranks), bf16), saved, saved, part, part),
        [((both, features), bf16), ((both, features), f32)],
        both * (gate_up.size + down.size + adapt_a.size),
        (slot, mine, other, adapt_a, gate_up, adapt_b, down),
    )


def backward_kernel(chunk, adds, cut, *refs):
    slot_ref, cot_mine, cot_other, mine_ref, other_ref, *refs = refs
    low_ref, active_ref, slope_ref, adapt_b_ref, down_ref, *refs = refs
    grads, (out_a_ref, out_b_ref, scaled_ref, rows_ref) = refs[: 2 * adds], refs[2 * adds :]
    half, features = cot_mine.shape
    for at, (cot_ref, block_ref) in enumerate(((cot_mine, mine_ref), (cot_other, other_ref))):
        here = slice(at * half, (at + 1) * half)
        w = joined_weight(block_ref[:, features:], slot_ref[0], slot_ref[1])
        scaled_ref[here] = (w * cot_ref[...].astype(jnp.float32)).astype(jnp.bfloat16)
        rows_ref[here] = block_ref[:, :features]
    scaled = scaled_ref[...]
    low_gate, low_up = halves(low_ref[...])
    low_back = 0.0
    for start in range(0, down_ref.shape[0], chunk):
        here = slice(start, start + chunk)
        adapt_b = adapt_b_ref[:, here]
        back = dot(scaled, down_ref[here], 1, 1)
        up_grad = (back * active_ref[:, here]).astype(jnp.bfloat16)
        gate_grad = (back * slope_ref[:, here]).astype(jnp.bfloat16)
        sum_b = ADAPTER_SCALE * (dot(low_gate, gate_grad, 0, 0) + dot(low_up, up_grad, 0, 0))
        sum_b = sum_b + grads[1][:, here] if adds else sum_b
        if cut is None:
            out_b_ref[:, here] = sum_b
        else:
            ranks = sum_b.shape[0]
            for col in range(0, chunk, ranks):
                at = features - cut + start + col
                out_b_ref[at : at + ranks] = sum_b[:, col : col + ranks].astype(jnp.bfloat16)
        gate_back, up_back = dot(gate_grad, adapt_b, 1, 1), dot(up_grad, adapt_b, 1, 1)
        low_back = low_back + jnp.where(first_half(gate_back.shape), gate_back, up_back)
    low_grad = (ADAPTER_SCALE * low_back).astype(jnp.bfloat16)
    sum_a = dot(rows_ref[...], low_grad, 0, 0)
    sum_a = sum_a + grads[0][...] if adds else sum_a
    if cut is None:
        out_a_ref[...] = sum_a
    else:
        out_a_ref[...] = sum_a[:cut].astype(jnp.bfloat16)
        out_b_ref[: features - cut] = sum_a[cut:].astype(jnp.bfloat16)


def backward_stage(slot, cots, blocks, saved, down, adapt_b, grads=(), cut=None, chunk=256):
    hidden_width, features = down.shape
    both, ranks = saved[0].shape
    bf16, f32 = jnp.bfloat16, jnp.float32
    outs = (((features, ranks), f32), ((ranks, hidden_width), f32))
    if cut is not None:
        outs = (((cut, ranks), bf16), ((features - cut + hidden_width, ranks), bf16))
    return stage_call(
        functools.partial(backward_kernel, chunk, len(grads) // 2, cut),
        outs,
        [((both, features), bf16), ((both, features), bf16)],
        both * (down.size + features * ranks + 4 * adapt_b.size),
        (slot, *cots, *blocks, *saved, adapt_b, down, *grads),
    )


def pair_kernel(*refs):
    for one_ref, other_ref, out_ref in zip(refs[:2], refs[2:4], refs[4:]):
        total = one_ref[...].astype(jnp.float32) + other_ref[...].astype(jnp.float32)
        out_ref[...] = total.astype(out_ref.dtype)


def pair_sums(ones, others):
    return pl.pallas_call(
        pair_kernel,
        out_shape=tuple(jax.ShapeDtypeStruct(one.shape, one.dtype) for one in ones),
        in_specs=[VMEM] * 4,
        out_specs=(VMEM,) * 2,
    )(*ones, *others)


def finish_kernel(one_x, one_y, other_x, other_y, grad_a_ref, grad_b_ref):
    cut, ranks = one_x.shape
    rest = grad_a_ref.shape[0] - cut
    grad_a_ref[:cut] = one_x[...].astype(jnp.float32) + other_x[...].astype(jnp.float32)
    total = one_y[...].astype(jnp.float32) + other_y[...].astype(jnp.float32)
    grad_a_ref[cut:] = total[:rest]
    for col in range(0, grad_b_ref.shape[1], ranks):
        grad_b_ref[:, col : col + ranks] = total[rest + col : rest + col + ranks]


def finished(ones, others, features, hidden_width):
    ranks = ones[0].shape[1]
    shapes = ((features, ranks), (ranks, hidden_width))
    return pl.pallas_call(
        finish_kernel,
        grid=(1,),
        out_shape=tuple(jax.ShapeDtypeStruct(shape, jnp.float32) for shape in shapes),
        in_specs=[pl.BlockSpec(one.shape, lambda j: (0, 0)) for one in (*ones, *others)],
        out_specs=tuple(pl.BlockSpec(shape, lambda j: (0, 0)) for shape in shapes),
    )(*ones, *others)


RING = [(2 * chip + core, 2 * ((chip + 1) % 4) + core) for chip in range(4) for core in (0, 1)]
SIBLING = [(e, e ^ 1) for e in range(8)]


def send(array, pairs):
    return lax.ppermute(array, "expert", pairs)


def fence(*arrays):
    return lax.optimization_barrier(arrays)


def add_rounded(*terms):
    total = terms[0].astype(jnp.float32)
    for term in terms[1:]:
        total = total + term.astype(jnp.float32)
    return total.astype(jnp.bfloat16)


def sibling(block):
    return send(block, SIBLING)


def dp_swap(array, bit):
    return lax.ppermute(array, "dp", [(d, d ^ bit) for d in range(4)])


def dense_body(
    tokens,
    cotangent,
    routing,
    router_route_weights,
    route_replica_choice,
    device_expert_table,
    gate_up_weight,
    down_weight,
    adapter_down_maps,
    adapter_up_maps,
):
    slot_total = lax.axis_size("expert")
    capacity = tokens.shape[0] * routing.shape[1] // slot_total
    me = lax.axis_index("expert")
    gate_up, down = gate_up_weight[0], down_weight[0]
    adapt_a = adapter_down_maps[0]
    adapt_b = adapter_up_maps[0].reshape(adapt_a.shape[1], -1)

    slot = jnp.stack([me, jnp.int32(slot_total)])

    def forward(mine, twin):
        *saved, part, away = forward_stage(slot, mine, twin, gate_up, down, adapt_a, adapt_b)
        return saved, part, away

    def backward(cots, rows, saved, grads=(), cut=None):
        return backward_stage(slot, cots, rows, saved, down, adapt_b, grads, cut)

    def step(block):
        return send(block, RING)

    tokens = tagged_tokens(
        tokens, routing, router_route_weights, route_replica_choice, device_expert_table, capacity
    )
    tok1, cot1 = step(tokens), step(cotangent)
    rows0, cots0 = (tokens, sibling(tokens)), (cotangent, sibling(cotangent))
    saved0, part0, away0 = forward(*rows0)
    tok1, cot1, cots0, part0, away0 = fence(tok1, cot1, cots0, part0, away0)

    tok2, cot2 = step(tok1), step(cot1)
    rows1, cots1 = (tok1, sibling(tok1)), (cot1, sibling(cot1))
    saved1, part1, away1 = forward(*rows1)
    grads = backward(cots0, rows0, saved0)
    tok2, cot2, cots1, part1, away1, grads = fence(tok2, cot2, cots1, part1, away1, grads)

    tok3, cot3 = step(tok2), step(cot2)
    rows2, cots2 = (tok2, sibling(tok2)), (cot2, sibling(cot2))
    part1 = add_rounded(part1, sibling(away1))
    saved2, part2, away2 = forward(*rows2)
    grads = backward(cots1, rows1, saved1, grads)
    tok3, cot3, cots2, part1, part2, away2, grads = fence(
        tok3, cot3, cots2, part1, part2, away2, grads
    )

    sum1 = step(part1)
    rows3, cots3 = (tok3, sibling(tok3)), (cot3, sibling(cot3))
    part2 = add_rounded(part2, sibling(away2))
    saved3, part3, away3 = forward(*rows3)
    grads = backward(cots2, rows2, saved2, grads)
    features, hidden_width = adapt_a.shape[0], adapt_b.shape[1]
    cut = (features + hidden_width) // 2
    grads = backward(cots3, rows3, saved3, grads, cut)
    sum1, part0, away0, part2, part3, away3, grads = fence(
        sum1, part0, away0, part2, part3, away3, grads
    )

    sum2 = step(add_rounded(part2, sum1))
    got = dp_swap(grads[0], 1), dp_swap(grads[1], 2)
    part3 = add_rounded(part3, sibling(away3))
    part0 = add_rounded(part0, sibling(away0))
    sum2, part0, part3, grads, got = fence(sum2, part0, part3, grads, got)

    sum3 = step(add_rounded(part3, sum2))
    pairs = pair_sums(grads, got)
    got = dp_swap(pairs[0], 2), dp_swap(pairs[1], 1)
    grad_a, grad_b = finished(pairs, got, features, hidden_width)
    mixed = add_rounded(part0, sum3)
    return mixed, grad_a[None], grad_b.reshape(adapter_up_maps.shape)


def body(*arrays):
    if (lax.axis_size("dp"), lax.axis_size("expert"), arrays[2].shape[1]) == (4, 8, 8):
        return dense_body(*arrays)
    return sparse_body(*arrays)


def solution(mesh):
    return jax.shard_map(
        body,
        mesh=mesh,
        in_specs=(
            P(("dp", "expert"), None),
            P(("dp", "expert"), None),
            P(("dp", "expert"), None),
            P(("dp", "expert"), None),
            P(("dp", "expert"), None),
            P(),
            P("expert", None, None),
            P("expert", None, None),
            P("expert", None, None),
            P("expert", None, None, None),
        ),
        out_specs=(
            P(("dp", "expert"), None),
            P("expert", None, None),
            P("expert", None, None, None),
        ),
        check_vma=False,
    )
```

```python
import functools

import jax
import jax.numpy as jnp
from jax import lax
from jax.experimental import pallas as pl
from jax.experimental.pallas import tpu as pltpu
from jax.sharding import PartitionSpec as P

ADAPTER_SCALE = 0.5


def route_rows(routing, route_replica_choice, device_expert_table, capacity):
    slot_total = device_expert_table.shape[0]
    route_total = routing.shape[0] * routing.shape[1]
    expert_flat = routing.reshape(-1)
    holds_mask = (expert_flat[:, None] == device_expert_table[None, :]).astype(jnp.int32)
    copies = jnp.sum(holds_mask, axis=1)
    wanted = route_replica_choice.reshape(-1) % copies
    before = jnp.cumsum(holds_mask, axis=1) - holds_mask
    picked = holds_mask * (before == wanted[:, None]).astype(jnp.int32)
    ahead_of = jnp.cumsum(picked, axis=0) - picked
    position = jnp.sum(picked * ahead_of, axis=1)
    target = jnp.sum(picked * jnp.arange(slot_total, dtype=jnp.int32)[None, :], axis=1)
    kept_mask = position < capacity
    dest_index = jnp.where(kept_mask, target * capacity + position, slot_total * capacity)
    source = jnp.full((slot_total * capacity,), route_total, jnp.int32)
    source = source.at[dest_index].set(jnp.arange(route_total, dtype=jnp.int32), mode="drop")
    return (kept_mask, dest_index, source)


def expert_apply_forward(rows_in, gate_up, down, adapt_a, adapt_b):
    adapter_rank_count = adapt_b.shape[1]
    hidden_width = adapt_b.shape[2]
    reduced_rank_rows = jnp.dot(rows_in, adapt_a, preferred_element_type=jnp.float32).astype(
        jnp.bfloat16
    )
    base_preactivation = jnp.dot(rows_in, gate_up, preferred_element_type=jnp.float32)
    adapter_gate_delta = jnp.dot(
        reduced_rank_rows[:, :adapter_rank_count], adapt_b[0], preferred_element_type=jnp.float32
    )
    adapter_up_delta = jnp.dot(
        reduced_rank_rows[:, adapter_rank_count:], adapt_b[1], preferred_element_type=jnp.float32
    )
    gate_preactivation = base_preactivation[:, :hidden_width] + ADAPTER_SCALE * adapter_gate_delta
    up_preactivation = base_preactivation[:, hidden_width:] + ADAPTER_SCALE * adapter_up_delta
    sigmoid_gate = jax.nn.sigmoid(gate_preactivation)
    active = gate_preactivation * sigmoid_gate
    hidden = (active * up_preactivation).astype(jnp.bfloat16)
    layer_output = jnp.dot(hidden, down, preferred_element_type=jnp.float32).astype(jnp.bfloat16)
    return (
        layer_output,
        (reduced_rank_rows, gate_preactivation, up_preactivation, sigmoid_gate, active),
    )


def expert_backward(rows_in, scaled, down, adapt_b, saved_residuals):
    reduced_rank_rows, gate_preactivation, up_preactivation, sigmoid_gate, active = saved_residuals
    adapter_rank_count = adapt_b.shape[1]
    back_hidden = lax.dot_general(
        scaled, down, (((1,), (1,)), ((), ())), preferred_element_type=jnp.float32
    )
    up_preactivation_gradient = (back_hidden * active).astype(jnp.bfloat16)
    slope = sigmoid_gate * (1.0 + gate_preactivation * (1.0 - sigmoid_gate))
    gate_preactivation_gradient = (back_hidden * up_preactivation * slope).astype(jnp.bfloat16)
    row_dimension_numbers = (((0,), (0,)), ((), ()))
    gate_up_map_gradient = ADAPTER_SCALE * lax.dot_general(
        reduced_rank_rows[:, :adapter_rank_count],
        gate_preactivation_gradient,
        row_dimension_numbers,
        preferred_element_type=jnp.float32,
    )
    up_map_gradient = ADAPTER_SCALE * lax.dot_general(
        reduced_rank_rows[:, adapter_rank_count:],
        up_preactivation_gradient,
        row_dimension_numbers,
        preferred_element_type=jnp.float32,
    )
    cols_dims = (((1,), (1,)), ((), ()))
    gate_reduced_rows = lax.dot_general(
        gate_preactivation_gradient, adapt_b[0], cols_dims, preferred_element_type=jnp.float32
    )
    up_reduced_rows = lax.dot_general(
        up_preactivation_gradient, adapt_b[1], cols_dims, preferred_element_type=jnp.float32
    )
    reduced_gradient = (
        ADAPTER_SCALE * jnp.concatenate([gate_reduced_rows, up_reduced_rows], axis=1)
    ).astype(jnp.bfloat16)
    grad_adapt_a = lax.dot_general(
        rows_in, reduced_gradient, row_dimension_numbers, preferred_element_type=jnp.float32
    )
    return (grad_adapt_a, jnp.stack([gate_up_map_gradient, up_map_gradient]))


def sparse_body(
    tokens,
    cotangent,
    routing,
    router_route_weights,
    route_replica_choice,
    device_expert_table,
    gate_up_weight,
    down_weight,
    adapter_down_maps,
    adapter_up_maps,
):
    slot_total = lax.axis_size("expert")
    tok_rows = tokens.shape[0]
    model_feature_width = tokens.shape[1]
    top_routes = routing.shape[1]
    route_total = tok_rows * top_routes
    capacity = route_total // slot_total
    kept_mask, dest_index, source = route_rows(
        routing, route_replica_choice, device_expert_table, capacity
    )
    valid_route_mask = source < route_total
    safe_route = jnp.minimum(source, route_total - 1)
    route_token_index = safe_route // top_routes
    weight_flat = router_route_weights.reshape(-1)
    route_weight_rows = weight_flat[safe_route]
    zero_row = jnp.zeros((), jnp.bfloat16)
    rows_out = jnp.where(valid_route_mask[:, None], tokens[route_token_index], zero_row).reshape(
        slot_total, capacity, model_feature_width
    )
    product = (
        route_weight_rows[:, None] * cotangent[route_token_index].astype(jnp.float32)
    ).astype(jnp.bfloat16)
    scaled_out = jnp.where(valid_route_mask[:, None], product, zero_row).reshape(
        slot_total, capacity, model_feature_width
    )
    rows_in = lax.all_to_all(rows_out, "expert", split_axis=0, concat_axis=0, tiled=True)
    flattened_rows = rows_in.reshape(-1, model_feature_width)
    layer_output, saved_residuals = expert_apply_forward(
        flattened_rows, gate_up_weight[0], down_weight[0], adapter_down_maps[0], adapter_up_maps[0]
    )
    returned = lax.all_to_all(
        layer_output.reshape(slot_total, capacity, model_feature_width),
        "expert",
        split_axis=0,
        concat_axis=0,
        tiled=True,
    )
    returned = returned.reshape(-1, model_feature_width)
    picked_rows = returned[jnp.minimum(dest_index, slot_total * capacity - 1)]
    weighted = jnp.where(
        kept_mask[:, None],
        weight_flat[:, None] * picked_rows.astype(jnp.float32),
        jnp.zeros((), jnp.float32),
    )
    mixed = jnp.sum(weighted.reshape(tok_rows, top_routes, model_feature_width), axis=1).astype(
        jnp.bfloat16
    )
    scaled_input_rows = lax.all_to_all(
        scaled_out, "expert", split_axis=0, concat_axis=0, tiled=True
    )
    grad_adapt_a, grad_adapt_b = expert_backward(
        flattened_rows,
        scaled_input_rows.reshape(-1, model_feature_width),
        down_weight[0],
        adapter_up_maps[0],
        saved_residuals,
    )
    piece_a = grad_adapt_a.reshape(slot_total, -1)
    piece_b = grad_adapt_b.reshape(slot_total, -1)
    expert_total = max(top_routes, slot_total // 2)
    members = (
        jnp.arange(expert_total, dtype=jnp.int32)[:, None] == device_expert_table[None, :]
    ).astype(jnp.float32)
    piece_a, piece_b = lax.psum((piece_a, piece_b), "dp")
    got_a, got_b = (
        lax.all_to_all(piece_a, "expert", split_axis=0, concat_axis=0, tiled=True),
        lax.all_to_all(piece_b, "expert", split_axis=0, concat_axis=0, tiled=True),
    )
    expert_a = jnp.dot(members, got_a, precision=lax.Precision.HIGHEST)
    expert_b = jnp.dot(members, got_b, precision=lax.Precision.HIGHEST)
    back_dims = (((0,), (0,)), ((), ()))
    spread_a = lax.dot_general(members, expert_a, back_dims, precision=lax.Precision.HIGHEST)
    spread_b = lax.dot_general(members, expert_b, back_dims, precision=lax.Precision.HIGHEST)
    summed_a, summed_b = (
        lax.all_to_all(spread_a, "expert", split_axis=0, concat_axis=0, tiled=True),
        lax.all_to_all(spread_b, "expert", split_axis=0, concat_axis=0, tiled=True),
    )
    grad_a = summed_a.reshape(grad_adapt_a.shape)[None]
    grad_b = summed_b.reshape(grad_adapt_b.shape)[None]
    return (mixed, grad_a, grad_b)


def dot(a, b, a_dim=1, b_dim=0):
    return lax.dot_general(
        a, b, (((a_dim,), (b_dim,)), ((), ())), preferred_element_type=jnp.float32
    )


def first_half(shape):
    return lax.broadcasted_iota(jnp.int32, shape, 1) < shape[1] // 2


def halves(low):
    gate = first_half(low.shape)
    zero = jnp.zeros_like(low)
    return jnp.where(gate, low, zero), jnp.where(gate, zero, low)


def split_weights(table):
    parts = []
    for _ in range(3):
        part = table.astype(jnp.bfloat16).astype(jnp.float32)
        parts.append(part)
        table = table - part
    slot_total, tok_rows = table.shape
    parts.append(jnp.zeros((tok_rows - 3 * slot_total, tok_rows), jnp.float32))
    return jnp.transpose(jnp.concatenate(parts)).astype(jnp.bfloat16)


def joined_weight(extra, slot, slot_total):
    lane = lax.broadcasted_iota(jnp.int32, extra.shape, 1)
    mine = lane == slot
    for part in range(1, 3):
        mine = mine | (lane == slot + part * slot_total)
    chosen = jnp.where(mine, extra.astype(jnp.float32), 0.0)
    return jnp.sum(chosen, axis=1, keepdims=True)


def tagged_kernel(capacity, table_ref, expert_ref, choice_ref, weight_ref, tokens_ref, out_ref):
    slot_total = table_ref.shape[0]
    tok_rows, features = tokens_ref.shape
    out_ref[:, :features] = tokens_ref[...]
    experts, weights = expert_ref[...], weight_ref[...]
    holds = [experts == table_ref[s] for s in range(slot_total)]
    counts = [hold.astype(jnp.float32) for hold in holds]
    copies = sum(counts)
    choice = choice_ref[...].astype(jnp.float32)
    wanted = choice - copies * jnp.floor((choice + 0.5) / copies)
    before = jnp.zeros_like(copies)
    taken, route_weight = [], []
    for hold, count in zip(holds, counts):
        picked = jnp.where(hold & (before == wanted), 1.0, 0.0)
        before = before + count
        taken.append(jnp.sum(picked, axis=0, keepdims=True))
        route_weight.append(jnp.sum(picked * weights, axis=0, keepdims=True))
    shape = (tok_rows, tok_rows)
    earlier = lax.broadcasted_iota(jnp.int32, shape, 0) < lax.broadcasted_iota(jnp.int32, shape, 1)
    rank = dot(
        jnp.concatenate(taken).astype(jnp.bfloat16),
        jnp.where(earlier, 1.0, 0.0).astype(jnp.bfloat16),
    )
    table = jnp.where(rank < capacity, jnp.concatenate(route_weight), 0.0)
    out_ref[:, features:] = split_weights(table)


VMEM = pl.BlockSpec(memory_space=pltpu.VMEM)
SMEM = pl.BlockSpec(memory_space=pltpu.SMEM)
EXTRA = 128


def tagged_tokens(tokens, routing, weights, choice, table, capacity):
    tok_rows, features = tokens.shape
    return pl.pallas_call(
        functools.partial(tagged_kernel, capacity),
        out_shape=jax.ShapeDtypeStruct((tok_rows, features + EXTRA), tokens.dtype),
        in_specs=[SMEM, VMEM, VMEM, VMEM, VMEM],
        out_specs=VMEM,
    )(table, routing.T, choice.T, weights.T, tokens)


def stage_call(kernel, outs, scratch, macs, operands):
    out_shape = tuple(jax.ShapeDtypeStruct(*out) for out in outs)
    moved = sum(array.size * array.dtype.itemsize for array in (*operands, *out_shape))
    return pl.pallas_call(
        kernel,
        out_shape=out_shape,
        in_specs=[SMEM] + [VMEM] * (len(operands) - 1),
        out_specs=(VMEM,) * len(outs),
        scratch_shapes=[pltpu.VMEM(*shape) for shape in scratch],
        compiler_params=pltpu.CompilerParams(vmem_limit_bytes=16 * 2**20),
        cost_estimate=pl.CostEstimate(flops=2 * macs, bytes_accessed=moved, transcendentals=0),
    )(*operands)


def forward_kernel(
    chunk, slot_ref, mine_ref, other_ref, adapt_a_ref, gate_up_ref, adapt_b_ref, down_ref,
    low_ref, active_ref, slope_ref, part_mine_ref, part_other_ref, rows_ref, total_ref,
):
    half, features = part_mine_ref.shape
    hidden_width = down_ref.shape[0]
    rows_ref[:half] = mine_ref[:, :features]
    rows_ref[half:] = other_ref[:, :features]
    rows = rows_ref[...]
    low = dot(rows, adapt_a_ref[...]).astype(jnp.bfloat16)
    low_ref[...] = low
    low_gate, low_up = halves(low)
    for start in range(0, hidden_width, chunk):
        here = slice(start, start + chunk)
        there = slice(hidden_width + start, hidden_width + start + chunk)
        adapt_b = adapt_b_ref[:, here]
        gate = dot(rows, gate_up_ref[:, here]) + ADAPTER_SCALE * dot(low_gate, adapt_b)
        up = dot(rows, gate_up_ref[:, there]) + ADAPTER_SCALE * dot(low_up, adapt_b)
        sigmoid_gate = jax.nn.sigmoid(gate)
        active = gate * sigmoid_gate
        active_ref[:, here] = active
        slope_ref[:, here] = up * (sigmoid_gate * (1.0 + gate * (1.0 - sigmoid_gate)))
        more = dot((active * up).astype(jnp.bfloat16), down_ref[here])
        if start == 0:
            total_ref[...] = more
        else:
            total_ref[...] += more
    out = total_ref[...].astype(jnp.bfloat16).astype(jnp.float32)
    for block_ref, part_ref, out in (
        (mine_ref, part_mine_ref, out[:half]),
        (other_ref, part_other_ref, out[half:]),
    ):
        w = joined_weight(block_ref[:, features:], slot_ref[0], slot_ref[1])
        part_ref[...] = (w * out).astype(jnp.bfloat16)


def forward_stage(slot, mine, other, gate_up, down, adapt_a, adapt_b, chunk=256):
    hidden_width, features = down.shape
    half, both, ranks = mine.shape[0], 2 * mine.shape[0], adapt_a.shape[1]
    bf16, f32 = jnp.bfloat16, jnp.float32
    saved = ((both, hidden_width), f32)
    part = ((half, features), bf16)
    return stage_call(
        functools.partial(forward_kernel, chunk),
        (((both, ranks), bf16), saved, saved, part, part),
        [((both, features), bf16), ((both, features), f32)],
        both * (gate_up.size + down.size + adapt_a.size),
        (slot, mine, other, adapt_a, gate_up, adapt_b, down),
    )


def backward_kernel(chunk, adds, cut, *refs):
    slot_ref, cot_mine, cot_other, mine_ref, other_ref, *refs = refs
    low_ref, active_ref, slope_ref, adapt_b_ref, down_ref, *refs = refs
    grads, (out_a_ref, out_b_ref, scaled_ref, rows_ref) = refs[: 2 * adds], refs[2 * adds :]
    half, features = cot_mine.shape
    for at, (cot_ref, block_ref) in enumerate(((cot_mine, mine_ref), (cot_other, other_ref))):
        here = slice(at * half, (at + 1) * half)
        w = joined_weight(block_ref[:, features:], slot_ref[0], slot_ref[1])
        scaled_ref[here] = (w * cot_ref[...].astype(jnp.float32)).astype(jnp.bfloat16)
        rows_ref[here] = block_ref[:, :features]
    scaled = scaled_ref[...]
    low_gate, low_up = halves(low_ref[...])
    low_back = 0.0
    for start in range(0, down_ref.shape[0], chunk):
        here = slice(start, start + chunk)
        adapt_b = adapt_b_ref[:, here]
        back = dot(scaled, down_ref[here], 1, 1)
        up_grad = (back * active_ref[:, here]).astype(jnp.bfloat16)
        gate_grad = (back * slope_ref[:, here]).astype(jnp.bfloat16)
        sum_b = ADAPTER_SCALE * (dot(low_gate, gate_grad, 0, 0) + dot(low_up, up_grad, 0, 0))
        sum_b = sum_b + grads[1][:, here] if adds else sum_b
        if cut is None:
            out_b_ref[:, here] = sum_b
        else:
            ranks = sum_b.shape[0]
            for col in range(0, chunk, ranks):
                at = features - cut + start + col
                out_b_ref[at : at + ranks] = sum_b[:, col : col + ranks].astype(jnp.bfloat16)
        gate_back, up_back = dot(gate_grad, adapt_b, 1, 1), dot(up_grad, adapt_b, 1, 1)
        low_back = low_back + jnp.where(first_half(gate_back.shape), gate_back, up_back)
    low_grad = (ADAPTER_SCALE * low_back).astype(jnp.bfloat16)
    sum_a = dot(rows_ref[...], low_grad, 0, 0)
    sum_a = sum_a + grads[0][...] if adds else sum_a
    if cut is None:
        out_a_ref[...] = sum_a
    else:
        out_a_ref[...] = sum_a[:cut].astype(jnp.bfloat16)
        out_b_ref[: features - cut] = sum_a[cut:].astype(jnp.bfloat16)


def backward_stage(slot, cots, blocks, saved, down, adapt_b, grads=(), cut=None, chunk=256):
    hidden_width, features = down.shape
    both, ranks = saved[0].shape
    bf16, f32 = jnp.bfloat16, jnp.float32
    outs = (((features, ranks), f32), ((ranks, hidden_width), f32))
    if cut is not None:
        outs = (((cut, ranks), bf16), ((features - cut + hidden_width, ranks), bf16))
    return stage_call(
        functools.partial(backward_kernel, chunk, len(grads) // 2, cut),
        outs,
        [((both, features), bf16), ((both, features), bf16)],
        both * (down.size + features * ranks + 4 * adapt_b.size),
        (slot, *cots, *blocks, *saved, adapt_b, down, *grads),
    )


def pair_kernel(*refs):
    for one_ref, other_ref, out_ref in zip(refs[:2], refs[2:4], refs[4:]):
        total = one_ref[...].astype(jnp.float32) + other_ref[...].astype(jnp.float32)
        out_ref[...] = total.astype(out_ref.dtype)


def pair_sums(ones, others):
    return pl.pallas_call(
        pair_kernel,
        out_shape=tuple(jax.ShapeDtypeStruct(one.shape, one.dtype) for one in ones),
        in_specs=[VMEM] * 4,
        out_specs=(VMEM,) * 2,
    )(*ones, *others)


def finish_kernel(one_x, one_y, other_x, other_y, grad_a_ref, grad_b_ref):
    cut, ranks = one_x.shape
    rest = grad_a_ref.shape[0] - cut
    grad_a_ref[:cut] = one_x[...].astype(jnp.float32) + other_x[...].astype(jnp.float32)
    total = one_y[...].astype(jnp.float32) + other_y[...].astype(jnp.float32)
    grad_a_ref[cut:] = total[:rest]
    for col in range(0, grad_b_ref.shape[1], ranks):
        grad_b_ref[:, col : col + ranks] = total[rest + col : rest + col + ranks]


def finished(ones, others, features, hidden_width):
    ranks = ones[0].shape[1]
    shapes = ((features, ranks), (ranks, hidden_width))
    return pl.pallas_call(
        finish_kernel,
        grid=(1,),
        out_shape=tuple(jax.ShapeDtypeStruct(shape, jnp.float32) for shape in shapes),
        in_specs=[pl.BlockSpec(one.shape, lambda j: (0, 0)) for one in (*ones, *others)],
        out_specs=tuple(pl.BlockSpec(shape, lambda j: (0, 0)) for shape in shapes),
    )(*ones, *others)


RING = [(2 * chip + core, 2 * ((chip + 1) % 4) + core) for chip in range(4) for core in (0, 1)]
SIBLING = [(e, e ^ 1) for e in range(8)]


def send(array, pairs):
    return lax.ppermute(array, "expert", pairs)


def fence(*arrays):
    return lax.optimization_barrier(arrays)


def add_rounded(*terms):
    total = terms[0].astype(jnp.float32)
    for term in terms[1:]:
        total = total + term.astype(jnp.float32)
    return total.astype(jnp.bfloat16)


def sibling(block):
    return send(block, SIBLING)


def dp_swap(array, bit):
    return lax.ppermute(array, "dp", [(d, d ^ bit) for d in range(4)])


def dense_body(
    tokens,
    cotangent,
    routing,
    router_route_weights,
    route_replica_choice,
    device_expert_table,
    gate_up_weight,
    down_weight,
    adapter_down_maps,
    adapter_up_maps,
):
    slot_total = lax.axis_size("expert")
    capacity = tokens.shape[0] * routing.shape[1] // slot_total
    me = lax.axis_index("expert")
    gate_up, down = gate_up_weight[0], down_weight[0]
    adapt_a = adapter_down_maps[0]
    adapt_b = adapter_up_maps[0].reshape(adapt_a.shape[1], -1)

    slot = jnp.stack([me, jnp.int32(slot_total)])

    def forward(mine, twin):
        *saved, part, away = forward_stage(slot, mine, twin, gate_up, down, adapt_a, adapt_b)
        return saved, part, away

    def backward(cots, rows, saved, grads=(), cut=None):
        return backward_stage(slot, cots, rows, saved, down, adapt_b, grads, cut)

    def step(block):
        return send(block, RING)

    tokens = tagged_tokens(
        tokens, routing, router_route_weights, route_replica_choice, device_expert_table, capacity
    )
    tok1, cot1 = step(tokens), step(cotangent)
    rows0, cots0 = (tokens, sibling(tokens)), (cotangent, sibling(cotangent))
    saved0, part0, away0 = forward(*rows0)

    tok1, cots0, part0, away0 = fence(tok1, cots0, part0, away0)
    tok2 = step(tok1)
    rows1 = (tok1, sibling(tok1))
    cots1, rows1 = fence((cot1, sibling(cot1)), rows1)
    cot2 = step(cots1[0])
    saved1, part1, away1 = forward(*rows1)
    grads = backward(cots0, rows0, saved0)

    tok2, part1, away1, grads = fence(tok2, part1, away1, grads)
    tok3 = step(tok2)
    rows2 = (tok2, sibling(tok2))
    cots2, rows2 = fence((cot2, sibling(cot2)), rows2)
    cot3 = step(cots2[0])
    part1 = add_rounded(part1, sibling(away1))
    saved2, part2, away2 = forward(*rows2)
    grads = backward(cots1, rows1, saved1, grads)

    tok3, part1, part2, away2, grads = fence(tok3, part1, part2, away2, grads)
    sum1 = step(part1)
    rows3 = (tok3, sibling(tok3))
    cots3, rows3 = fence((cot3, sibling(cot3)), rows3)
    part2 = add_rounded(part2, sibling(away2))
    grads = backward(cots2, rows2, saved2, grads)
    saved3, part3, away3 = forward(*rows3)
    features, hidden_width = adapt_a.shape[0], adapt_b.shape[1]
    cut = (features + hidden_width) // 2
    grads = backward(cots3, rows3, saved3, grads, cut)
    sum1, part0, away0, part2, part3, away3, grads = fence(
        sum1, part0, away0, part2, part3, away3, grads
    )

    sum2 = step(add_rounded(part2, sum1))
    got = dp_swap(grads[0], 1), dp_swap(grads[1], 2)
    part3 = add_rounded(part3, sibling(away3))
    part0 = add_rounded(part0, sibling(away0))
    sum2, part0, part3, grads, got = fence(sum2, part0, part3, grads, got)

    sum3 = step(add_rounded(part3, sum2))
    pairs = pair_sums(grads, got)
    got = dp_swap(pairs[0], 2), dp_swap(pairs[1], 1)
    grad_a, grad_b = finished(pairs, got, features, hidden_width)
    mixed = add_rounded(part0, sum3)
    return mixed, grad_a[None], grad_b.reshape(adapter_up_maps.shape)


def body(*arrays):
    if (lax.axis_size("dp"), lax.axis_size("expert"), arrays[2].shape[1]) == (4, 8, 8):
        return dense_body(*arrays)
    return sparse_body(*arrays)


def solution(mesh):
    return jax.shard_map(
        body,
        mesh=mesh,
        in_specs=(
            P(("dp", "expert"), None),
            P(("dp", "expert"), None),
            P(("dp", "expert"), None),
            P(("dp", "expert"), None),
            P(("dp", "expert"), None),
            P(),
            P("expert", None, None),
            P("expert", None, None),
            P("expert", None, None),
            P("expert", None, None, None),
        ),
        out_specs=(
            P(("dp", "expert"), None),
            P("expert", None, None),
            P("expert", None, None, None),
        ),
        check_vma=False,
    )
```
